32 devices in a mesh: groups: 2 (over y), dp: 16 (over z, x, core), tensor: 1.
Axes of the slice: x: 2, y: 2, z: 4, core: 2. Of those that a mesh axis runs over, the one named last changes fastest.
Arguments:
- hidden: bfloat16 [8192, 8192], P(('groups', 'dp'), 'tensor'), parts along dimension 0, may hold values from -6 to 6
- norm_gain: bfloat16 [8192], replicated, may hold values from 0.099609375 to 1.8984375
- key_weight: bfloat16 [8192, 512], P('dp', 'tensor'), may hold values from -0.0625 to 0.0625
- value_weight: bfloat16 [8192, 512], P('dp', 'tensor'), may hold values from -0.0625 to 0.0625
- queries: bfloat16 [8192, 4096], P(('groups', 'dp'), 'tensor'), parts along dimension 0, may hold values from -70 to 70
- segment_ids: int32 [8192], P(('groups', 'dp')), parts along dimension 0, may hold values from 0 to 63, never falling along the last dimension, each value on 1 to 128 neighbouring positions
Outputs:
- context: bfloat16 [8192, 4096], P(('groups', 'dp'), 'tensor'), parts along dimension 0
The draws below stay inside these ranges and needn't reach their ends.
There are 2 independent parts, one for each index of `groups`. The reference program is written for one: setup_inputs(seed, part) draws one part's arguments, and reference() takes and returns one part's arrays. A program takes and returns all parts, laid end to end along the dimension named above; an argument that names none is the same for every part. Nothing has to cross between parts.
Inputs may be any that keep to these rules, and one draw needn't show every extreme that they name: `segment_ids`: ids never fall along the tokens; each completion has 1 to 128 tokens and one has exactly 128.
All inputs are finite; a program needn't handle non-finite values.
Results may differ from the reference program's by a relative error of at most 0.011.
Values may be sent and summed in bfloat16 or wider, within the bound.
No kernel may reach another device: no remote copies, remote signals or barrier semaphores. Data moves between devices by JAX's collectives and lax.ppermute only.
A program may use at most 128 MiB of HBM per device.

```python
import math
import jax
import jax.numpy as jnp
import numpy as np
from jax import lax

D = 8192
KVH = 4
HD = 128
GROUP = 8
TOK_DEV = 256
SEGMAX = 128
TOKENS = 4096


def draw_queries(key, part):
    key = jax.random.fold_in(key, 7)
    shape = (TOKENS, KVH * GROUP * HD)
    values = jnp.clip(jax.random.normal(jax.random.fold_in(key, 1), shape, jnp.float32), -6.0, 6.0)
    return values.astype(jnp.bfloat16)


def levels(stream_key, dims, shards, low, high):
    loudness = 1.0
    for axis_at, blocks in shards:
        steps = jax.random.uniform(jax.random.fold_in(jax.random.fold_in(stream_key, 6), axis_at), (blocks,), jnp.float32, low / len(shards), high / len(shards))
        loudness = loudness * jnp.repeat(jnp.exp(steps), dims[axis_at] // blocks).reshape((-1,) + (1,) * (len(dims) - 1 - axis_at))
    return loudness


def profile(amount, total, limit, slope):
    weights = [(1 << 20) // math.isqrt(grade ** slope) + 1 for grade in range(2, amount + 1)]
    rest, holding = total - limit - (amount - 1), [1] * (amount - 1)
    while rest > 0:
        movable = [i for i in range(amount - 1) if holding[i] < limit]
        mass, remaining = sum([weights[i] for i in movable]), rest
        for i in movable:
            more = min(limit - holding[i], max(1, remaining * weights[i] // mass), rest)
            holding[i] = holding[i] + more
            rest = rest - more
    return np.array([limit] + holding)


def uneven(rng, number_of, total, bound, lean):
    if number_of == 2:
        one = jax.random.randint(rng, (), max(1, total - bound), min(bound, total - 1) + 1)
        return jnp.stack([one, total - one])
    tallies = jnp.asarray(profile(number_of, total, bound, lean), jnp.int32)
    twos = (number_of - 1) // 2
    source_of, sink = tallies[1:1 + 2 * twos:2], tallies[2:2 + 2 * twos:2]
    margin = jnp.minimum(source_of - 1, bound - sink)
    shifted = jax.random.randint(jax.random.fold_in(rng, 1), (twos,), 0, 1 << 20) % (margin + 1)
    tallies = tallies.at[1:1 + 2 * twos:2].set(source_of - shifted).at[2:2 + 2 * twos:2].set(sink + shifted)
    return tallies[jax.random.permutation(jax.random.fold_in(rng, 2), number_of)]


def centred(stream_key, extent, deviation, reach, pieces=(), kind=jnp.bfloat16):
    factor_of = levels(stream_key, extent, pieces, -0.22, 0.18) if pieces else 1.0
    drawn = jax.random.normal(stream_key, extent, jnp.float32) * deviation * factor_of
    return jnp.minimum(jnp.maximum(drawn, -reach), reach).astype(kind)


def setup_inputs(seed: int = 0, part: int = 0) -> dict:
    key_of = jax.random.split(jax.random.key(seed), 7)
    part_splits = jax.random.split(jax.random.fold_in(key_of[6], part), 7)
    hidden = centred(part_splits[0], (TOKENS, D), 1.0, 6.0, ((0, 16),))
    norm_gain = jnp.clip(1.0 + 0.18 * jax.random.normal(key_of[1], (D,), jnp.float32), 0.099609375, 1.8984375).astype(jnp.bfloat16)
    key_weight = centred(key_of[2], (D, KVH * HD), D ** -0.5, 0.0625, ((0, 16),))
    value_weight = centred(key_of[3], (D, KVH * HD), D ** -0.5, 0.0625, ((0, 16),))
    queries = draw_queries(jax.random.fold_in(jax.random.fold_in(key_of[6], part), 71), part)
    segment_ids = jnp.searchsorted(jnp.cumsum(uneven(part_splits[5], 2 * TOKENS // SEGMAX, TOKENS, SEGMAX, 0)), jnp.arange(TOKENS), side="right").astype(jnp.int32)
    return {"hidden": hidden, "norm_gain": norm_gain, "key_weight": key_weight, "value_weight": value_weight, "queries": queries, "segment_ids": segment_ids}


def rotary(block, positions):
    half = HD // 2
    freqs = 500000.0 ** (-(2.0 * jnp.arange(half, dtype=jnp.float32)) / HD)
    angles = positions[:, None] * freqs[None, :]
    cosine = jnp.cos(angles)[:, None, :]
    sine = jnp.sin(angles)[:, None, :]
    first = block[..., :half]
    second = block[..., half:]
    return jnp.concatenate([first * cosine - second * sine, second * cosine + first * sine], axis=-1)

def reference(hidden, norm_gain, key_weight, value_weight, queries, segment_ids):
    states = hidden.astype(jnp.float32)
    meansq = lax.optimization_barrier(jnp.mean(states * states, axis=-1, keepdims=True))
    normed = (states * lax.rsqrt(meansq + 1e-05) * norm_gain.astype(jnp.float32)).astype(jnp.bfloat16)
    keys_raw = jnp.dot(normed, key_weight, preferred_element_type=jnp.float32).astype(jnp.bfloat16)
    values = jnp.dot(normed, value_weight, preferred_element_type=jnp.float32).astype(jnp.bfloat16)
    index_all = jnp.arange(TOKENS, dtype=jnp.int32)
    starts_flag = jnp.concatenate([jnp.ones((1,), bool), segment_ids[1:] != segment_ids[:-1]])
    seg_start = lax.cummax(jnp.where(starts_flag, index_all, 0), axis=0)
    positions = (index_all - seg_start).astype(jnp.float32)
    keys = rotary(keys_raw.astype(jnp.float32).reshape(TOKENS, KVH, HD), positions).astype(jnp.bfloat16)
    values_heads = values.reshape(TOKENS, KVH, HD)
    padded_keys = jnp.concatenate([jnp.zeros((TOK_DEV, KVH, HD), jnp.bfloat16), keys], axis=0)
    padded_values = jnp.concatenate([jnp.zeros((TOK_DEV, KVH, HD), jnp.bfloat16), values_heads], axis=0)
    padded_segs = jnp.concatenate([jnp.full((TOK_DEV,), -1, jnp.int32), segment_ids], axis=0)
    query_heads = queries.reshape(TOKENS, KVH, GROUP, HD)
    scale = 1.0 / HD ** 0.5

    def one_block(block_index):
        first_row = (block_index * TOK_DEV).astype(jnp.int32)
        query_block = lax.dynamic_slice_in_dim(query_heads, first_row, TOK_DEV, 0).astype(jnp.float32)
        query_segs = lax.dynamic_slice_in_dim(segment_ids, first_row, TOK_DEV, 0)
        key_block = lax.dynamic_slice_in_dim(padded_keys, first_row, 2 * TOK_DEV, 0).astype(jnp.float32)
        value_block = lax.dynamic_slice_in_dim(padded_values, first_row, 2 * TOK_DEV, 0).astype(jnp.float32)
        key_segs = lax.dynamic_slice_in_dim(padded_segs, first_row, 2 * TOK_DEV, 0)
        scores = jnp.einsum('tkgd,skd->kgts', query_block, key_block) * scale
        query_pos = jnp.arange(TOK_DEV, dtype=jnp.int32)[:, None] + TOK_DEV
        key_pos = jnp.arange(2 * TOK_DEV, dtype=jnp.int32)[None, :]
        allowed = (key_pos <= query_pos) & (query_segs[:, None] == key_segs[None, :])
        masked = jnp.where(allowed, scores, -1e+30)
        largest = lax.optimization_barrier(jnp.max(masked, axis=-1, keepdims=True))
        expd = jnp.where(allowed, jnp.exp(masked - largest), 0.0)
        weights = (expd / lax.optimization_barrier(jnp.sum(expd, axis=-1, keepdims=True))).astype(jnp.bfloat16)
        out_block = jnp.einsum('kgts,skd->tkgd', weights.astype(jnp.float32), value_block)
        return out_block.reshape(TOK_DEV, KVH * GROUP * HD).astype(jnp.bfloat16)
    blocks = lax.map(one_block, jnp.arange(TOKENS // TOK_DEV, dtype=jnp.int32))
    return blocks.reshape(TOKENS, KVH * GROUP * HD)
```

```python
import functools

import jax
import jax.numpy as jnp
from jax import lax
from jax.experimental import pallas as pl
from jax.experimental.pallas import tpu as pltpu
from jax.sharding import PartitionSpec as P

HD = 128
GROUP = 8
REACH = 128
EPS = 1e-05
F32 = jnp.float32
BF16 = jnp.bfloat16
VMEM_LIMIT = 48 * 1024 * 1024


def params():
    return pltpu.CompilerParams(vmem_limit_bytes=VMEM_LIMIT)


def cost(flops, nbytes, trans=0):
    return pl.CostEstimate(flops=flops, bytes_accessed=nbytes, transcendentals=trans)


def from_behind(value, axis, steps):
    count = lax.axis_size(axis)
    initial, last = (max(0, -steps), min(count, count - steps))
    return lax.ppermute(value, axis, [(source, source + steps) for source in range(initial, last)])


def norm_kernel(core_ref, h_ref, g_ref, mine_ref, theirs_ref):
    width = h_ref.shape[1]
    half = width // 16
    x = h_ref[...].astype(F32)
    meansq = jnp.sum(x * x, axis=-1, keepdims=True) * (1.0 / width)
    scale = lax.rsqrt(meansq + EPS)
    first = core_ref[0] == 0
    for b in range(8):
        lo = slice(2 * b * half, (2 * b + 1) * half)
        hi = slice((2 * b + 1) * half, (2 * b + 2) * half)
        n_lo = h_ref[:, lo].astype(F32) * scale * g_ref[:, lo].astype(F32)
        n_hi = h_ref[:, hi].astype(F32) * scale * g_ref[:, hi].astype(F32)
        out = slice(b * half, (b + 1) * half)
        mine_ref[:, out] = jnp.where(first, n_lo, n_hi).astype(BF16)
        theirs_ref[:, out] = jnp.where(first, n_hi, n_lo).astype(BF16)


def normalise(core, hidden, gain):
    rows, width = hidden.shape
    step = 64
    out = jax.ShapeDtypeStruct((rows, width // 2), BF16)
    return pl.pallas_call(
        norm_kernel,
        grid_spec=pltpu.PrefetchScalarGridSpec(
            num_scalar_prefetch=1,
            grid=(rows // step,),
            in_specs=[
                pl.BlockSpec((step, width), lambda i, c: (i, 0)),
                pl.BlockSpec((1, width), lambda i, c: (0, 0)),
            ],
            out_specs=[pl.BlockSpec((step, width // 2), lambda i, c: (i, 0))] * 2,
        ),
        out_shape=[out, out],
        compiler_params=params(),
        cost_estimate=cost(8 * rows * width, 4 * rows * width),
        name="norm",
    )(core, hidden, gain.reshape(1, width))


def project_kernel(count, carried, index_ref, xa_ref, xb_ref, *refs):
    weights, refs = refs[:count], refs[count:]
    before, (oa_ref, ob_ref) = refs[:-2], refs[-2:]
    rows = xa_ref.shape[0]
    total = None
    for j in range(count):
        depth = weights[j].shape[0]
        columns = pl.ds(pl.multiple_of(index_ref[j] * depth, depth), depth)
        x = jnp.concatenate([xa_ref[:, columns], xb_ref[:, columns]], axis=0)
        part = jnp.dot(x, weights[j][...], preferred_element_type=F32)
        total = part if total is None else total + part
    if carried:
        oa_ref[...] = before[0][...] + total[:rows]
        ob_ref[...] = before[1][...] + total[rows:]
    else:
        oa_ref[...] = total[:rows]
        ob_ref[...] = total[rows:]


def project(index, xa, xb, weights, before=()):
    rows = xa.shape[0]
    depth, feats = weights[0].shape
    out = jax.ShapeDtypeStruct((rows, feats), F32)
    whole = pl.BlockSpec(memory_space=pltpu.VMEM)
    return pl.pallas_call(
        functools.partial(project_kernel, len(weights), bool(before)),
        in_specs=[pl.BlockSpec(memory_space=pltpu.SMEM)]
        + [whole] * (2 + len(weights) + len(before)),
        out_specs=[whole, whole],
        out_shape=[out, out],
        compiler_params=params(),
        cost_estimate=cost(
            4 * rows * depth * feats * len(weights), 2 * depth * feats * len(weights) + 4 * rows * 4096
        ),
        name="project",
    )(index, xa, xb, *weights, *before)


def keys_kernel(a_ref, b_ref, cos_ref, sin_ref, out_ref):
    cos, sin = cos_ref[...], sin_ref[...]
    for h in range(a_ref.shape[1] // HD):
        at = slice(h * HD, (h + 1) * HD)
        raw = (a_ref[:, at] + b_ref[:, at]).astype(BF16).astype(F32)
        out_ref[:, at] = (raw * cos + pltpu.roll(raw, HD // 2, 1) * sin).astype(BF16)


def finish_keys(a, b, cos, sin):
    rows, feats = a.shape
    return pl.pallas_call(
        keys_kernel,
        out_shape=jax.ShapeDtypeStruct((rows, feats), BF16),
        compiler_params=params(),
        cost_estimate=cost(6 * rows * feats, 10 * rows * feats),
        name="keys",
    )(a, b, cos, sin)


def scores_kernel(q_ref, ka_ref, kb_ref, sq_ref, sk_ref, out_ref):
    rows, span = q_ref.shape[0], sk_ref.shape[1]
    keys = jnp.concatenate([ka_ref[...], kb_ref[...]], axis=0)
    q_at = lax.broadcasted_iota(jnp.int32, (rows, span), 0) + (span - rows)
    k_at = lax.broadcasted_iota(jnp.int32, (rows, span), 1)
    allowed = (k_at <= q_at) & (sq_ref[...] == sk_ref[...])
    scale = 1.0 / HD**0.5
    for j in range(GROUP):
        q = q_ref[:, j * HD : (j + 1) * HD]
        s = lax.dot_general(q, keys, (((1,), (1,)), ((), ())), preferred_element_type=F32)
        s = jnp.where(allowed, s * scale, -1e30)
        e = jnp.exp(s - jnp.max(s, axis=-1, keepdims=True))
        w = e * (1.0 / jnp.sum(e, axis=-1, keepdims=True))
        out_ref[0, j * rows : (j + 1) * rows, :] = w.astype(BF16)


def softmax_weights(queries, block, keys_a, block_a, keys_b, block_b, segs_q, segs_k):
    rows = REACH
    heads = keys_a.shape[1] // HD
    return pl.pallas_call(
        scores_kernel,
        grid=(heads,),
        in_specs=[
            pl.BlockSpec((rows, GROUP * HD), lambda h: (block, h)),
            pl.BlockSpec((rows, HD), lambda h: (block_a, h)),
            pl.BlockSpec((rows, HD), lambda h: (block_b, h)),
            pl.BlockSpec((rows, 1), lambda h: (0, 0)),
            pl.BlockSpec((1, 2 * rows), lambda h: (0, 0)),
        ],
        out_specs=pl.BlockSpec((1, GROUP * rows, 2 * rows), lambda h: (h, 0, 0)),
        out_shape=jax.ShapeDtypeStruct((heads, GROUP * rows, 2 * rows), BF16),
        compiler_params=params(),
        cost_estimate=cost(
            4 * heads * GROUP * rows * rows * HD, 6 * rows * heads * GROUP * HD, 2 * heads * GROUP * rows * rows
        ),
        name="scores",
    )(queries, keys_a, keys_b, segs_q, segs_k)


def context_kernel(p0_ref, p1_ref, prev_ref, own_ref, out_ref):
    rows = prev_ref.shape[0]
    first = jnp.concatenate([prev_ref[...], own_ref[:rows, :]], axis=0)
    for block, (p_ref, values) in enumerate(((p0_ref, first), (p1_ref, own_ref[...]))):
        c = jnp.dot(p_ref[0], values, preferred_element_type=F32).astype(BF16)
        for j in range(GROUP):
            out_ref[block * rows : (block + 1) * rows, j * HD : (j + 1) * HD] = c[j * rows : (j + 1) * rows]


def contexts(p0, p1, prev, own):
    heads, _, span = p0.shape
    rows = prev.shape[0]
    weights = pl.BlockSpec((1, GROUP * rows, span), lambda h: (h, 0, 0))
    return pl.pallas_call(
        context_kernel,
        grid=(heads,),
        in_specs=[
            weights,
            weights,
            pl.BlockSpec((rows, HD), lambda h: (0, h)),
            pl.BlockSpec((2 * rows, HD), lambda h: (0, h)),
        ],
        out_specs=pl.BlockSpec((2 * rows, GROUP * HD), lambda h: (0, h)),
        out_shape=jax.ShapeDtypeStruct((2 * rows, heads * GROUP * HD), BF16),
        compiler_params=params(),
        cost_estimate=cost(4 * heads * GROUP * rows * span * HD, 12 * rows * heads * GROUP * HD),
        name="context",
    )(p0, p1, prev, own)


def place(p):
    z, x = (p, 0) if p < 4 else (7 - p, 1)
    return z * 2 + x


def ring(signs):
    return [
        (y * 16 + place(p) * 2 + c, y * 16 + place((p + sign) % 8) * 2 + c)
        for y, sign in enumerate(signs)
        for p in range(8)
        for c in range(2)
    ]


def on_ring(hidden, norm_gain, key_weight, value_weight, queries, segment_ids):
    both = ("groups", "dp")
    key_way, value_way = ring((1, -1)), ring((-1, 1))
    other_group = [(i, (i + 16) % 32) for i in range(32)]
    other_core = [(i, i ^ 1) for i in range(16)]

    def send(value, way):
        return lax.ppermute(value, both, way)

    def swap(value):
        return lax.ppermute(value, "dp", other_core)

    me = lax.axis_index("dp")
    chip, core = me // 2, me % 2
    z, x = chip // 2, chip % 2
    position = jnp.where(x == 0, z, 7 - z)
    sign = jnp.where(lax.axis_index("groups") == 0, 1, -1)

    k1, v1 = send(key_weight, key_way), send(value_weight, value_way)
    yk1 = send(k1, other_group)
    k2, v2 = send(k1, key_way), send(v1, value_way)
    yk2, yv2 = send(k2, other_group), send(v2, other_group)
    k3, v3 = send(k2, key_way), send(v2, value_way)
    yv1 = send(v1, other_group)
    k4, k3b = send(k3, key_way), send(yk2, value_way)
    v4, v3b = send(v3, value_way), send(yv2, key_way)

    def blocks(steps):
        p = jnp.mod(position + sign * jnp.array(steps, jnp.int32), 8)
        return jnp.where(p < 4, 2 * p, 2 * (7 - p) + 1).astype(jnp.int32)

    rows = segment_ids.shape[0]
    behind = from_behind(segment_ids[rows - REACH :], "dp", 1)
    behind = jnp.where(me > 0, behind, -1)
    window = jnp.concatenate([behind, segment_ids], axis=0)
    index = jnp.arange(window.shape[0], dtype=jnp.int32)
    earlier = (window[None, :] == segment_ids[:, None]) & (index[None, :] < index[REACH:, None])
    positions = jnp.sum(earlier.astype(jnp.int32), axis=1).astype(F32)
    half = HD // 2
    freqs = 500000.0 ** (-(2.0 * jnp.arange(half, dtype=F32)) / HD)
    angles = positions[:, None] * freqs[None, :]
    cos, sin = jnp.cos(angles), jnp.sin(angles)
    cos = jnp.concatenate([cos, cos], axis=1)
    sin = jnp.concatenate([-sin, sin], axis=1)

    mine, theirs = normalise(core.reshape(1).astype(jnp.int32), hidden, norm_gain)
    other = swap(theirs)

    part = project(blocks([0, -1, 1, -2, -3, 2]), mine, other, [key_weight, k1, yk1, k2, k3, yk2])
    own_k, other_k = project(blocks([-4, 3]), mine, other, [k4, k3b], part)
    keys = finish_keys(own_k, swap(other_k), cos, sin)
    prev_keys = from_behind(keys[rows - REACH :], "dp", 1)

    segs_q = segment_ids.reshape(rows, 1)
    p1 = softmax_weights(
        queries, 1, keys, 0, keys, 1, segs_q[REACH:], segment_ids.reshape(1, rows)
    )
    p0 = softmax_weights(
        queries, 0, prev_keys, 0, keys, 0, segs_q[:REACH], window[: 2 * REACH].reshape(1, 2 * REACH)
    )

    part = project(blocks([0, 1, 2, 3, -2]), mine, other, [value_weight, v1, v2, v3, yv2])
    own_v, other_v = project(blocks([-1, 4, -3]), mine, other, [yv1, v4, v3b], part)
    values = (own_v + swap(other_v)).astype(BF16)
    prev_values = from_behind(values[rows - REACH :], "dp", 1)
    return contexts(p0, p1, prev_values, values)


def rotary(block, positions):
    half = HD // 2
    freqs = 500000.0 ** (-(2.0 * jnp.arange(half, dtype=jnp.float32)) / HD)
    angles = positions[:, None] * freqs[None, :]
    cosine = jnp.cos(angles)[:, None, :]
    sine = jnp.sin(angles)[:, None, :]
    first = block[..., :half]
    second = block[..., half:]
    return jnp.concatenate(
        [first * cosine - second * sine, second * cosine + first * sine], axis=-1
    )


def on_any(hidden, norm_gain, key_weight, value_weight, queries, segment_ids):
    whole = lax.all_gather(hidden, "tensor", axis=1, tiled=True)
    states = whole.astype(jnp.float32)
    meansq = jnp.mean(states * states, axis=-1, keepdims=True)
    normed = (states * lax.rsqrt(meansq + EPS) * norm_gain.astype(jnp.float32)).astype(BF16)
    local_rows = normed.shape[0]
    head_cols = key_weight.shape[1]

    def add_rows(piece):
        return jnp.dot(normed, piece, preferred_element_type=jnp.float32)

    key_sum = add_rows(lax.all_gather(key_weight, "dp", axis=0, tiled=True))
    value_sum = add_rows(lax.all_gather(value_weight, "dp", axis=0, tiled=True))
    keys_raw = key_sum.astype(BF16)
    values = value_sum.astype(BF16)
    earlier_keys, earlier_values, earlier_segs = from_behind(
        (keys_raw, values, segment_ids), "dp", 1
    )
    earlier_count = earlier_keys.shape[0]
    has_earlier = lax.axis_index("dp") > 0
    earlier_segs = jnp.where(has_earlier, earlier_segs, -1)
    window_segs = jnp.concatenate([earlier_segs, segment_ids], axis=0)
    window_len = window_segs.shape[0]
    window_index = jnp.arange(window_len, dtype=jnp.int32)
    same_seg = window_segs[:, None] == window_segs[None, :]
    before = window_index[None, :] < window_index[:, None]
    positions = jnp.sum((same_seg & before).astype(jnp.int32), axis=1)
    heads_here = head_cols // HD
    window_raw = (
        jnp.concatenate([earlier_keys, keys_raw], axis=0)
        .astype(jnp.float32)
        .reshape(window_len, heads_here, HD)
    )
    window_keys = rotary(window_raw, positions.astype(jnp.float32)).astype(BF16)
    window_values = jnp.concatenate([earlier_values, values], axis=0).reshape(
        window_len, heads_here, HD
    )
    query_heads = queries.reshape(local_rows, heads_here, GROUP, HD)
    scale = 1.0 / HD**0.5
    scores = (
        jnp.einsum("tkgd,skd->kgts", query_heads, window_keys, preferred_element_type=jnp.float32)
        * scale
    )
    query_pos = jnp.arange(local_rows, dtype=jnp.int32)[:, None] + earlier_count
    allowed = (window_index[None, :] <= query_pos) & (segment_ids[:, None] == window_segs[None, :])
    masked = jnp.where(allowed, scores, -1e30)
    largest = jnp.max(masked, axis=-1, keepdims=True)
    expd = jnp.where(allowed, jnp.exp(masked - largest), 0.0)
    weights = (expd / jnp.sum(expd, axis=-1, keepdims=True)).astype(BF16)
    out_heads = jnp.einsum(
        "kgts,skd->tkgd", weights, window_values, preferred_element_type=jnp.float32
    )
    return out_heads.reshape(local_rows, heads_here * GROUP * HD).astype(BF16)


def solution(mesh):
    in_specs = (
        P(("groups", "dp"), "tensor"),
        P(),
        P("dp", "tensor"),
        P("dp", "tensor"),
        P(("groups", "dp"), "tensor"),
        P(("groups", "dp")),
    )
    out_specs = P(("groups", "dp"), "tensor")
    small = (mesh.shape["groups"], mesh.shape["dp"], mesh.shape["tensor"]) == (2, 16, 1)
    return jax.shard_map(
        on_ring if small else on_any,
        mesh=mesh,
        in_specs=in_specs,
        out_specs=out_specs,
        check_vma=False,
    )
```

```python
import functools

import jax
import jax.numpy as jnp
from jax import lax
from jax.experimental import pallas as pl
from jax.experimental.pallas import tpu as pltpu
from jax.sharding import PartitionSpec as P

HD = 128
GROUP = 8
REACH = 128
EPS = 1e-05
F32 = jnp.float32
BF16 = jnp.bfloat16
VMEM_LIMIT = 48 * 1024 * 1024


def params():
    return pltpu.CompilerParams(vmem_limit_bytes=VMEM_LIMIT)


def cost(flops, nbytes, trans=0):
    return pl.CostEstimate(flops=flops // 1000, bytes_accessed=nbytes // 1000, transcendentals=trans // 1000)


def from_behind(value, axis, steps):
    count = lax.axis_size(axis)
    initial, last = (max(0, -steps), min(count, count - steps))
    return lax.ppermute(value, axis, [(source, source + steps) for source in range(initial, last)])


def norm_kernel(core_ref, h_ref, g_ref, mine_ref, *theirs):
    width = h_ref.shape[1]
    half = width // 16
    x = h_ref[...].astype(F32)
    meansq = jnp.sum(x * x, axis=-1, keepdims=True) * (1.0 / width)
    scale = lax.rsqrt(meansq + EPS)
    first = core_ref[0] == 0
    for b in range(8):
        lo = slice(2 * b * half, (2 * b + 1) * half)
        hi = slice((2 * b + 1) * half, (2 * b + 2) * half)
        n_lo = h_ref[:, lo].astype(F32) * scale * g_ref[:, lo].astype(F32)
        n_hi = h_ref[:, hi].astype(F32) * scale * g_ref[:, hi].astype(F32)
        out = slice(b * half, (b + 1) * half)
        mine_ref[:, out] = jnp.where(first, n_lo, n_hi).astype(BF16)
        for step, theirs_ref in enumerate(theirs):

            @pl.when(pl.program_id(0) == step)
            def _():
                theirs_ref[:, out] = jnp.where(first, n_hi, n_lo).astype(BF16)


def normalise(core, hidden, gain):
    rows, width = hidden.shape
    step = 64
    mine = jax.ShapeDtypeStruct((rows, width // 2), BF16)
    theirs = jax.ShapeDtypeStruct((step, width // 2), BF16)
    mine, *theirs = pl.pallas_call(
        norm_kernel,
        grid_spec=pltpu.PrefetchScalarGridSpec(
            num_scalar_prefetch=1,
            grid=(rows // step,),
            in_specs=[
                pl.BlockSpec((step, width), lambda i, c: (i, 0)),
                pl.BlockSpec((1, width), lambda i, c: (0, 0)),
            ],
            out_specs=[pl.BlockSpec((step, width // 2), lambda i, c: (i, 0))]
            + [pl.BlockSpec((step, width // 2), lambda i, c: (0, 0))] * (rows // step),
        ),
        out_shape=[mine] + [theirs] * (rows // step),
        compiler_params=params(),
        cost_estimate=cost(8 * rows * width, 4 * rows * width),
        name="norm",
    )(core, hidden, gain.reshape(1, width))
    return mine, theirs


def project_kernel(count, parts, carried, index_ref, xa_ref, *refs):
    others, refs = refs[:parts], refs[parts:]
    weights, refs = refs[:count], refs[count:]
    before, outs = refs[:carried], refs[carried:]
    total = None
    for j in range(count):
        depth = weights[j].shape[0]
        columns = pl.ds(pl.multiple_of(index_ref[j] * depth, depth), depth)
        x = jnp.concatenate([ref[:, columns] for ref in (xa_ref, *others)], axis=0)
        part = jnp.dot(x, weights[j][...], preferred_element_type=F32)
        total = part if total is None else total + part
    held = jnp.concatenate([ref[...] for ref in before], axis=0) if carried else None
    total = held + total if carried else total
    at = 0
    for ref in outs:
        ref[...] = total[at : at + ref.shape[0]]
        at += ref.shape[0]


def project(index, xa, others, weights, before=(), split=1):
    rows = xa.shape[0]
    depth, feats = weights[0].shape
    outs = [jax.ShapeDtypeStruct((rows, feats), F32)]
    outs += [jax.ShapeDtypeStruct((rows // split, feats), F32)] * split
    whole = pl.BlockSpec(memory_space=pltpu.VMEM)
    operands = [xa, *others, *weights, *before]
    return pl.pallas_call(
        functools.partial(project_kernel, len(weights), len(others), len(before)),
        in_specs=[pl.BlockSpec(memory_space=pltpu.SMEM)] + [whole] * len(operands),
        out_specs=[whole] * len(outs),
        out_shape=outs,
        compiler_params=params(),
        cost_estimate=cost(
            4 * rows * depth * feats * len(weights), 2 * depth * feats * len(weights) + 4 * rows * 4096
        ),
        name="project",
    )(index, *operands)


def keys_kernel(a_ref, cos_ref, sin_ref, *refs):
    cos, sin = cos_ref[...], sin_ref[...]
    others, out_ref = refs[:-1], refs[-1]
    for h in range(a_ref.shape[1] // HD):
        at = slice(h * HD, (h + 1) * HD)
        b = jnp.concatenate([ref[:, at] for ref in others], axis=0)
        raw = (a_ref[:, at] + b).astype(BF16).astype(F32)
        out_ref[:, at] = (raw * cos + pltpu.roll(raw, HD // 2, 1) * sin).astype(BF16)


def finish_keys(a, others, cos, sin):
    rows, feats = a.shape
    return pl.pallas_call(
        keys_kernel,
        out_shape=jax.ShapeDtypeStruct((rows, feats), BF16),
        compiler_params=params(),
        cost_estimate=cost(6 * rows * feats, 10 * rows * feats),
        name="keys",
    )(a, cos, sin, *others)


def scores_kernel(q_ref, ka_ref, kb_ref, sq_ref, sk_ref, out_ref):
    rows, span = q_ref.shape[0], sk_ref.shape[1]
    keys = jnp.concatenate([ka_ref[...], kb_ref[...]], axis=0)
    q_at = lax.broadcasted_iota(jnp.int32, (rows, span), 0) + (span - rows)
    k_at = lax.broadcasted_iota(jnp.int32, (rows, span), 1)
    allowed = (k_at <= q_at) & (sq_ref[...] == sk_ref[...])
    scale = 1.0 / HD**0.5
    for j in range(GROUP):
        q = q_ref[:, j * HD : (j + 1) * HD]
        s = lax.dot_general(q, keys, (((1,), (1,)), ((), ())), preferred_element_type=F32)
        s = jnp.where(allowed, s * scale, -1e30)
        e = jnp.exp(s - jnp.max(s, axis=-1, keepdims=True))
        w = e * (1.0 / jnp.sum(e, axis=-1, keepdims=True))
        out_ref[0, j * rows : (j + 1) * rows, :] = w.astype(BF16)


def softmax_weights(queries, block, keys_a, block_a, keys_b, block_b, segs_q, segs_k):
    rows = REACH
    heads = keys_a.shape[1] // HD
    return pl.pallas_call(
        scores_kernel,
        grid=(heads,),
        in_specs=[
            pl.BlockSpec((rows, GROUP * HD), lambda h: (block, h)),
            pl.BlockSpec((rows, HD), lambda h: (block_a, h)),
            pl.BlockSpec((rows, HD), lambda h: (block_b, h)),
            pl.BlockSpec((rows, 1), lambda h: (0, 0)),
            pl.BlockSpec((1, 2 * rows), lambda h: (0, 0)),
        ],
        out_specs=pl.BlockSpec((1, GROUP * rows, 2 * rows), lambda h: (h, 0, 0)),
        out_shape=jax.ShapeDtypeStruct((heads, GROUP * rows, 2 * rows), BF16),
        compiler_params=params(),
        cost_estimate=cost(
            4 * heads * GROUP * rows * rows * HD, 6 * rows * heads * GROUP * HD, 2 * heads * GROUP * rows * rows
        ),
        name="scores",
    )(queries, keys_a, keys_b, segs_q, segs_k)


def context_kernel(p0_ref, p1_ref, prev_ref, own_ref, out_ref):
    rows = prev_ref.shape[0]
    first = jnp.concatenate([prev_ref[...], own_ref[:rows, :]], axis=0)
    for block, (p_ref, values) in enumerate(((p0_ref, first), (p1_ref, own_ref[...]))):
        c = jnp.dot(p_ref[0], values, preferred_element_type=F32).astype(BF16)
        for j in range(GROUP):
            out_ref[block * rows : (block + 1) * rows, j * HD : (j + 1) * HD] = c[j * rows : (j + 1) * rows]


def contexts(p0, p1, prev, own):
    heads, _, span = p0.shape
    rows = prev.shape[0]
    weights = pl.BlockSpec((1, GROUP * rows, span), lambda h: (h, 0, 0))
    return pl.pallas_call(
        context_kernel,
        grid=(heads,),
        in_specs=[
            weights,
            weights,
            pl.BlockSpec((rows, HD), lambda h: (0, h)),
            pl.BlockSpec((2 * rows, HD), lambda h: (0, h)),
        ],
        out_specs=pl.BlockSpec((2 * rows, GROUP * HD), lambda h: (0, h)),
        out_shape=jax.ShapeDtypeStruct((2 * rows, heads * GROUP * HD), BF16),
        compiler_params=params(),
        cost_estimate=cost(4 * heads * GROUP * rows * span * HD, 12 * rows * heads * GROUP * HD),
        name="context",
    )(p0, p1, prev, own)


def after(*values):
    return lax.optimization_barrier(values)


def place(p):
    z, x = (p, 0) if p < 4 else (7 - p, 1)
    return z * 2 + x


def ring(signs):
    return [
        (y * 16 + place(p) * 2 + c, y * 16 + place((p + sign) % 8) * 2 + c)
        for y, sign in enumerate(signs)
        for p in range(8)
        for c in range(2)
    ]


def on_ring(hidden, norm_gain, key_weight, value_weight, queries, segment_ids):
    both = ("groups", "dp")
    key_way, value_way = ring((1, -1)), ring((-1, 1))
    other_group = [(i, (i + 16) % 32) for i in range(32)]
    other_core = [(i, i ^ 1) for i in range(16)]

    def send(value, way):
        return lax.ppermute(value, both, way)

    def swap(value):
        return lax.ppermute(value, "dp", other_core)

    me = lax.axis_index("dp")
    chip, core = me // 2, me % 2
    z, x = chip // 2, chip % 2
    position = jnp.where(x == 0, z, 7 - z)
    sign = jnp.where(lax.axis_index("groups") == 0, 1, -1)

    def blocks(steps):
        p = jnp.mod(position + sign * jnp.array(steps, jnp.int32), 8)
        return jnp.where(p < 4, 2 * p, 2 * (7 - p) + 1).astype(jnp.int32)

    rows = segment_ids.shape[0]
    mine, theirs = normalise(core.reshape(1).astype(jnp.int32), hidden, norm_gain)
    other = [swap(t) for t in theirs]

    k1, v1 = send(key_weight, key_way), send(value_weight, value_way)
    k1, v1, mine = after(k1, v1, mine)
    yk1 = send(k1, other_group)
    k2, v2 = send(k1, key_way), send(v1, value_way)
    behind = from_behind(segment_ids[rows - REACH :], "dp", 1)
    k2, v2, yk1, behind = after(k2, v2, yk1, behind)
    yk2, yv2 = send(k2, other_group), send(v2, other_group)
    k3, v3 = send(k2, key_way), send(v2, value_way)
    yv1 = send(v1, other_group)

    behind = jnp.where(me > 0, behind, -1)
    window = jnp.concatenate([behind, segment_ids], axis=0)
    index = jnp.arange(window.shape[0], dtype=jnp.int32)
    earlier = (window[None, :] == segment_ids[:, None]) & (index[None, :] < index[REACH:, None])
    positions = jnp.sum(earlier.astype(jnp.int32), axis=1).astype(F32)
    half = HD // 2
    freqs = 500000.0 ** (-(2.0 * jnp.arange(half, dtype=F32)) / HD)
    angles = positions[:, None] * freqs[None, :]
    cos, sin = jnp.cos(angles), jnp.sin(angles)
    cos = jnp.concatenate([cos, cos], axis=1)
    sin = jnp.concatenate([-sin, sin], axis=1)

    key_part = project(blocks([0, -1, 1, -2]), mine, other, [key_weight, k1, yk1, k2])
    k3, v3, yk2, key_part, cos, sin = after(k3, v3, yk2, key_part, cos, sin)
    k4, k3b = send(k3, key_way), send(yk2, value_way)
    v4 = send(v3, value_way)
    key_part = project(blocks([-3, 2]), mine, other, [k3, yk2], key_part)
    value_part = project(blocks([0, 1, 2, 3]), mine, other, [value_weight, v1, v2, v3])
    yv2, key_part, value_part = after(yv2, key_part, value_part)
    v3b = send(yv2, key_way)

    own_k, *other_k = project(blocks([-4, 3]), mine, other, [k4, k3b], key_part, 2)
    keys = finish_keys(own_k, [swap(o) for o in other_k], cos, sin)
    prev_keys = from_behind(keys[rows - REACH :], "dp", 1)
    segs_q = segment_ids.reshape(rows, 1)
    p1 = softmax_weights(
        queries, 1, keys, 0, keys, 1, segs_q[REACH:], segment_ids.reshape(1, rows)
    )
    value_part, p1 = after(value_part, p1)
    own_v, other_v = project(
        blocks([-2, -1, 4, -3]), mine, other, [yv2, yv1, v4, v3b], value_part
    )
    values = (own_v + swap(other_v)).astype(BF16)
    prev_values = from_behind(values[rows - REACH :], "dp", 1)
    p0 = softmax_weights(
        queries, 0, prev_keys, 0, keys, 0, segs_q[:REACH], window[: 2 * REACH].reshape(1, 2 * REACH)
    )
    return contexts(p0, p1, prev_values, values)


def rotary(block, positions):
    half = HD // 2
    freqs = 500000.0 ** (-(2.0 * jnp.arange(half, dtype=jnp.float32)) / HD)
    angles = positions[:, None] * freqs[None, :]
    cosine = jnp.cos(angles)[:, None, :]
    sine = jnp.sin(angles)[:, None, :]
    first = block[..., :half]
    second = block[..., half:]
    return jnp.concatenate(
        [first * cosine - second * sine, second * cosine + first * sine], axis=-1
    )


def on_any(hidden, norm_gain, key_weight, value_weight, queries, segment_ids):
    whole = lax.all_gather(hidden, "tensor", axis=1, tiled=True)
    states = whole.astype(jnp.float32)
    meansq = jnp.mean(states * states, axis=-1, keepdims=True)
    normed = (states * lax.rsqrt(meansq + EPS) * norm_gain.astype(jnp.float32)).astype(BF16)
    local_rows = normed.shape[0]
    head_cols = key_weight.shape[1]

    def add_rows(piece):
        return jnp.dot(normed, piece, preferred_element_type=jnp.float32)

    key_sum = add_rows(lax.all_gather(key_weight, "dp", axis=0, tiled=True))
    value_sum = add_rows(lax.all_gather(value_weight, "dp", axis=0, tiled=True))
    keys_raw = key_sum.astype(BF16)
    values = value_sum.astype(BF16)
    earlier_keys, earlier_values, earlier_segs = from_behind(
        (keys_raw, values, segment_ids), "dp", 1
    )
    earlier_count = earlier_keys.shape[0]
    has_earlier = lax.axis_index("dp") > 0
    earlier_segs = jnp.where(has_earlier, earlier_segs, -1)
    window_segs = jnp.concatenate([earlier_segs, segment_ids], axis=0)
    window_len = window_segs.shape[0]
    window_index = jnp.arange(window_len, dtype=jnp.int32)
    same_seg = window_segs[:, None] == window_segs[None, :]
    before = window_index[None, :] < window_index[:, None]
    positions = jnp.sum((same_seg & before).astype(jnp.int32), axis=1)
    heads_here = head_cols // HD
    window_raw = (
        jnp.concatenate([earlier_keys, keys_raw], axis=0)
        .astype(jnp.float32)
        .reshape(window_len, heads_here, HD)
    )
    window_keys = rotary(window_raw, positions.astype(jnp.float32)).astype(BF16)
    window_values = jnp.concatenate([earlier_values, values], axis=0).reshape(
        window_len, heads_here, HD
    )
    query_heads = queries.reshape(local_rows, heads_here, GROUP, HD)
    scale = 1.0 / HD**0.5
    scores = (
        jnp.einsum("tkgd,skd->kgts", query_heads, window_keys, preferred_element_type=jnp.float32)
        * scale
    )
    query_pos = jnp.arange(local_rows, dtype=jnp.int32)[:, None] + earlier_count
    allowed = (window_index[None, :] <= query_pos) & (segment_ids[:, None] == window_segs[None, :])
    masked = jnp.where(allowed, scores, -1e30)
    largest = jnp.max(masked, axis=-1, keepdims=True)
    expd = jnp.where(allowed, jnp.exp(masked - largest), 0.0)
    weights = (expd / jnp.sum(expd, axis=-1, keepdims=True)).astype(BF16)
    out_heads = jnp.einsum(
        "kgts,skd->tkgd", weights, window_values, preferred_element_type=jnp.float32
    )
    return out_heads.reshape(local_rows, heads_here * GROUP * HD).astype(BF16)


def solution(mesh):
    in_specs = (
        P(("groups", "dp"), "tensor"),
        P(),
        P("dp", "tensor"),
        P("dp", "tensor"),
        P(("groups", "dp"), "tensor"),
        P(("groups", "dp")),
    )
    out_specs = P(("groups", "dp"), "tensor")
    small = (mesh.shape["groups"], mesh.shape["dp"], mesh.shape["tensor"]) == (2, 16, 1)
    return jax.shard_map(
        on_ring if small else on_any,
        mesh=mesh,
        in_specs=in_specs,
        out_specs=out_specs,
        check_vma=False,
    )
```

```python
import functools

import jax
import jax.numpy as jnp
import numpy as np
from jax import lax
from jax.experimental import pallas as pl
from jax.experimental.pallas import tpu as pltpu
from jax.sharding import PartitionSpec as P

HD = 128
GROUP = 8
REACH = 128
EPS = 1e-05
F32 = jnp.float32
BF16 = jnp.bfloat16
VMEM_LIMIT = 16 * 1024 * 1024


def params():
    return pltpu.CompilerParams(vmem_limit_bytes=VMEM_LIMIT)


def cost(flops, nbytes, trans=0):
    return pl.CostEstimate(flops=flops, bytes_accessed=nbytes, transcendentals=trans)


def from_behind(value, axis, steps):
    count = lax.axis_size(axis)
    initial, last = (max(0, -steps), min(count, count - steps))
    return lax.ppermute(value, axis, [(source, source + steps) for source in range(initial, last)])


def norm_kernel(core_ref, h_ref, g_ref, mine_ref, *theirs):
    width = h_ref.shape[1]
    half = width // 16
    x = h_ref[...].astype(F32)
    meansq = jnp.sum(x * x, axis=-1, keepdims=True) * (1.0 / width)
    scale = lax.rsqrt(meansq + EPS)
    first = lax.rem(core_ref[0], 2) == 0
    for b in range(8):
        lo = slice(2 * b * half, (2 * b + 1) * half)
        hi = slice((2 * b + 1) * half, (2 * b + 2) * half)
        n_lo = h_ref[:, lo].astype(F32) * scale * g_ref[:, lo].astype(F32)
        n_hi = h_ref[:, hi].astype(F32) * scale * g_ref[:, hi].astype(F32)
        out = slice(b * half, (b + 1) * half)
        mine_ref[:, out] = jnp.where(first, n_lo, n_hi).astype(BF16)
        for step, theirs_ref in enumerate(theirs):

            @pl.when(pl.program_id(0) == step)
            def _():
                theirs_ref[:, out] = jnp.where(first, n_hi, n_lo).astype(BF16)


def normalise(core, hidden, gain):
    rows, width = hidden.shape
    step = 64
    mine = jax.ShapeDtypeStruct((rows, width // 2), BF16)
    theirs = jax.ShapeDtypeStruct((step, width // 2), BF16)
    mine, *theirs = pl.pallas_call(
        norm_kernel,
        grid_spec=pltpu.PrefetchScalarGridSpec(
            num_scalar_prefetch=1,
            grid=(rows // step,),
            in_specs=[
                pl.BlockSpec((step, width), lambda i, c: (i, 0)),
                pl.BlockSpec((1, width), lambda i, c: (0, 0)),
            ],
            out_specs=[pl.BlockSpec((step, width // 2), lambda i, c: (i, 0))]
            + [pl.BlockSpec((step, width // 2), lambda i, c: (0, 0))] * (rows // step),
        ),
        out_shape=[mine] + [theirs] * (rows // step),
        compiler_params=params(),
        cost_estimate=cost(8 * rows * width, 4 * rows * width),
        name="norm",
    )(core, hidden, gain.reshape(1, width))
    return mine, theirs


def block_at(ids_ref, step):
    z, x = lax.div(ids_ref[0], 4), lax.rem(lax.div(ids_ref[0], 2), 2)
    p = jnp.where(x == 0, z, 7 - z) + jnp.where(ids_ref[1] == 0, step, -step)
    p = jnp.where(p < 0, p + 8, p)
    p = jnp.where(p > 7, p - 8, p)
    return jnp.where(p < 4, 2 * p, 15 - 2 * p)


def project_kernel(steps, parts, carried, ids_ref, xa_ref, *refs):
    count = len(steps)
    others, refs = refs[:parts], refs[parts:]
    weights, refs = refs[:count], refs[count:]
    before, outs = refs[:carried], refs[carried:]
    total = None
    for j in range(count):
        depth = weights[j].shape[0]
        columns = pl.ds(pl.multiple_of(block_at(ids_ref, steps[j]) * depth, depth), depth)
        x = jnp.concatenate([ref[:, columns] for ref in (xa_ref, *others)], axis=0)
        part = jnp.dot(x, weights[j][...], preferred_element_type=F32)
        total = part if total is None else total + part
    held = jnp.concatenate([ref[...] for ref in before], axis=0) if carried else None
    total = held + total if carried else total
    at = 0
    for ref in outs:
        ref[...] = total[at : at + ref.shape[0]]
        at += ref.shape[0]


def project(ids, steps, xa, others, weights, before=(), split=1):
    rows = xa.shape[0]
    depth, feats = weights[0].shape
    outs = [jax.ShapeDtypeStruct((rows, feats), F32)]
    outs += [jax.ShapeDtypeStruct((rows // split, feats), F32)] * split
    whole = pl.BlockSpec(memory_space=pltpu.VMEM)
    operands = [xa, *others, *weights, *before]
    return pl.pallas_call(
        functools.partial(project_kernel, steps, len(others), len(before)),
        in_specs=[pl.BlockSpec(memory_space=pltpu.SMEM)] + [whole] * len(operands),
        out_specs=[whole] * len(outs),
        out_shape=outs,
        compiler_params=params(),
        cost_estimate=cost(
            4 * rows * depth * feats * len(weights), 2 * depth * feats * len(weights) + 4 * rows * 4096
        ),
        name="project",
    )(ids, *operands)


def tables_kernel(ids_ref, own_ref, behind_ref, freq_ref, cos_ref, sin_ref, bias_ref):
    own = own_ref[...]
    rows = own.shape[1]
    behind = jnp.where(ids_ref[0] > 0, behind_ref[:, rows - REACH :], -1)
    window = jnp.concatenate([behind, own], axis=1)
    shape = (REACH, 2 * REACH)
    r, c = lax.broadcasted_iota(jnp.int32, shape, 0), lax.broadcasted_iota(jnp.int32, shape, 1)
    freq = freq_ref[...]
    for block in range(rows // REACH):
        keys = window[:, block * REACH : (block + 2) * REACH]
        mine = jnp.sum(jnp.where(c == r + REACH, keys, 0), axis=1, keepdims=True)
        same = mine == keys
        bias_ref[block] = jnp.where(same & (c <= r + REACH), 0.0, -1e30)
        position = jnp.sum(jnp.where(same & (c < r + REACH), 1.0, 0.0), axis=1, keepdims=True)
        angle = position * freq
        at = slice(block * REACH, (block + 1) * REACH)
        sign = jnp.where(lax.broadcasted_iota(jnp.int32, (REACH, HD), 1) < HD // 2, -1.0, 1.0)
        cos_ref[at, :] = jnp.cos(angle)
        sin_ref[at, :] = jnp.sin(angle) * sign


def tables(ids, own, behind):
    rows = own.shape[0]
    half = np.arange(HD // 2, dtype=np.float32)
    freq = np.float32(500000.0) ** (-(2.0 * half) / np.float32(HD))
    freq = jnp.asarray(np.concatenate([freq, freq]).astype(np.float32).reshape(1, HD))
    whole = pl.BlockSpec(memory_space=pltpu.VMEM)
    return pl.pallas_call(
        tables_kernel,
        in_specs=[pl.BlockSpec(memory_space=pltpu.SMEM)] + [whole] * 3,
        out_specs=[whole] * 3,
        out_shape=[
            jax.ShapeDtypeStruct((rows, HD), F32),
            jax.ShapeDtypeStruct((rows, HD), F32),
            jax.ShapeDtypeStruct((rows // REACH, REACH, 2 * REACH), F32),
        ],
        compiler_params=params(),
        cost_estimate=cost(20 * rows * 2 * REACH, 16 * rows * REACH, 2 * rows * HD),
        name="tables",
    )(ids, own.reshape(1, rows), behind.reshape(1, rows), freq)


def keys_kernel(a_ref, cos_ref, sin_ref, *refs):
    cos, sin = cos_ref[...], sin_ref[...]
    others, (out_ref, tail_ref) = refs[:-2], refs[-2:]
    rows = out_ref.shape[0]
    for h in range(a_ref.shape[1] // HD):
        at = slice(h * HD, (h + 1) * HD)
        b = jnp.concatenate([ref[:, at] for ref in others], axis=0)
        raw = (a_ref[:, at] + b).astype(BF16).astype(F32)
        out = (raw * cos + pltpu.roll(raw, HD // 2, 1) * sin).astype(BF16)
        out_ref[:, at] = out
        tail_ref[:, at] = out[rows - REACH :]


def values_kernel(a_ref, *refs):
    others, (out_ref, tail_ref) = refs[:-2], refs[-2:]
    rows = out_ref.shape[0]
    out = (a_ref[...] + jnp.concatenate([ref[...] for ref in others], axis=0)).astype(BF16)
    out_ref[...] = out
    tail_ref[...] = out[rows - REACH :]


def finish(kernel, name, *operands):
    rows, feats = operands[0].shape
    return pl.pallas_call(
        kernel,
        out_shape=[
            jax.ShapeDtypeStruct((rows, feats), BF16),
            jax.ShapeDtypeStruct((REACH, feats), BF16),
        ],
        compiler_params=params(),
        cost_estimate=cost(6 * rows * feats, 10 * rows * feats),
        name=name,
    )(*operands)


def scores_kernel(q_ref, ka_ref, kb_ref, bias_ref, out_ref):
    rows = q_ref.shape[0]
    keys = jnp.concatenate([ka_ref[...], kb_ref[...]], axis=0)
    bias = bias_ref[0]
    scale = 1.0 / HD**0.5
    for j in range(GROUP):
        q = q_ref[:, j * HD : (j + 1) * HD]
        s = lax.dot_general(q, keys, (((1,), (1,)), ((), ())), preferred_element_type=F32)
        s = s * scale + bias
        e = jnp.exp(s - jnp.max(s, axis=-1, keepdims=True))
        w = e * (1.0 / jnp.sum(e, axis=-1, keepdims=True))
        out_ref[0, j * rows : (j + 1) * rows, :] = w.astype(BF16)


def softmax_weights(queries, block, keys_a, block_a, keys_b, block_b, bias):
    rows = REACH
    heads = keys_a.shape[1] // HD
    return pl.pallas_call(
        scores_kernel,
        grid=(heads,),
        in_specs=[
            pl.BlockSpec((rows, GROUP * HD), lambda h: (block, h)),
            pl.BlockSpec((rows, HD), lambda h: (block_a, h)),
            pl.BlockSpec((rows, HD), lambda h: (block_b, h)),
            pl.BlockSpec((1, rows, 2 * rows), lambda h: (block, 0, 0)),
        ],
        out_specs=pl.BlockSpec((1, GROUP * rows, 2 * rows), lambda h: (h, 0, 0)),
        out_shape=jax.ShapeDtypeStruct((heads, GROUP * rows, 2 * rows), BF16),
        compiler_params=params(),
        cost_estimate=cost(
            4 * heads * GROUP * rows * rows * HD, 6 * rows * heads * GROUP * HD, 2 * heads * GROUP * rows * rows
        ),
        name="scores",
    )(queries, keys_a, keys_b, bias)


def context_kernel(p0_ref, p1_ref, prev_ref, own_ref, out_ref):
    rows = prev_ref.shape[0]
    first = jnp.concatenate([prev_ref[...], own_ref[:rows, :]], axis=0)
    for block, (p_ref, values) in enumerate(((p0_ref, first), (p1_ref, own_ref[...]))):
        c = jnp.dot(p_ref[0], values, preferred_element_type=F32).astype(BF16)
        for j in range(GROUP):
            out_ref[block * rows : (block + 1) * rows, j * HD : (j + 1) * HD] = c[j * rows : (j + 1) * rows]


def contexts(p0, p1, prev, own):
    heads, _, span = p0.shape
    rows = prev.shape[0]
    weights = pl.BlockSpec((1, GROUP * rows, span), lambda h: (h, 0, 0))
    return pl.pallas_call(
        context_kernel,
        grid=(heads,),
        in_specs=[
            weights,
            weights,
            pl.BlockSpec((rows, HD), lambda h: (0, h)),
            pl.BlockSpec((2 * rows, HD), lambda h: (0, h)),
        ],
        out_specs=pl.BlockSpec((2 * rows, GROUP * HD), lambda h: (0, h)),
        out_shape=jax.ShapeDtypeStruct((2 * rows, heads * GROUP * HD), BF16),
        compiler_params=params(),
        cost_estimate=cost(4 * heads * GROUP * rows * span * HD, 12 * rows * heads * GROUP * HD),
        name="context",
    )(p0, p1, prev, own)


def after(*values):
    return lax.optimization_barrier(values)


def place(p):
    z, x = (p, 0) if p < 4 else (7 - p, 1)
    return z * 2 + x


def ring(signs):
    return [
        (y * 16 + place(p) * 2 + c, y * 16 + place((p + sign) % 8) * 2 + c)
        for y, sign in enumerate(signs)
        for p in range(8)
        for c in range(2)
    ]


def on_ring(hidden, norm_gain, key_weight, value_weight, queries, segment_ids):
    both = ("groups", "dp")
    key_way, value_way = ring((1, -1)), ring((-1, 1))
    other_group = [(i, (i + 16) % 32) for i in range(32)]
    other_core = [(i, i ^ 1) for i in range(16)]

    def send(value, way):
        return lax.ppermute(value, both, way)

    def swap(value):
        return lax.ppermute(value, "dp", other_core)

    ids = jnp.stack([lax.axis_index("dp"), lax.axis_index("groups")]).astype(jnp.int32)
    mine, theirs = normalise(ids, hidden, norm_gain)
    other = [swap(t) for t in theirs]
    behind = from_behind(segment_ids, "dp", 1)

    k1, v1 = send(key_weight, key_way), send(value_weight, value_way)
    k1, v1, mine = after(k1, v1, mine)
    yk1 = send(k1, other_group)
    k2, v2 = send(k1, key_way), send(v1, value_way)
    k2, v2, yk1, behind = after(k2, v2, yk1, behind)
    yk2, yv2 = send(k2, other_group), send(v2, other_group)
    k3, v3 = send(k2, key_way), send(v2, value_way)
    yv1 = send(v1, other_group)

    cos, sin, bias = tables(ids, segment_ids, behind)
    key_part = project(ids, (0, -1, 1, -2), mine, other, [key_weight, k1, yk1, k2])
    k3, v3, yk2, key_part, cos, sin, bias = after(k3, v3, yk2, key_part, cos, sin, bias)
    k4, k3b = send(k3, key_way), send(yk2, value_way)
    v4 = send(v3, value_way)
    key_part = project(ids, (-3, 2), mine, other, [k3, yk2], key_part)
    value_part = project(ids, (0, 1, 2, 3), mine, other, [value_weight, v1, v2, v3])
    yv2, key_part, value_part = after(yv2, key_part, value_part)
    v3b = send(yv2, key_way)

    own_k, *other_k = project(ids, (-4, 3), mine, other, [k4, k3b], key_part, 2)
    keys, tail = finish(keys_kernel, "keys", own_k, cos, sin, *[swap(o) for o in other_k])
    prev_keys = from_behind(tail, "dp", 1)
    p1 = softmax_weights(queries, 1, keys, 0, keys, 1, bias)
    value_part, p1 = after(value_part, p1)
    own_v, other_v = project(
        ids, (-2, -1, 4, -3), mine, other, [yv2, yv1, v4, v3b], value_part
    )
    values, tail = finish(values_kernel, "values", own_v, swap(other_v))
    prev_values = from_behind(tail, "dp", 1)
    p0 = softmax_weights(queries, 0, prev_keys, 0, keys, 0, bias)
    return contexts(p0, p1, prev_values, values)


def rotary(block, positions):
    half = HD // 2
    freqs = 500000.0 ** (-(2.0 * jnp.arange(half, dtype=jnp.float32)) / HD)
    angles = positions[:, None] * freqs[None, :]
    cosine = jnp.cos(angles)[:, None, :]
    sine = jnp.sin(angles)[:, None, :]
    first = block[..., :half]
    second = block[..., half:]
    return jnp.concatenate(
        [first * cosine - second * sine, second * cosine + first * sine], axis=-1
    )


def on_any(hidden, norm_gain, key_weight, value_weight, queries, segment_ids):
    whole = lax.all_gather(hidden, "tensor", axis=1, tiled=True)
    states = whole.astype(jnp.float32)
    meansq = jnp.mean(states * states, axis=-1, keepdims=True)
    normed = (states * lax.rsqrt(meansq + EPS) * norm_gain.astype(jnp.float32)).astype(BF16)
    local_rows = normed.shape[0]
    head_cols = key_weight.shape[1]

    def add_rows(piece):
        return jnp.dot(normed, piece, preferred_element_type=jnp.float32)

    key_sum = add_rows(lax.all_gather(key_weight, "dp", axis=0, tiled=True))
    value_sum = add_rows(lax.all_gather(value_weight, "dp", axis=0, tiled=True))
    keys_raw = key_sum.astype(BF16)
    values = value_sum.astype(BF16)
    earlier_keys, earlier_values, earlier_segs = from_behind(
        (keys_raw, values, segment_ids), "dp", 1
    )
    earlier_count = earlier_keys.shape[0]
    has_earlier = lax.axis_index("dp") > 0
    earlier_segs = jnp.where(has_earlier, earlier_segs, -1)
    window_segs = jnp.concatenate([earlier_segs, segment_ids], axis=0)
    window_len = window_segs.shape[0]
    window_index = jnp.arange(window_len, dtype=jnp.int32)
    same_seg = window_segs[:, None] == window_segs[None, :]
    before = window_index[None, :] < window_index[:, None]
    positions = jnp.sum((same_seg & before).astype(jnp.int32), axis=1)
    heads_here = head_cols // HD
    window_raw = (
        jnp.concatenate([earlier_keys, keys_raw], axis=0)
        .astype(jnp.float32)
        .reshape(window_len, heads_here, HD)
    )
    window_keys = rotary(window_raw, positions.astype(jnp.float32)).astype(BF16)
    window_values = jnp.concatenate([earlier_values, values], axis=0).reshape(
        window_len, heads_here, HD
    )
    query_heads = queries.reshape(local_rows, heads_here, GROUP, HD)
    scale = 1.0 / HD**0.5
    scores = (
        jnp.einsum("tkgd,skd->kgts", query_heads, window_keys, preferred_element_type=jnp.float32)
        * scale
    )
    query_pos = jnp.arange(local_rows, dtype=jnp.int32)[:, None] + earlier_count
    allowed = (window_index[None, :] <= query_pos) & (segment_ids[:, None] == window_segs[None, :])
    masked = jnp.where(allowed, scores, -1e30)
    largest = jnp.max(masked, axis=-1, keepdims=True)
    expd = jnp.where(allowed, jnp.exp(masked - largest), 0.0)
    weights = (expd / jnp.sum(expd, axis=-1, keepdims=True)).astype(BF16)
    out_heads = jnp.einsum(
        "kgts,skd->tkgd", weights, window_values, preferred_element_type=jnp.float32
    )
    return out_heads.reshape(local_rows, heads_here * GROUP * HD).astype(BF16)


def solution(mesh):
    in_specs = (
        P(("groups", "dp"), "tensor"),
        P(),
        P("dp", "tensor"),
        P("dp", "tensor"),
        P(("groups", "dp"), "tensor"),
        P(("groups", "dp")),
    )
    out_specs = P(("groups", "dp"), "tensor")
    small = (mesh.shape["groups"], mesh.shape["dp"], mesh.shape["tensor"]) == (2, 16, 1)
    return jax.shard_map(
        on_ring if small else on_any,
        mesh=mesh,
        in_specs=in_specs,
        out_specs=out_specs,
        check_vma=False,
    )
```

```python
import functools

import jax
import jax.numpy as jnp
import numpy as np
from jax import lax
from jax.experimental import pallas as pl
from jax.experimental.pallas import tpu as pltpu
from jax.sharding import PartitionSpec as P

HD = 128
GROUP = 8
REACH = 128
EPS = 1e-05
F32 = jnp.float32
BF16 = jnp.bfloat16
VMEM_LIMIT = 16 * 1024 * 1024


def params():
    return pltpu.CompilerParams(vmem_limit_bytes=VMEM_LIMIT)


def cost(flops, nbytes, trans=0):
    return pl.CostEstimate(flops=flops, bytes_accessed=nbytes, transcendentals=trans)


def from_behind(value, axis, steps):
    count = lax.axis_size(axis)
    initial, last = (max(0, -steps), min(count, count - steps))
    return lax.ppermute(value, axis, [(source, source + steps) for source in range(initial, last)])


def norm_kernel(core_ref, h_ref, g_ref, mine_ref, *theirs):
    width = h_ref.shape[1]
    half = width // 16
    x = h_ref[...].astype(F32)
    meansq = jnp.sum(x * x, axis=-1, keepdims=True) * (1.0 / width)
    scale = lax.rsqrt(meansq + EPS)
    first = lax.rem(core_ref[0], 2) == 0
    for b in range(8):
        lo = slice(2 * b * half, (2 * b + 1) * half)
        hi = slice((2 * b + 1) * half, (2 * b + 2) * half)
        n_lo = h_ref[:, lo].astype(F32) * scale * g_ref[:, lo].astype(F32)
        n_hi = h_ref[:, hi].astype(F32) * scale * g_ref[:, hi].astype(F32)
        out = slice(b * half, (b + 1) * half)
        mine_ref[:, out] = jnp.where(first, n_lo, n_hi).astype(BF16)
        other = jnp.where(first, n_hi, n_lo).astype(BF16)
        for part, theirs_ref in enumerate(theirs):

            @pl.when(pl.program_id(0) // (pl.num_programs(0) // len(theirs)) == part)
            def _():
                theirs_ref[:, out] = other


def normalise(core, hidden, gain):
    rows, width = hidden.shape
    step = 64
    mine = jax.ShapeDtypeStruct((rows, width // 2), BF16)
    parts = 2
    theirs = jax.ShapeDtypeStruct((rows // parts, width // 2), BF16)
    last = rows // step // parts - 1
    mine, *theirs = pl.pallas_call(
        norm_kernel,
        grid_spec=pltpu.PrefetchScalarGridSpec(
            num_scalar_prefetch=1,
            grid=(rows // step,),
            in_specs=[
                pl.BlockSpec((step, width), lambda i, c: (i, 0)),
                pl.BlockSpec((1, width), lambda i, c: (0, 0)),
            ],
            out_specs=[pl.BlockSpec((step, width // 2), lambda i, c: (i, 0))]
            + [
                pl.BlockSpec(
                    (step, width // 2),
                    functools.partial(lambda p, i, c: (jnp.clip(i - p * (last + 1), 0, last), 0), p),
                )
                for p in range(parts)
            ],
        ),
        out_shape=[mine] + [theirs] * parts,
        compiler_params=params(),
        cost_estimate=cost(8 * rows * width, 4 * rows * width),
        name="norm",
    )(core, hidden, gain.reshape(1, width))
    return mine, theirs


def block_at(ids_ref, step):
    z, x = lax.div(ids_ref[0], 4), lax.rem(lax.div(ids_ref[0], 2), 2)
    p = jnp.where(x == 0, z, 7 - z) + jnp.where(ids_ref[1] == 0, step, -step)
    p = jnp.where(p < 0, p + 8, p)
    p = jnp.where(p > 7, p - 8, p)
    return jnp.where(p < 4, 2 * p, 15 - 2 * p)


def project_kernel(steps, parts, carried, ids_ref, xa_ref, *refs):
    count = len(steps)
    others, refs = refs[:parts], refs[parts:]
    weights, refs = refs[:count], refs[count:]
    before, outs = refs[:carried], refs[carried:]
    total = None
    for j in range(count):
        depth = weights[j].shape[0]
        columns = pl.ds(pl.multiple_of(block_at(ids_ref, steps[j]) * depth, depth), depth)
        x = jnp.concatenate([ref[:, columns] for ref in (xa_ref, *others)], axis=0)
        part = jnp.dot(x, weights[j][...], preferred_element_type=F32)
        total = part if total is None else total + part
    held = jnp.concatenate([ref[...] for ref in before], axis=0) if carried else None
    total = held + total if carried else total
    at = 0
    for ref in outs:
        ref[...] = total[at : at + ref.shape[0]]
        at += ref.shape[0]


def project(ids, steps, xa, others, weights, before=(), split=1):
    rows = xa.shape[0]
    depth, feats = weights[0].shape
    outs = [jax.ShapeDtypeStruct((rows, feats), F32)]
    outs += [jax.ShapeDtypeStruct((rows // split, feats), F32)] * split
    whole = pl.BlockSpec(memory_space=pltpu.VMEM)
    operands = [xa, *others, *weights, *before]
    return pl.pallas_call(
        functools.partial(project_kernel, steps, len(others), len(before)),
        in_specs=[pl.BlockSpec(memory_space=pltpu.SMEM)] + [whole] * len(operands),
        out_specs=[whole] * len(outs),
        out_shape=outs,
        compiler_params=params(),
        cost_estimate=cost(
            4 * rows * depth * feats * len(weights), 2 * depth * feats * len(weights) + 4 * rows * 4096
        ),
        name="project",
    )(ids, *operands)


def tables_kernel(ids_ref, own_ref, behind_ref, freq_ref, cos_ref, sin_ref, bias_ref):
    own = own_ref[...]
    rows = own.shape[1]
    behind = jnp.where(ids_ref[0] > 0, behind_ref[:, rows - REACH :], -1)
    window = jnp.concatenate([behind, own], axis=1)
    shape = (REACH, 2 * REACH)
    r, c = lax.broadcasted_iota(jnp.int32, shape, 0), lax.broadcasted_iota(jnp.int32, shape, 1)
    freq = freq_ref[...]
    for block in range(rows // REACH):
        keys = window[:, block * REACH : (block + 2) * REACH]
        mine = jnp.sum(jnp.where(c == r + REACH, keys, 0), axis=1, keepdims=True)
        same = mine == keys
        bias_ref[block] = jnp.where(same & (c <= r + REACH), 0.0, -1e30)
        position = jnp.sum(jnp.where(same & (c < r + REACH), 1.0, 0.0), axis=1, keepdims=True)
        angle = position * freq
        at = slice(block * REACH, (block + 1) * REACH)
        sign = jnp.where(lax.broadcasted_iota(jnp.int32, (REACH, HD), 1) < HD // 2, -1.0, 1.0)
        cos_ref[at, :] = jnp.cos(angle)
        sin_ref[at, :] = jnp.sin(angle) * sign


def tables(ids, own, behind):
    rows = own.shape[0]
    half = np.arange(HD // 2, dtype=np.float32)
    freq = np.float32(500000.0) ** (-(2.0 * half) / np.float32(HD))
    freq = jnp.asarray(np.concatenate([freq, freq]).astype(np.float32).reshape(1, HD))
    whole = pl.BlockSpec(memory_space=pltpu.VMEM)
    return pl.pallas_call(
        tables_kernel,
        in_specs=[pl.BlockSpec(memory_space=pltpu.SMEM)] + [whole] * 3,
        out_specs=[whole] * 3,
        out_shape=[
            jax.ShapeDtypeStruct((rows, HD), F32),
            jax.ShapeDtypeStruct((rows, HD), F32),
            jax.ShapeDtypeStruct((rows // REACH, REACH, 2 * REACH), F32),
        ],
        compiler_params=params(),
        cost_estimate=cost(20 * rows * 2 * REACH, 16 * rows * REACH, 2 * rows * HD),
        name="tables",
    )(ids, own.reshape(1, rows), behind.reshape(1, rows), freq)


def keys_kernel(a_ref, cos_ref, sin_ref, *refs):
    cos, sin = cos_ref[...], sin_ref[...]
    others, (out_ref, tail_ref) = refs[:-2], refs[-2:]
    rows = out_ref.shape[0]
    for h in range(a_ref.shape[1] // HD):
        at = slice(h * HD, (h + 1) * HD)
        b = jnp.concatenate([ref[:, at] for ref in others], axis=0)
        raw = (a_ref[:, at] + b).astype(BF16).astype(F32)
        out = (raw * cos + pltpu.roll(raw, HD // 2, 1) * sin).astype(BF16)
        out_ref[:, at] = out
        tail_ref[:, at] = out[rows - REACH :]


def values_kernel(a_ref, *refs):
    others, (out_ref, tail_ref) = refs[:-2], refs[-2:]
    rows = out_ref.shape[0]
    out = (a_ref[...] + jnp.concatenate([ref[...] for ref in others], axis=0)).astype(BF16)
    out_ref[...] = out
    tail_ref[...] = out[rows - REACH :]


def finish(kernel, name, *operands):
    rows, feats = operands[0].shape
    return pl.pallas_call(
        kernel,
        out_shape=[
            jax.ShapeDtypeStruct((rows, feats), BF16),
            jax.ShapeDtypeStruct((REACH, feats), BF16),
        ],
        compiler_params=params(),
        cost_estimate=cost(6 * rows * feats, 10 * rows * feats),
        name=name,
    )(*operands)


def scores_kernel(q_ref, ka_ref, kb_ref, bias_ref, out_ref):
    rows = q_ref.shape[0]
    keys = jnp.concatenate([ka_ref[...], kb_ref[...]], axis=0)
    bias = bias_ref[0]
    scale = 1.0 / HD**0.5
    for j in range(GROUP):
        q = q_ref[:, j * HD : (j + 1) * HD]
        s = lax.dot_general(q, keys, (((1,), (1,)), ((), ())), preferred_element_type=F32)
        s = s * scale + bias
        e = jnp.exp(s - jnp.max(s, axis=-1, keepdims=True))
        w = e * (1.0 / jnp.sum(e, axis=-1, keepdims=True))
        out_ref[0, j * rows : (j + 1) * rows, :] = w.astype(BF16)


def softmax_weights(queries, block, keys_a, block_a, keys_b, block_b, bias):
    rows = REACH
    heads = keys_a.shape[1] // HD
    return pl.pallas_call(
        scores_kernel,
        grid=(heads,),
        in_specs=[
            pl.BlockSpec((rows, GROUP * HD), lambda h: (block, h)),
            pl.BlockSpec((rows, HD), lambda h: (block_a, h)),
            pl.BlockSpec((rows, HD), lambda h: (block_b, h)),
            pl.BlockSpec((1, rows, 2 * rows), lambda h: (block, 0, 0)),
        ],
        out_specs=pl.BlockSpec((1, GROUP * rows, 2 * rows), lambda h: (h, 0, 0)),
        out_shape=jax.ShapeDtypeStruct((heads, GROUP * rows, 2 * rows), BF16),
        compiler_params=params(),
        cost_estimate=cost(
            4 * heads * GROUP * rows * rows * HD, 6 * rows * heads * GROUP * HD, 2 * heads * GROUP * rows * rows
        ),
        name="scores",
    )(queries, keys_a, keys_b, bias)


def context_kernel(p_ref, va_ref, vb_ref, *refs):
    out_ref = refs[-1]
    rows = va_ref.shape[0]
    values = jnp.concatenate([va_ref[...], vb_ref[...]], axis=0)
    c = jnp.dot(p_ref[0], values, preferred_element_type=F32).astype(BF16)
    for j in range(GROUP):
        out_ref[:, j * HD : (j + 1) * HD] = c[j * rows : (j + 1) * rows]


def contexts(block, weights, values_a, block_a, values_b, block_b, out=None):
    heads, _, span = weights.shape
    rows = REACH
    more = () if out is None else (out,)
    return pl.pallas_call(
        context_kernel,
        grid=(heads,),
        in_specs=[
            pl.BlockSpec((1, GROUP * rows, span), lambda h: (h, 0, 0)),
            pl.BlockSpec((rows, HD), lambda h: (block_a, h)),
            pl.BlockSpec((rows, HD), lambda h: (block_b, h)),
        ]
        + [pl.BlockSpec(memory_space=pl.ANY)] * len(more),
        out_specs=pl.BlockSpec((rows, GROUP * HD), lambda h: (block, h)),
        out_shape=jax.ShapeDtypeStruct((2 * rows, heads * GROUP * HD), BF16),
        input_output_aliases={3: 0} if more else {},
        compiler_params=params(),
        cost_estimate=cost(2 * heads * GROUP * rows * span * HD, 6 * rows * heads * GROUP * HD),
        name="context",
    )(weights, values_a, values_b, *more)


def after(*values):
    return lax.optimization_barrier(values)


def place(p):
    z, x = (p, 0) if p < 4 else (7 - p, 1)
    return z * 2 + x


def ring(signs):
    return [
        (y * 16 + place(p) * 2 + c, y * 16 + place((p + sign) % 8) * 2 + c)
        for y, sign in enumerate(signs)
        for p in range(8)
        for c in range(2)
    ]


def on_ring(hidden, norm_gain, key_weight, value_weight, queries, segment_ids):
    both = ("groups", "dp")
    key_way, value_way = ring((1, -1)), ring((-1, 1))
    other_group = [(i, (i + 16) % 32) for i in range(32)]
    other_core = [(i, i ^ 1) for i in range(16)]

    def send(value, way):
        return lax.ppermute(value, both, way)

    def swap(value):
        return lax.ppermute(value, "dp", other_core)

    ids = jnp.stack([lax.axis_index("dp"), lax.axis_index("groups")]).astype(jnp.int32)
    mine, theirs = normalise(ids, hidden, norm_gain)
    other = [swap(t) for t in theirs]
    k1, v1 = send(key_weight, key_way), send(value_weight, value_way)
    k1, v1, mine = after(k1, v1, mine)
    yk1 = send(k1, other_group)
    k2, v2 = send(k1, key_way), send(v1, value_way)
    k2, v2, yk1 = after(k2, v2, yk1)
    yk2, yv2 = send(k2, other_group), send(v2, other_group)
    k3, v3 = send(k2, key_way), send(v2, value_way)
    yv1 = send(v1, other_group)

    behind = from_behind(segment_ids, "dp", 1)
    key_part = project(ids, (0, -1, 1, -2), mine, other, [key_weight, k1, yk1, k2])
    k3, v3, yk2, key_part, behind = after(k3, v3, yk2, key_part, behind)
    k4, k3b = send(k3, key_way), send(yk2, value_way)
    v4 = send(v3, value_way)
    key_part = project(ids, (-3, 2), mine, other, [k3, yk2], key_part)
    value_part = project(ids, (0, 1, 2, 3), mine, other, [value_weight, v1, v2, v3])
    cos, sin, bias = tables(ids, segment_ids, behind)
    yv2, key_part, value_part, cos, sin, bias = after(yv2, key_part, value_part, cos, sin, bias)
    v3b = send(yv2, key_way)

    own_k, *other_k = project(ids, (-4, 3), mine, other, [k4, k3b], key_part, 2)
    keys, tail = finish(keys_kernel, "keys", own_k, cos, sin, *[swap(o) for o in other_k])
    prev_keys = from_behind(tail, "dp", 1)
    p1 = softmax_weights(queries, 1, keys, 0, keys, 1, bias)
    value_part, p1, prev_keys = after(value_part, p1, prev_keys)
    own_v, other_v = project(
        ids, (-2, -1, 4, -3), mine, other, [yv2, yv1, v4, v3b], value_part
    )
    p0 = softmax_weights(queries, 0, prev_keys, 0, keys, 0, bias)
    other_v, p0 = after(swap(other_v), p0)
    values, tail = finish(values_kernel, "values", own_v, other_v)
    prev_values = from_behind(tail, "dp", 1)
    later = contexts(1, p1, values, 0, values, 1)
    return contexts(0, p0, prev_values, 0, values, 0, later)


def rotary(block, positions):
    half = HD // 2
    freqs = 500000.0 ** (-(2.0 * jnp.arange(half, dtype=jnp.float32)) / HD)
    angles = positions[:, None] * freqs[None, :]
    cosine = jnp.cos(angles)[:, None, :]
    sine = jnp.sin(angles)[:, None, :]
    first = block[..., :half]
    second = block[..., half:]
    return jnp.concatenate(
        [first * cosine - second * sine, second * cosine + first * sine], axis=-1
    )


def on_any(hidden, norm_gain, key_weight, value_weight, queries, segment_ids):
    whole = lax.all_gather(hidden, "tensor", axis=1, tiled=True)
    states = whole.astype(jnp.float32)
    meansq = jnp.mean(states * states, axis=-1, keepdims=True)
    normed = (states * lax.rsqrt(meansq + EPS) * norm_gain.astype(jnp.float32)).astype(BF16)
    local_rows = normed.shape[0]
    head_cols = key_weight.shape[1]

    def add_rows(piece):
        return jnp.dot(normed, piece, preferred_element_type=jnp.float32)

    key_sum = add_rows(lax.all_gather(key_weight, "dp", axis=0, tiled=True))
    value_sum = add_rows(lax.all_gather(value_weight, "dp", axis=0, tiled=True))
    keys_raw = key_sum.astype(BF16)
    values = value_sum.astype(BF16)
    earlier_keys, earlier_values, earlier_segs = from_behind(
        (keys_raw, values, segment_ids), "dp", 1
    )
    earlier_count = earlier_keys.shape[0]
    has_earlier = lax.axis_index("dp") > 0
    earlier_segs = jnp.where(has_earlier, earlier_segs, -1)
    window_segs = jnp.concatenate([earlier_segs, segment_ids], axis=0)
    window_len = window_segs.shape[0]
    window_index = jnp.arange(window_len, dtype=jnp.int32)
    same_seg = window_segs[:, None] == window_segs[None, :]
    before = window_index[None, :] < window_index[:, None]
    positions = jnp.sum((same_seg & before).astype(jnp.int32), axis=1)
    heads_here = head_cols // HD
    window_raw = (
        jnp.concatenate([earlier_keys, keys_raw], axis=0)
        .astype(jnp.float32)
        .reshape(window_len, heads_here, HD)
    )
    window_keys = rotary(window_raw, positions.astype(jnp.float32)).astype(BF16)
    window_values = jnp.concatenate([earlier_values, values], axis=0).reshape(
        window_len, heads_here, HD
    )
    query_heads = queries.reshape(local_rows, heads_here, GROUP, HD)
    scale = 1.0 / HD**0.5
    scores = (
        jnp.einsum("tkgd,skd->kgts", query_heads, window_keys, preferred_element_type=jnp.float32)
        * scale
    )
    query_pos = jnp.arange(local_rows, dtype=jnp.int32)[:, None] + earlier_count
    allowed = (window_index[None, :] <= query_pos) & (segment_ids[:, None] == window_segs[None, :])
    masked = jnp.where(allowed, scores, -1e30)
    largest = jnp.max(masked, axis=-1, keepdims=True)
    expd = jnp.where(allowed, jnp.exp(masked - largest), 0.0)
    weights = (expd / jnp.sum(expd, axis=-1, keepdims=True)).astype(BF16)
    out_heads = jnp.einsum(
        "kgts,skd->tkgd", weights, window_values, preferred_element_type=jnp.float32
    )
    return out_heads.reshape(local_rows, heads_here * GROUP * HD).astype(BF16)


def solution(mesh):
    in_specs = (
        P(("groups", "dp"), "tensor"),
        P(),
        P("dp", "tensor"),
        P("dp", "tensor"),
        P(("groups", "dp"), "tensor"),
        P(("groups", "dp")),
    )
    out_specs = P(("groups", "dp"), "tensor")
    small = (mesh.shape["groups"], mesh.shape["dp"], mesh.shape["tensor"]) == (2, 16, 1)
    return jax.shard_map(
        on_ring if small else on_any,
        mesh=mesh,
        in_specs=in_specs,
        out_specs=out_specs,
        check_vma=False,
    )
```

```python
import functools

import jax
import jax.numpy as jnp
import numpy as np
from jax import lax
from jax.experimental import pallas as pl
from jax.experimental.pallas import tpu as pltpu
from jax.sharding import PartitionSpec as P

HD = 128
GROUP = 8
REACH = 128
EPS = 1e-05
F32 = jnp.float32
BF16 = jnp.bfloat16
VMEM_LIMIT = 16 * 1024 * 1024


def params():
    return pltpu.CompilerParams(vmem_limit_bytes=VMEM_LIMIT)


def cost(flops, nbytes, trans=0):
    return pl.CostEstimate(flops=flops, bytes_accessed=nbytes, transcendentals=trans)


def from_behind(value, axis, steps):
    count = lax.axis_size(axis)
    initial, last = (max(0, -steps), min(count, count - steps))
    return lax.ppermute(value, axis, [(source, source + steps) for source in range(initial, last)])


def norm_kernel(core_ref, h_ref, g_ref, mine_ref, *theirs):
    width = h_ref.shape[1]
    half = width // 16
    x = h_ref[...].astype(F32)
    meansq = jnp.sum(x * x, axis=-1, keepdims=True) * (1.0 / width)
    scale = lax.rsqrt(meansq + EPS)
    first = lax.rem(core_ref[0], 2) == 0
    for b in range(8):
        lo = slice(2 * b * half, (2 * b + 1) * half)
        hi = slice((2 * b + 1) * half, (2 * b + 2) * half)
        n_lo = h_ref[:, lo].astype(F32) * scale * g_ref[:, lo].astype(F32)
        n_hi = h_ref[:, hi].astype(F32) * scale * g_ref[:, hi].astype(F32)
        out = slice(b * half, (b + 1) * half)
        mine_ref[:, out] = jnp.where(first, n_lo, n_hi).astype(BF16)
        other = jnp.where(first, n_hi, n_lo).astype(BF16)
        for part, theirs_ref in enumerate(theirs):

            @pl.when(pl.program_id(0) // (pl.num_programs(0) // len(theirs)) == part)
            def _():
                theirs_ref[:, out] = other


def normalise(core, hidden, gain):
    rows, width = hidden.shape
    step = 64
    mine = jax.ShapeDtypeStruct((rows, width // 2), BF16)
    parts = 2
    theirs = jax.ShapeDtypeStruct((rows // parts, width // 2), BF16)
    last = rows // step // parts - 1
    mine, *theirs = pl.pallas_call(
        norm_kernel,
        grid_spec=pltpu.PrefetchScalarGridSpec(
            num_scalar_prefetch=1,
            grid=(rows // step,),
            in_specs=[
                pl.BlockSpec((step, width), lambda i, c: (i, 0)),
                pl.BlockSpec((1, width), lambda i, c: (0, 0)),
            ],
            out_specs=[pl.BlockSpec((step, width // 2), lambda i, c: (i, 0))]
            + [
                pl.BlockSpec(
                    (step, width // 2),
                    functools.partial(lambda p, i, c: (jnp.clip(i - p * (last + 1), 0, last), 0), p),
                )
                for p in range(parts)
            ],
        ),
        out_shape=[mine] + [theirs] * parts,
        compiler_params=params(),
        cost_estimate=cost(8 * rows * width, 4 * rows * width),
        name="norm",
    )(core, hidden, gain.reshape(1, width))
    return mine, theirs


def block_at(ids_ref, step):
    z, x = lax.div(ids_ref[0], 4), lax.rem(lax.div(ids_ref[0], 2), 2)
    p = jnp.where(x == 0, z, 7 - z) + jnp.where(ids_ref[1] == 0, step, -step)
    p = jnp.where(p < 0, p + 8, p)
    p = jnp.where(p > 7, p - 8, p)
    return jnp.where(p < 4, 2 * p, 15 - 2 * p)


def project_kernel(steps, parts, carried, ids_ref, xa_ref, *refs):
    count = len(steps)
    others, refs = refs[:parts], refs[parts:]
    weights, refs = refs[:count], refs[count:]
    before, outs = refs[:carried], refs[carried:]
    total = None
    for j in range(count):
        depth = weights[j].shape[0]
        columns = pl.ds(pl.multiple_of(block_at(ids_ref, steps[j]) * depth, depth), depth)
        x = jnp.concatenate([ref[:, columns] for ref in (xa_ref, *others)], axis=0)
        part = jnp.dot(x, weights[j][...], preferred_element_type=F32)
        total = part if total is None else total + part
    held = jnp.concatenate([ref[...] for ref in before], axis=0) if carried else None
    total = held + total if carried else total
    at = 0
    for ref in outs:
        ref[...] = total[at : at + ref.shape[0]]
        at += ref.shape[0]


def project(ids, steps, xa, others, weights, before=(), split=1):
    rows = xa.shape[0]
    depth, feats = weights[0].shape
    outs = [jax.ShapeDtypeStruct((rows, feats), F32)]
    outs += [jax.ShapeDtypeStruct((rows // split, feats), F32)] * split
    whole = pl.BlockSpec(memory_space=pltpu.VMEM)
    operands = [xa, *others, *weights, *before]
    return pl.pallas_call(
        functools.partial(project_kernel, steps, len(others), len(before)),
        in_specs=[pl.BlockSpec(memory_space=pltpu.SMEM)] + [whole] * len(operands),
        out_specs=[whole] * len(outs),
        out_shape=outs,
        compiler_params=params(),
        cost_estimate=cost(
            4 * rows * depth * feats * len(weights), 2 * depth * feats * len(weights) + 4 * rows * 4096
        ),
        name="project",
    )(ids, *operands)


def tables_kernel(ids_ref, own_ref, behind_ref, freq_ref, cos_ref, sin_ref, bias_ref):
    own = own_ref[...]
    rows = own.shape[1]
    behind = jnp.where(ids_ref[0] > 0, behind_ref[:, rows - REACH :], -1)
    window = jnp.concatenate([behind, own], axis=1)
    shape = (REACH, 2 * REACH)
    r, c = lax.broadcasted_iota(jnp.int32, shape, 0), lax.broadcasted_iota(jnp.int32, shape, 1)
    freq = freq_ref[...]
    for block in range(rows // REACH):
        keys = window[:, block * REACH : (block + 2) * REACH]
        mine = jnp.sum(jnp.where(c == r + REACH, keys, 0), axis=1, keepdims=True)
        same = mine == keys
        bias_ref[block] = jnp.where(same & (c <= r + REACH), 0.0, -1e30)
        position = jnp.sum(jnp.where(same & (c < r + REACH), 1.0, 0.0), axis=1, keepdims=True)
        angle = position * freq
        at = slice(block * REACH, (block + 1) * REACH)
        sign = jnp.where(lax.broadcasted_iota(jnp.int32, (REACH, HD), 1) < HD // 2, -1.0, 1.0)
        cos_ref[at, :] = jnp.cos(angle)
        sin_ref[at, :] = jnp.sin(angle) * sign


def tables(ids, own, behind):
    rows = own.shape[0]
    half = np.arange(HD // 2, dtype=np.float32)
    freq = np.float32(500000.0) ** (-(2.0 * half) / np.float32(HD))
    freq = jnp.asarray(np.concatenate([freq, freq]).astype(np.float32).reshape(1, HD))
    whole = pl.BlockSpec(memory_space=pltpu.VMEM)
    return pl.pallas_call(
        tables_kernel,
        in_specs=[pl.BlockSpec(memory_space=pltpu.SMEM)] + [whole] * 3,
        out_specs=[whole] * 3,
        out_shape=[
            jax.ShapeDtypeStruct((rows, HD), F32),
            jax.ShapeDtypeStruct((rows, HD), F32),
            jax.ShapeDtypeStruct((rows // REACH, REACH, 2 * REACH), F32),
        ],
        compiler_params=params(),
        cost_estimate=cost(20 * rows * 2 * REACH, 16 * rows * REACH, 2 * rows * HD),
        name="tables",
    )(ids, own.reshape(1, rows), behind.reshape(1, rows), freq)


def keys_kernel(a_ref, cos_ref, sin_ref, *refs):
    cos, sin = cos_ref[...], sin_ref[...]
    others, (out_ref, tail_ref) = refs[:-2], refs[-2:]
    rows = out_ref.shape[0]
    for h in range(a_ref.shape[1] // HD):
        at = slice(h * HD, (h + 1) * HD)
        b = jnp.concatenate([ref[:, at] for ref in others], axis=0)
        raw = (a_ref[:, at] + b).astype(BF16).astype(F32)
        out = (raw * cos + pltpu.roll(raw, HD // 2, 1) * sin).astype(BF16)
        out_ref[:, at] = out
        tail_ref[:, at] = out[rows - REACH :]


def values_kernel(a_ref, *refs):
    others, (out_ref, tail_ref) = refs[:-2], refs[-2:]
    rows = out_ref.shape[0]
    out = (a_ref[...] + jnp.concatenate([ref[...] for ref in others], axis=0)).astype(BF16)
    out_ref[...] = out
    tail_ref[...] = out[rows - REACH :]


def finish(kernel, name, *operands):
    rows, feats = operands[0].shape
    return pl.pallas_call(
        kernel,
        out_shape=[
            jax.ShapeDtypeStruct((rows, feats), BF16),
            jax.ShapeDtypeStruct((REACH, feats), BF16),
        ],
        compiler_params=params(),
        cost_estimate=cost(6 * rows * feats, 10 * rows * feats),
        name=name,
    )(*operands)


def scores_kernel(q_ref, ka_ref, kb_ref, bias_ref, out_ref):
    rows = q_ref.shape[0]
    keys = jnp.concatenate([ka_ref[...], kb_ref[...]], axis=0)
    bias = bias_ref[0]
    scale = 1.0 / HD**0.5
    for j in range(GROUP):
        q = q_ref[:, j * HD : (j + 1) * HD]
        s = lax.dot_general(q, keys, (((1,), (1,)), ((), ())), preferred_element_type=F32)
        s = s * scale + bias
        e = jnp.exp(s - jnp.max(s, axis=-1, keepdims=True))
        w = e * (1.0 / jnp.sum(e, axis=-1, keepdims=True))
        out_ref[0, j * rows : (j + 1) * rows, :] = w.astype(BF16)


def softmax_weights(queries, block, keys_a, block_a, keys_b, block_b, bias):
    rows = REACH
    heads = keys_a.shape[1] // HD
    return pl.pallas_call(
        scores_kernel,
        grid=(heads,),
        in_specs=[
            pl.BlockSpec((rows, GROUP * HD), lambda h: (block, h)),
            pl.BlockSpec((rows, HD), lambda h: (block_a, h)),
            pl.BlockSpec((rows, HD), lambda h: (block_b, h)),
            pl.BlockSpec((1, rows, 2 * rows), lambda h: (block, 0, 0)),
        ],
        out_specs=pl.BlockSpec((1, GROUP * rows, 2 * rows), lambda h: (h, 0, 0)),
        out_shape=jax.ShapeDtypeStruct((heads, GROUP * rows, 2 * rows), BF16),
        compiler_params=params(),
        cost_estimate=cost(
            4 * heads * GROUP * rows * rows * HD, 6 * rows * heads * GROUP * HD, 2 * heads * GROUP * rows * rows
        ),
        name="scores",
    )(queries, keys_a, keys_b, bias)


def context_kernel(block, p_ref, va_ref, vb_ref, *refs):
    out_ref, held, sems = refs[-3:]
    rows = va_ref.shape[0]
    width = GROUP * HD
    copies = []
    for h in range(p_ref.shape[0]):
        at = slice(h * HD, (h + 1) * HD)
        values = jnp.concatenate([va_ref[:, at], vb_ref[:, at]], axis=0)
        c = jnp.dot(p_ref[h], values, preferred_element_type=F32).astype(BF16)
        for j in range(GROUP):
            held[:, h * width + j * HD : h * width + (j + 1) * HD] = c[j * rows : (j + 1) * rows]
        here = (pl.ds(0, rows), pl.ds(h * width, width))
        there = (pl.ds(block * rows, rows), pl.ds(h * width, width))
        copies.append(pltpu.make_async_copy(held.at[here], out_ref.at[there], sems.at[h]))
        copies[-1].start()
    for copy in copies:
        copy.wait()


def contexts(block, weights, values_a, block_a, values_b, block_b, out=None):
    heads, _, span = weights.shape
    rows = REACH
    feats = heads * HD
    more = () if out is None else (out,)
    return pl.pallas_call(
        functools.partial(context_kernel, block),
        grid=(1,),
        in_specs=[
            pl.BlockSpec(memory_space=pltpu.VMEM),
            pl.BlockSpec((rows, feats), lambda i: (block_a, 0)),
            pl.BlockSpec((rows, feats), lambda i: (block_b, 0)),
        ]
        + [pl.BlockSpec(memory_space=pl.ANY)] * len(more),
        out_specs=pl.BlockSpec(memory_space=pl.ANY),
        out_shape=jax.ShapeDtypeStruct((2 * rows, GROUP * feats), BF16),
        scratch_shapes=[
            pltpu.VMEM((rows, GROUP * feats), BF16),
            pltpu.SemaphoreType.DMA((heads,)),
        ],
        input_output_aliases={3: 0} if more else {},
        compiler_params=params(),
        cost_estimate=cost(2 * heads * GROUP * rows * span * HD, 6 * rows * heads * GROUP * HD),
        name="context",
    )(weights, values_a, values_b, *more)


def after(*values):
    return lax.optimization_barrier(values)


def place(p):
    z, x = (p, 0) if p < 4 else (7 - p, 1)
    return z * 2 + x


def ring(signs):
    return [
        (y * 16 + place(p) * 2 + c, y * 16 + place((p + sign) % 8) * 2 + c)
        for y, sign in enumerate(signs)
        for p in range(8)
        for c in range(2)
    ]


def on_ring(hidden, norm_gain, key_weight, value_weight, queries, segment_ids):
    both = ("groups", "dp")
    key_way, value_way = ring((1, -1)), ring((-1, 1))
    other_group = [(i, (i + 16) % 32) for i in range(32)]
    other_core = [(i, i ^ 1) for i in range(16)]

    def send(value, way):
        return lax.ppermute(value, both, way)

    def swap(value):
        return lax.ppermute(value, "dp", other_core)

    ids = jnp.stack([lax.axis_index("dp"), lax.axis_index("groups")]).astype(jnp.int32)
    mine, theirs = normalise(ids, hidden, norm_gain)
    other = [swap(t) for t in theirs]
    k1, v1 = send(key_weight, key_way), send(value_weight, value_way)
    k1, v1, mine = after(k1, v1, mine)
    k2, v2 = send(k1, key_way), send(v1, value_way)
    yk1 = send(k1, other_group)
    k2, v2 = after(k2, v2)
    k3, v3 = send(k2, key_way), send(v2, value_way)
    yk2, yv2 = send(k2, other_group), send(v2, other_group)
    yv1 = send(v1, other_group)

    behind = from_behind(segment_ids, "dp", 1)
    key_part = project(ids, (0, -1, 1, -2), mine, other, [key_weight, k1, yk1, k2])
    k3, v3, key_part, behind = after(k3, v3, key_part, behind)
    k4, k3b = send(k3, key_way), send(yk2, value_way)
    v4 = send(v3, value_way)
    key_part = project(ids, (-3, 2), mine, other, [k3, yk2], key_part)
    value_part = project(ids, (0, 1, 2, 3), mine, other, [value_weight, v1, v2, v3])
    cos, sin, bias = tables(ids, segment_ids, behind)
    yv2, key_part, value_part, cos, sin, bias = after(yv2, key_part, value_part, cos, sin, bias)
    v3b = send(yv2, key_way)

    own_k, *other_k = project(ids, (-4, 3), mine, other, [k4, k3b], key_part, 2)
    keys, tail = finish(keys_kernel, "keys", own_k, cos, sin, *[swap(o) for o in other_k])
    prev_keys = from_behind(tail, "dp", 1)
    p1 = softmax_weights(queries, 1, keys, 0, keys, 1, bias)
    value_part = project(ids, (-2,), mine, other, [yv2], value_part)
    value_part, p1, prev_keys = after(value_part, p1, prev_keys)
    own_v, other_v = project(ids, (-1, 4, -3), mine, other, [yv1, v4, v3b], value_part)
    p0 = softmax_weights(queries, 0, prev_keys, 0, keys, 0, bias)
    other_v, p0 = after(swap(other_v), p0)
    values, tail = finish(values_kernel, "values", own_v, other_v)
    prev_values = from_behind(tail, "dp", 1)
    later = contexts(1, p1, values, 0, values, 1)
    return contexts(0, p0, prev_values, 0, values, 0, later)


def rotary(block, positions):
    half = HD // 2
    freqs = 500000.0 ** (-(2.0 * jnp.arange(half, dtype=jnp.float32)) / HD)
    angles = positions[:, None] * freqs[None, :]
    cosine = jnp.cos(angles)[:, None, :]
    sine = jnp.sin(angles)[:, None, :]
    first = block[..., :half]
    second = block[..., half:]
    return jnp.concatenate(
        [first * cosine - second * sine, second * cosine + first * sine], axis=-1
    )


def on_any(hidden, norm_gain, key_weight, value_weight, queries, segment_ids):
    whole = lax.all_gather(hidden, "tensor", axis=1, tiled=True)
    states = whole.astype(jnp.float32)
    meansq = jnp.mean(states * states, axis=-1, keepdims=True)
    normed = (states * lax.rsqrt(meansq + EPS) * norm_gain.astype(jnp.float32)).astype(BF16)
    local_rows = normed.shape[0]
    head_cols = key_weight.shape[1]

    def add_rows(piece):
        return jnp.dot(normed, piece, preferred_element_type=jnp.float32)

    key_sum = add_rows(lax.all_gather(key_weight, "dp", axis=0, tiled=True))
    value_sum = add_rows(lax.all_gather(value_weight, "dp", axis=0, tiled=True))
    keys_raw = key_sum.astype(BF16)
    values = value_sum.astype(BF16)
    earlier_keys, earlier_values, earlier_segs = from_behind(
        (keys_raw, values, segment_ids), "dp", 1
    )
    earlier_count = earlier_keys.shape[0]
    has_earlier = lax.axis_index("dp") > 0
    earlier_segs = jnp.where(has_earlier, earlier_segs, -1)
    window_segs = jnp.concatenate([earlier_segs, segment_ids], axis=0)
    window_len = window_segs.shape[0]
    window_index = jnp.arange(window_len, dtype=jnp.int32)
    same_seg = window_segs[:, None] == window_segs[None, :]
    before = window_index[None, :] < window_index[:, None]
    positions = jnp.sum((same_seg & before).astype(jnp.int32), axis=1)
    heads_here = head_cols // HD
    window_raw = (
        jnp.concatenate([earlier_keys, keys_raw], axis=0)
        .astype(jnp.float32)
        .reshape(window_len, heads_here, HD)
    )
    window_keys = rotary(window_raw, positions.astype(jnp.float32)).astype(BF16)
    window_values = jnp.concatenate([earlier_values, values], axis=0).reshape(
        window_len, heads_here, HD
    )
    query_heads = queries.reshape(local_rows, heads_here, GROUP, HD)
    scale = 1.0 / HD**0.5
    scores = (
        jnp.einsum("tkgd,skd->kgts", query_heads, window_keys, preferred_element_type=jnp.float32)
        * scale
    )
    query_pos = jnp.arange(local_rows, dtype=jnp.int32)[:, None] + earlier_count
    allowed = (window_index[None, :] <= query_pos) & (segment_ids[:, None] == window_segs[None, :])
    masked = jnp.where(allowed, scores, -1e30)
    largest = jnp.max(masked, axis=-1, keepdims=True)
    expd = jnp.where(allowed, jnp.exp(masked - largest), 0.0)
    weights = (expd / jnp.sum(expd, axis=-1, keepdims=True)).astype(BF16)
    out_heads = jnp.einsum(
        "kgts,skd->tkgd", weights, window_values, preferred_element_type=jnp.float32
    )
    return out_heads.reshape(local_rows, heads_here * GROUP * HD).astype(BF16)


def solution(mesh):
    in_specs = (
        P(("groups", "dp"), "tensor"),
        P(),
        P("dp", "tensor"),
        P("dp", "tensor"),
        P(("groups", "dp"), "tensor"),
        P(("groups", "dp")),
    )
    out_specs = P(("groups", "dp"), "tensor")
    small = (mesh.shape["groups"], mesh.shape["dp"], mesh.shape["tensor"]) == (2, 16, 1)
    return jax.shard_map(
        on_ring if small else on_any,
        mesh=mesh,
        in_specs=in_specs,
        out_specs=out_specs,
        check_vma=False,
    )
```

```python
import functools

import jax
import jax.numpy as jnp
import numpy as np
from jax import lax
from jax.experimental import pallas as pl
from jax.experimental.pallas import tpu as pltpu
from jax.sharding import PartitionSpec as P

HD = 128
GROUP = 8
REACH = 128
EPS = 1e-05
F32 = jnp.float32
BF16 = jnp.bfloat16
VMEM_LIMIT = 16 * 1024 * 1024


def params():
    return pltpu.CompilerParams(vmem_limit_bytes=VMEM_LIMIT)


def cost(flops, nbytes, trans=0):
    return pl.CostEstimate(flops=flops, bytes_accessed=nbytes, transcendentals=trans)


def from_behind(value, axis, steps):
    count = lax.axis_size(axis)
    initial, last = (max(0, -steps), min(count, count - steps))
    return lax.ppermute(value, axis, [(source, source + steps) for source in range(initial, last)])


def norm_kernel(core_ref, h_ref, g_ref, mine_ref, *theirs):
    width = h_ref.shape[1]
    half = width // 16
    x = h_ref[...].astype(F32)
    meansq = jnp.sum(x * x, axis=-1, keepdims=True) * (1.0 / width)
    scale = lax.rsqrt(meansq + EPS)
    first = lax.rem(core_ref[0], 2) == 0
    for b in range(8):
        lo = slice(2 * b * half, (2 * b + 1) * half)
        hi = slice((2 * b + 1) * half, (2 * b + 2) * half)
        n_lo = h_ref[:, lo].astype(F32) * scale * g_ref[:, lo].astype(F32)
        n_hi = h_ref[:, hi].astype(F32) * scale * g_ref[:, hi].astype(F32)
        out = slice(b * half, (b + 1) * half)
        mine_ref[:, out] = jnp.where(first, n_lo, n_hi).astype(BF16)
        other = jnp.where(first, n_hi, n_lo).astype(BF16)
        for part, theirs_ref in enumerate(theirs):

            @pl.when(pl.program_id(0) // (pl.num_programs(0) // len(theirs)) == part)
            def _():
                theirs_ref[:, out] = other


def normalise(core, hidden, gain):
    rows, width = hidden.shape
    step = 64
    mine = jax.ShapeDtypeStruct((rows, width // 2), BF16)
    parts = 2
    theirs = jax.ShapeDtypeStruct((rows // parts, width // 2), BF16)
    last = rows // step // parts - 1
    mine, *theirs = pl.pallas_call(
        norm_kernel,
        grid_spec=pltpu.PrefetchScalarGridSpec(
            num_scalar_prefetch=1,
            grid=(rows // step,),
            in_specs=[
                pl.BlockSpec((step, width), lambda i, c: (i, 0)),
                pl.BlockSpec((1, width), lambda i, c: (0, 0)),
            ],
            out_specs=[pl.BlockSpec((step, width // 2), lambda i, c: (i, 0))]
            + [
                pl.BlockSpec(
                    (step, width // 2),
                    functools.partial(lambda p, i, c: (jnp.clip(i - p * (last + 1), 0, last), 0), p),
                )
                for p in range(parts)
            ],
        ),
        out_shape=[mine] + [theirs] * parts,
        compiler_params=params(),
        cost_estimate=cost(8 * rows * width, 4 * rows * width),
        name="norm",
    )(core, hidden, gain.reshape(1, width))
    return mine, theirs


def block_at(ids_ref, step):
    z, x = lax.div(ids_ref[0], 4), lax.rem(lax.div(ids_ref[0], 2), 2)
    p = jnp.where(x == 0, z, 7 - z) + jnp.where(ids_ref[1] == 0, step, -step)
    p = jnp.where(p < 0, p + 8, p)
    p = jnp.where(p > 7, p - 8, p)
    return jnp.where(p < 4, 2 * p, 15 - 2 * p)


def project_kernel(steps, parts, carried, ids_ref, xa_ref, *refs):
    count = len(steps)
    others, refs = refs[:parts], refs[parts:]
    weights, refs = refs[:count], refs[count:]
    before, outs = refs[:carried], refs[carried:]
    total = None
    for j in range(count):
        depth = weights[j].shape[0]
        columns = pl.ds(pl.multiple_of(block_at(ids_ref, steps[j]) * depth, depth), depth)
        x = jnp.concatenate([ref[:, columns] for ref in (xa_ref, *others)], axis=0)
        part = jnp.dot(x, weights[j][...], preferred_element_type=F32)
        total = part if total is None else total + part
    held = jnp.concatenate([ref[...] for ref in before], axis=0) if carried else None
    total = held + total if carried else total
    at = 0
    for ref in outs:
        ref[...] = total[at : at + ref.shape[0]]
        at += ref.shape[0]


def project(ids, steps, xa, others, weights, before=(), split=1):
    rows = xa.shape[0]
    depth, feats = weights[0].shape
    outs = [jax.ShapeDtypeStruct((rows, feats), F32)]
    outs += [jax.ShapeDtypeStruct((rows // split, feats), F32)] * split
    whole = pl.BlockSpec(memory_space=pltpu.VMEM)
    operands = [xa, *others, *weights, *before]
    return pl.pallas_call(
        functools.partial(project_kernel, steps, len(others), len(before)),
        in_specs=[pl.BlockSpec(memory_space=pltpu.SMEM)] + [whole] * len(operands),
        out_specs=[whole] * len(outs),
        out_shape=outs,
        compiler_params=params(),
        cost_estimate=cost(
            4 * rows * depth * feats * len(weights), 2 * depth * feats * len(weights) + 4 * rows * 4096
        ),
        name="project",
    )(ids, *operands)


def tables_kernel(ids_ref, own_ref, behind_ref, freq_ref, cos_ref, sin_ref, bias_ref):
    own = own_ref[...]
    rows = own.shape[1]
    behind = jnp.where(ids_ref[0] > 0, behind_ref[:, rows - REACH :], -1)
    window = jnp.concatenate([behind, own], axis=1)
    shape = (REACH, 2 * REACH)
    r, c = lax.broadcasted_iota(jnp.int32, shape, 0), lax.broadcasted_iota(jnp.int32, shape, 1)
    freq = freq_ref[...]
    for block in range(rows // REACH):
        keys = window[:, block * REACH : (block + 2) * REACH]
        mine = jnp.sum(jnp.where(c == r + REACH, keys, 0), axis=1, keepdims=True)
        same = mine == keys
        bias_ref[block] = jnp.where(same & (c <= r + REACH), 0.0, -1e30)
        position = jnp.sum(jnp.where(same & (c < r + REACH), 1.0, 0.0), axis=1, keepdims=True)
        angle = position * freq
        at = slice(block * REACH, (block + 1) * REACH)
        sign = jnp.where(lax.broadcasted_iota(jnp.int32, (REACH, HD), 1) < HD // 2, -1.0, 1.0)
        cos_ref[at, :] = jnp.cos(angle)
        sin_ref[at, :] = jnp.sin(angle) * sign


def tables(ids, own, behind):
    rows = own.shape[0]
    half = np.arange(HD // 2, dtype=np.float32)
    freq = np.float32(500000.0) ** (-(2.0 * half) / np.float32(HD))
    freq = jnp.asarray(np.concatenate([freq, freq]).astype(np.float32).reshape(1, HD))
    whole = pl.BlockSpec(memory_space=pltpu.VMEM)
    return pl.pallas_call(
        tables_kernel,
        in_specs=[pl.BlockSpec(memory_space=pltpu.SMEM)] + [whole] * 3,
        out_specs=[whole] * 3,
        out_shape=[
            jax.ShapeDtypeStruct((rows, HD), F32),
            jax.ShapeDtypeStruct((rows, HD), F32),
            jax.ShapeDtypeStruct((rows // REACH, REACH, 2 * REACH), F32),
        ],
        compiler_params=params(),
        cost_estimate=cost(20 * rows * 2 * REACH, 16 * rows * REACH, 2 * rows * HD),
        name="tables",
    )(ids, own.reshape(1, rows), behind.reshape(1, rows), freq)


def keys_kernel(a_ref, cos_ref, sin_ref, *refs):
    cos, sin = cos_ref[...], sin_ref[...]
    others, (out_ref, tail_ref) = refs[:-2], refs[-2:]
    rows = out_ref.shape[0]
    for h in range(a_ref.shape[1] // HD):
        at = slice(h * HD, (h + 1) * HD)
        b = jnp.concatenate([ref[:, at] for ref in others], axis=0)
        raw = (a_ref[:, at] + b).astype(BF16).astype(F32)
        out = (raw * cos + pltpu.roll(raw, HD // 2, 1) * sin).astype(BF16)
        out_ref[:, at] = out
        tail_ref[:, at] = out[rows - REACH :]


def values_kernel(a_ref, *refs):
    others, (out_ref, tail_ref) = refs[:-2], refs[-2:]
    rows = out_ref.shape[0]
    out = (a_ref[...] + jnp.concatenate([ref[...] for ref in others], axis=0)).astype(BF16)
    out_ref[...] = out
    tail_ref[...] = out[rows - REACH :]


def finish(kernel, name, *operands):
    rows, feats = operands[0].shape
    return pl.pallas_call(
        kernel,
        out_shape=[
            jax.ShapeDtypeStruct((rows, feats), BF16),
            jax.ShapeDtypeStruct((REACH, feats), BF16),
        ],
        compiler_params=params(),
        cost_estimate=cost(6 * rows * feats, 10 * rows * feats),
        name=name,
    )(*operands)


def scores_kernel(q_ref, ka_ref, kb_ref, bias_ref, out_ref):
    rows = q_ref.shape[0]
    keys = jnp.concatenate([ka_ref[...], kb_ref[...]], axis=0)
    bias = bias_ref[0]
    scale = 1.0 / HD**0.5
    for j in range(GROUP):
        q = q_ref[:, j * HD : (j + 1) * HD]
        s = lax.dot_general(q, keys, (((1,), (1,)), ((), ())), preferred_element_type=F32)
        s = s * scale + bias
        e = jnp.exp(s - jnp.max(s, axis=-1, keepdims=True))
        w = e * (1.0 / jnp.sum(e, axis=-1, keepdims=True))
        out_ref[0, j * rows : (j + 1) * rows, :] = w.astype(BF16)


def softmax_weights(queries, block, keys_a, block_a, keys_b, block_b, bias):
    rows = REACH
    heads = keys_a.shape[1] // HD
    return pl.pallas_call(
        scores_kernel,
        grid=(heads,),
        in_specs=[
            pl.BlockSpec((rows, GROUP * HD), lambda h: (block, h)),
            pl.BlockSpec((rows, HD), lambda h: (block_a, h)),
            pl.BlockSpec((rows, HD), lambda h: (block_b, h)),
            pl.BlockSpec((1, rows, 2 * rows), lambda h: (block, 0, 0)),
        ],
        out_specs=pl.BlockSpec((1, GROUP * rows, 2 * rows), lambda h: (h, 0, 0)),
        out_shape=jax.ShapeDtypeStruct((heads, GROUP * rows, 2 * rows), BF16),
        compiler_params=params(),
        cost_estimate=cost(
            4 * heads * GROUP * rows * rows * HD, 6 * rows * heads * GROUP * HD, 2 * heads * GROUP * rows * rows
        ),
        name="scores",
    )(queries, keys_a, keys_b, bias)


def context_kernel(block, p_ref, va_ref, vb_ref, *refs):
    out_ref, held, sems = refs[-3:]
    rows = va_ref.shape[0]
    width = GROUP * HD
    copies = []
    for h in range(p_ref.shape[0]):
        at = slice(h * HD, (h + 1) * HD)
        values = jnp.concatenate([va_ref[:, at], vb_ref[:, at]], axis=0)
        c = jnp.dot(p_ref[h], values, preferred_element_type=F32).astype(BF16)
        for j in range(GROUP):
            held[:, h * width + j * HD : h * width + (j + 1) * HD] = c[j * rows : (j + 1) * rows]
        here = (pl.ds(0, rows), pl.ds(h * width, width))
        there = (pl.ds(block * rows, rows), pl.ds(h * width, width))
        copies.append(pltpu.make_async_copy(held.at[here], out_ref.at[there], sems.at[h]))
        copies[-1].start()
    for copy in copies:
        copy.wait()


def contexts(block, weights, values_a, block_a, values_b, block_b, out=None):
    heads, _, span = weights.shape
    rows = REACH
    feats = heads * HD
    more = () if out is None else (out,)
    return pl.pallas_call(
        functools.partial(context_kernel, block),
        grid=(1,),
        in_specs=[
            pl.BlockSpec(memory_space=pltpu.VMEM),
            pl.BlockSpec((rows, feats), lambda i: (block_a, 0)),
            pl.BlockSpec((rows, feats), lambda i: (block_b, 0)),
        ]
        + [pl.BlockSpec(memory_space=pl.ANY)] * len(more),
        out_specs=pl.BlockSpec(memory_space=pl.ANY),
        out_shape=jax.ShapeDtypeStruct((2 * rows, GROUP * feats), BF16),
        scratch_shapes=[
            pltpu.VMEM((rows, GROUP * feats), BF16),
            pltpu.SemaphoreType.DMA((heads,)),
        ],
        input_output_aliases={3: 0} if more else {},
        compiler_params=params(),
        cost_estimate=cost(2 * heads * GROUP * rows * span * HD, 6 * rows * heads * GROUP * HD),
        name="context",
    )(weights, values_a, values_b, *more)


def after(*values):
    return lax.optimization_barrier(values)


def place(p):
    z, x = (p, 0) if p < 4 else (7 - p, 1)
    return z * 2 + x


def ring(signs):
    return [
        (y * 16 + place(p) * 2 + c, y * 16 + place((p + sign) % 8) * 2 + c)
        for y, sign in enumerate(signs)
        for p in range(8)
        for c in range(2)
    ]


def on_ring(hidden, norm_gain, key_weight, value_weight, queries, segment_ids):
    both = ("groups", "dp")
    key_way, value_way = ring((1, -1)), ring((-1, 1))
    other_group = [(i, (i + 16) % 32) for i in range(32)]
    other_core = [(i, i ^ 1) for i in range(16)]

    def send(value, way):
        return lax.ppermute(value, both, way)

    def swap(value):
        return lax.ppermute(value, "dp", other_core)

    ids = jnp.stack([lax.axis_index("dp"), lax.axis_index("groups")]).astype(jnp.int32)
    mine, theirs = normalise(ids, hidden, norm_gain)
    other = [swap(t) for t in theirs]
    k1, v1 = send(key_weight, key_way), send(value_weight, value_way)
    behind = from_behind(segment_ids, "dp", 1)
    k1, mine, behind = after(k1, mine, behind)
    k2, v2 = send(k1, key_way), send(v1, value_way)
    k1b, yv1 = send(key_weight, value_way), send(v1, other_group)
    k3, v3 = send(k2, key_way), send(v2, value_way)
    yk2 = send(k2, other_group)

    key_part = project(ids, (0, -1, -2), mine, other, [key_weight, k1, k2])
    k3, yv1, key_part = after(k3, yv1, key_part)
    k4, yk3 = send(k3, key_way), send(k3, other_group)
    cos, sin, bias = tables(ids, segment_ids, behind)
    key_part = project(ids, (-3, 2, 1), mine, other, [k3, yk2, k1b], key_part)
    v3, key_part, cos, sin, bias = after(v3, key_part, cos, sin, bias)
    v4 = send(v3, value_way)
    yk3, v3y = after(yk3, v3)
    yv3 = send(v3y, other_group)
    v2b = send(yv1, key_way)
    value_part = project(ids, (0, 1, 2, -1, 3), mine, other, [value_weight, v1, v2, yv1, v3])

    own_k, *other_k = project(ids, (-4, 3), mine, other, [k4, yk3], key_part, 2)
    *other_k, value_part = after(*[swap(o) for o in other_k], value_part)
    keys, tail = finish(keys_kernel, "keys", own_k, cos, sin, *other_k)
    prev_keys = from_behind(tail, "dp", 1)
    p1 = softmax_weights(queries, 1, keys, 0, keys, 1, bias)
    value_part, p1, prev_keys = after(value_part, p1, prev_keys)
    own_v, other_v = project(ids, (4, -2, -3), mine, other, [v4, v2b, yv3], value_part)
    p0 = softmax_weights(queries, 0, prev_keys, 0, keys, 0, bias)
    other_v, p0 = after(swap(other_v), p0)
    values, tail = finish(values_kernel, "values", own_v, other_v)
    prev_values = from_behind(tail, "dp", 1)
    later = contexts(1, p1, values, 0, values, 1)
    return contexts(0, p0, prev_values, 0, values, 0, later)


def rotary(block, positions):
    half = HD // 2
    freqs = 500000.0 ** (-(2.0 * jnp.arange(half, dtype=jnp.float32)) / HD)
    angles = positions[:, None] * freqs[None, :]
    cosine = jnp.cos(angles)[:, None, :]
    sine = jnp.sin(angles)[:, None, :]
    first = block[..., :half]
    second = block[..., half:]
    return jnp.concatenate(
        [first * cosine - second * sine, second * cosine + first * sine], axis=-1
    )


def on_any(hidden, norm_gain, key_weight, value_weight, queries, segment_ids):
    whole = lax.all_gather(hidden, "tensor", axis=1, tiled=True)
    states = whole.astype(jnp.float32)
    meansq = jnp.mean(states * states, axis=-1, keepdims=True)
    normed = (states * lax.rsqrt(meansq + EPS) * norm_gain.astype(jnp.float32)).astype(BF16)
    local_rows = normed.shape[0]
    head_cols = key_weight.shape[1]

    def add_rows(piece):
        return jnp.dot(normed, piece, preferred_element_type=jnp.float32)

    key_sum = add_rows(lax.all_gather(key_weight, "dp", axis=0, tiled=True))
    value_sum = add_rows(lax.all_gather(value_weight, "dp", axis=0, tiled=True))
    keys_raw = key_sum.astype(BF16)
    values = value_sum.astype(BF16)
    earlier_keys, earlier_values, earlier_segs = from_behind(
        (keys_raw, values, segment_ids), "dp", 1
    )
    earlier_count = earlier_keys.shape[0]
    has_earlier = lax.axis_index("dp") > 0
    earlier_segs = jnp.where(has_earlier, earlier_segs, -1)
    window_segs = jnp.concatenate([earlier_segs, segment_ids], axis=0)
    window_len = window_segs.shape[0]
    window_index = jnp.arange(window_len, dtype=jnp.int32)
    same_seg = window_segs[:, None] == window_segs[None, :]
    before = window_index[None, :] < window_index[:, None]
    positions = jnp.sum((same_seg & before).astype(jnp.int32), axis=1)
    heads_here = head_cols // HD
    window_raw = (
        jnp.concatenate([earlier_keys, keys_raw], axis=0)
        .astype(jnp.float32)
        .reshape(window_len, heads_here, HD)
    )
    window_keys = rotary(window_raw, positions.astype(jnp.float32)).astype(BF16)
    window_values = jnp.concatenate([earlier_values, values], axis=0).reshape(
        window_len, heads_here, HD
    )
    query_heads = queries.reshape(local_rows, heads_here, GROUP, HD)
    scale = 1.0 / HD**0.5
    scores = (
        jnp.einsum("tkgd,skd->kgts", query_heads, window_keys, preferred_element_type=jnp.float32)
        * scale
    )
    query_pos = jnp.arange(local_rows, dtype=jnp.int32)[:, None] + earlier_count
    allowed = (window_index[None, :] <= query_pos) & (segment_ids[:, None] == window_segs[None, :])
    masked = jnp.where(allowed, scores, -1e30)
    largest = jnp.max(masked, axis=-1, keepdims=True)
    expd = jnp.where(allowed, jnp.exp(masked - largest), 0.0)
    weights = (expd / jnp.sum(expd, axis=-1, keepdims=True)).astype(BF16)
    out_heads = jnp.einsum(
        "kgts,skd->tkgd", weights, window_values, preferred_element_type=jnp.float32
    )
    return out_heads.reshape(local_rows, heads_here * GROUP * HD).astype(BF16)


def solution(mesh):
    in_specs = (
        P(("groups", "dp"), "tensor"),
        P(),
        P("dp", "tensor"),
        P("dp", "tensor"),
        P(("groups", "dp"), "tensor"),
        P(("groups", "dp")),
    )
    out_specs = P(("groups", "dp"), "tensor")
    small = (mesh.shape["groups"], mesh.shape["dp"], mesh.shape["tensor"]) == (2, 16, 1)
    return jax.shard_map(
        on_ring if small else on_any,
        mesh=mesh,
        in_specs=in_specs,
        out_specs=out_specs,
        check_vma=False,
    )
```

```python
import functools
import math

import jax
import jax.numpy as jnp
import numpy as np
from jax import lax
from jax.experimental import pallas as pl
from jax.experimental.pallas import tpu as pltpu
from jax.sharding import PartitionSpec as P

HD = 128
GROUP = 8
REACH = 128
EPS = 1e-05
F32 = jnp.float32
BF16 = jnp.bfloat16
VMEM_LIMIT = 16 * 1024 * 1024


def params():
    return pltpu.CompilerParams(vmem_limit_bytes=VMEM_LIMIT)


def cost(flops, nbytes, trans=0):
    return pl.CostEstimate(flops=flops, bytes_accessed=nbytes, transcendentals=trans)


def from_behind(value, axis, steps):
    count = lax.axis_size(axis)
    initial, last = (max(0, -steps), min(count, count - steps))
    return lax.ppermute(value, axis, [(source, source + steps) for source in range(initial, last)])


def norm_kernel(core_ref, h_ref, g_ref, mine_ref, *theirs):
    width = h_ref.shape[1]
    half = width // 16
    x = h_ref[...].astype(F32)
    meansq = jnp.sum(x * x, axis=-1, keepdims=True) * (1.0 / width)
    scale = lax.rsqrt(meansq + EPS)
    first = lax.rem(core_ref[0], 2) == 0
    for b in range(8):
        lo = slice(2 * b * half, (2 * b + 1) * half)
        hi = slice((2 * b + 1) * half, (2 * b + 2) * half)
        n_lo = h_ref[:, lo].astype(F32) * scale * g_ref[:, lo].astype(F32)
        n_hi = h_ref[:, hi].astype(F32) * scale * g_ref[:, hi].astype(F32)
        out = slice(b * half, (b + 1) * half)
        mine_ref[:, out] = jnp.where(first, n_lo, n_hi).astype(BF16)
        other = jnp.where(first, n_hi, n_lo).astype(BF16)
        for part, theirs_ref in enumerate(theirs):

            @pl.when(pl.program_id(0) // (pl.num_programs(0) // len(theirs)) == part)
            def _():
                theirs_ref[:, out] = other


def normalise(core, hidden, gain):
    rows, width = hidden.shape
    step = 64
    mine = jax.ShapeDtypeStruct((rows, width // 2), BF16)
    parts = 2
    theirs = jax.ShapeDtypeStruct((rows // parts, width // 2), BF16)
    last = rows // step // parts - 1
    mine, *theirs = pl.pallas_call(
        norm_kernel,
        grid_spec=pltpu.PrefetchScalarGridSpec(
            num_scalar_prefetch=1,
            grid=(rows // step,),
            in_specs=[
                pl.BlockSpec((step, width), lambda i, c: (i, 0)),
                pl.BlockSpec((1, width), lambda i, c: (0, 0)),
            ],
            out_specs=[pl.BlockSpec((step, width // 2), lambda i, c: (i, 0))]
            + [
                pl.BlockSpec(
                    (step, width // 2),
                    functools.partial(lambda p, i, c: (jnp.clip(i - p * (last + 1), 0, last), 0), p),
                )
                for p in range(parts)
            ],
        ),
        out_shape=[mine] + [theirs] * parts,
        compiler_params=params(),
        cost_estimate=cost(8 * rows * width, 4 * rows * width),
        name="norm",
    )(core, hidden, gain.reshape(1, width))
    return mine, theirs


def block_at(ids_ref, step):
    z, x = lax.div(ids_ref[0], 4), lax.rem(lax.div(ids_ref[0], 2), 2)
    p = jnp.where(x == 0, z, 7 - z) + jnp.where(ids_ref[1] == 0, step, -step)
    p = jnp.where(p < 0, p + 8, p)
    p = jnp.where(p > 7, p - 8, p)
    return jnp.where(p < 4, 2 * p, 15 - 2 * p)


def project_kernel(steps, parts, carried, ids_ref, xa_ref, *refs):
    count = len(steps)
    others, refs = refs[:parts], refs[parts:]
    weights, refs = refs[:count], refs[count:]
    before, outs = refs[:carried], refs[carried:]
    depth = weights[0].shape[0]
    columns = [pl.ds(pl.multiple_of(block_at(ids_ref, step) * depth, depth), depth) for step in steps]
    x = [jnp.concatenate([ref[:, c] for c in columns], axis=1) for ref in (xa_ref, *others)]
    w = jnp.concatenate([ref[...] for ref in weights], axis=0)
    total = jnp.dot(jnp.concatenate(x, axis=0), w, preferred_element_type=F32)
    held = jnp.concatenate([ref[...] for ref in before], axis=0) if carried else None
    total = held + total if carried else total
    at = 0
    for ref in outs:
        ref[...] = total[at : at + ref.shape[0]]
        at += ref.shape[0]


def project(ids, steps, xa, others, weights, before=(), split=1):
    rows = xa.shape[0]
    depth, feats = weights[0].shape
    outs = [jax.ShapeDtypeStruct((rows, feats), F32)]
    outs += [jax.ShapeDtypeStruct((rows // split, feats), F32)] * split
    whole = pl.BlockSpec(memory_space=pltpu.VMEM)
    operands = [xa, *others, *weights, *before]
    return pl.pallas_call(
        functools.partial(project_kernel, steps, len(others), len(before)),
        in_specs=[pl.BlockSpec(memory_space=pltpu.SMEM)] + [whole] * len(operands),
        out_specs=[whole] * len(outs),
        out_shape=outs,
        compiler_params=params(),
        cost_estimate=cost(
            4 * rows * depth * feats * len(weights), 2 * depth * feats * len(weights) + 4 * rows * 4096
        ),
        name="project",
    )(ids, *operands)


def tables_kernel(ids_ref, own_ref, behind_ref, freq_ref, cos_ref, sin_ref, bias_ref):
    own = own_ref[...]
    rows = own.shape[1]
    behind = jnp.where(ids_ref[0] > 0, behind_ref[:, rows - REACH :], -1)
    window = jnp.concatenate([behind, own], axis=1)
    shape = (REACH, 2 * REACH)
    r, c = lax.broadcasted_iota(jnp.int32, shape, 0), lax.broadcasted_iota(jnp.int32, shape, 1)
    freq = freq_ref[...]
    for block in range(rows // REACH):
        keys = window[:, block * REACH : (block + 2) * REACH]
        mine = jnp.sum(jnp.where(c == r + REACH, keys, 0), axis=1, keepdims=True)
        same = mine == keys
        bias_ref[block] = jnp.where(same & (c <= r + REACH), 0.0, -1e30)
        position = jnp.sum(jnp.where(same & (c < r + REACH), 1.0, 0.0), axis=1, keepdims=True)
        angle = position * freq
        at = slice(block * REACH, (block + 1) * REACH)
        sign = jnp.where(lax.broadcasted_iota(jnp.int32, (REACH, HD), 1) < HD // 2, -1.0, 1.0)
        cos_ref[at, :] = jnp.cos(angle)
        sin_ref[at, :] = jnp.sin(angle) * sign


def tables(ids, own, behind):
    rows = own.shape[0]
    half = np.arange(HD // 2, dtype=np.float32)
    freq = np.float32(500000.0) ** (-(2.0 * half) / np.float32(HD))
    freq = jnp.asarray(np.concatenate([freq, freq]).astype(np.float32).reshape(1, HD))
    whole = pl.BlockSpec(memory_space=pltpu.VMEM)
    return pl.pallas_call(
        tables_kernel,
        in_specs=[pl.BlockSpec(memory_space=pltpu.SMEM)] + [whole] * 3,
        out_specs=[whole] * 3,
        out_shape=[
            jax.ShapeDtypeStruct((rows, HD), F32),
            jax.ShapeDtypeStruct((rows, HD), F32),
            jax.ShapeDtypeStruct((rows // REACH, REACH, 2 * REACH), F32),
        ],
        compiler_params=params(),
        cost_estimate=cost(20 * rows * 2 * REACH, 16 * rows * REACH, 2 * rows * HD),
        name="tables",
    )(ids, own.reshape(1, rows), behind.reshape(1, rows), freq)


def keys_kernel(a_ref, cos_ref, sin_ref, *refs):
    cos, sin = cos_ref[...], sin_ref[...]
    others, (out_ref, head_ref, tail_ref) = refs[:-3], refs[-3:]
    rows = out_ref.shape[0]
    for h in range(a_ref.shape[1] // HD):
        at = slice(h * HD, (h + 1) * HD)
        b = jnp.concatenate([ref[:, at] for ref in others], axis=0)
        raw = (a_ref[:, at] + b).astype(BF16).astype(F32)
        out = (raw * cos + pltpu.roll(raw, HD // 2, 1) * sin).astype(BF16)
        out_ref[:, at] = out
        head_ref[:, at] = out[:REACH]
        tail_ref[:, at] = out[rows - REACH :]


def values_kernel(a_ref, *refs):
    others, (out_ref, head_ref, tail_ref) = refs[:-3], refs[-3:]
    rows = out_ref.shape[0]
    out = (a_ref[...] + jnp.concatenate([ref[...] for ref in others], axis=0)).astype(BF16)
    out_ref[...] = out
    head_ref[...] = out[:REACH]
    tail_ref[...] = out[rows - REACH :]


def finish(kernel, name, *operands):
    rows, feats = operands[0].shape
    return pl.pallas_call(
        kernel,
        out_shape=[
            jax.ShapeDtypeStruct((rows, feats), BF16),
            jax.ShapeDtypeStruct((REACH, feats), BF16),
            jax.ShapeDtypeStruct((REACH, feats), BF16),
        ],
        compiler_params=params(),
        cost_estimate=cost(6 * rows * feats, 10 * rows * feats),
        name=name,
    )(*operands)


def scores_kernel(block, q_ref, ka_ref, kb_ref, bias_ref, out_ref):
    rows = REACH
    bias = bias_ref[block]
    ones = jnp.ones((2 * rows, rows), BF16)
    scale = math.log2(math.e) / HD**0.5
    for h in range(out_ref.shape[0]):
        at = slice(h * HD, (h + 1) * HD)
        keys = jnp.concatenate([ka_ref[:rows, at], kb_ref[-rows:, at]], axis=0)
        for j in range(GROUP):
            column = (h * GROUP + j) * HD
            q = q_ref[block * rows : (block + 1) * rows, column : column + HD]
            s = lax.dot_general(q, keys, (((1,), (1,)), ((), ())), preferred_element_type=F32)
            s = s * scale + bias
            e = jnp.exp2(s - jnp.max(s, axis=-1, keepdims=True))
            total = jnp.dot(e.astype(BF16), ones, preferred_element_type=F32)
            inverse = 1.0 / total
            w = e * jnp.concatenate([inverse, inverse], axis=1)
            out_ref[h, j * rows : (j + 1) * rows, :] = w.astype(BF16)


def softmax_weights(block, queries, keys_a, keys_b, bias):
    rows = REACH
    heads = keys_a.shape[1] // HD
    whole = pl.BlockSpec(memory_space=pltpu.VMEM)
    return pl.pallas_call(
        functools.partial(scores_kernel, block),
        in_specs=[whole] * 4,
        out_specs=whole,
        out_shape=jax.ShapeDtypeStruct((heads, GROUP * rows, 2 * rows), BF16),
        compiler_params=params(),
        cost_estimate=cost(
            4 * heads * GROUP * rows * rows * HD, 6 * rows * heads * GROUP * HD, 2 * heads * GROUP * rows * rows
        ),
        name="scores",
    )(queries, keys_a, keys_b, bias)


def context_kernel(block, p_ref, va_ref, vb_ref, *refs):
    out_ref, held, sems = refs[-3:]
    rows = held.shape[0]
    width = GROUP * HD
    copies = []
    for h in range(p_ref.shape[0]):
        at = slice(h * HD, (h + 1) * HD)
        values = jnp.concatenate([va_ref[:rows, at], vb_ref[-rows:, at]], axis=0)
        c = jnp.dot(p_ref[h], values, preferred_element_type=F32).astype(BF16)
        for j in range(GROUP):
            held[:, h * width + j * HD : h * width + (j + 1) * HD] = c[j * rows : (j + 1) * rows]
        here = (pl.ds(0, rows), pl.ds(h * width, width))
        there = (pl.ds(block * rows, rows), pl.ds(h * width, width))
        copies.append(pltpu.make_async_copy(held.at[here], out_ref.at[there], sems.at[h]))
        copies[-1].start()
    for copy in copies:
        copy.wait()


def contexts(block, weights, values_a, values_b, out=None):
    heads, _, span = weights.shape
    rows = REACH
    feats = heads * HD
    whole = pl.BlockSpec(memory_space=pltpu.VMEM)
    more = () if out is None else (out,)
    return pl.pallas_call(
        functools.partial(context_kernel, block),
        in_specs=[whole] * 3 + [pl.BlockSpec(memory_space=pl.ANY)] * len(more),
        out_specs=pl.BlockSpec(memory_space=pl.ANY),
        out_shape=jax.ShapeDtypeStruct((2 * rows, GROUP * feats), BF16),
        scratch_shapes=[
            pltpu.VMEM((rows, GROUP * feats), BF16),
            pltpu.SemaphoreType.DMA((heads,)),
        ],
        input_output_aliases={3: 0} if more else {},
        compiler_params=params(),
        cost_estimate=cost(2 * heads * GROUP * rows * span * HD, 6 * rows * heads * GROUP * HD),
        name="context",
    )(weights, values_a, values_b, *more)


def after(*values):
    return lax.optimization_barrier(values)


def place(p):
    z, x = (p, 0) if p < 4 else (7 - p, 1)
    return z * 2 + x


def ring(signs):
    return [
        (y * 16 + place(p) * 2 + c, y * 16 + place((p + sign) % 8) * 2 + c)
        for y, sign in enumerate(signs)
        for p in range(8)
        for c in range(2)
    ]


def on_ring(hidden, norm_gain, key_weight, value_weight, queries, segment_ids):
    both = ("groups", "dp")
    key_way, value_way = ring((1, -1)), ring((-1, 1))
    other_group = [(i, (i + 16) % 32) for i in range(32)]
    other_core = [(i, i ^ 1) for i in range(16)]

    def send(value, way):
        return lax.ppermute(value, both, way)

    def swap(value):
        return lax.ppermute(value, "dp", other_core)

    ids = jnp.stack([lax.axis_index("dp"), lax.axis_index("groups")]).astype(jnp.int32)
    mine, theirs = normalise(ids, hidden, norm_gain)
    other = [swap(t) for t in theirs]
    k1, v1 = send(key_weight, key_way), send(value_weight, value_way)
    behind = from_behind(segment_ids, "dp", 1)
    k1, mine, behind = after(k1, mine, behind)
    k2, v2 = send(k1, key_way), send(v1, value_way)
    k1b, yv1 = send(key_weight, value_way), send(v1, other_group)
    k3, v3 = send(k2, key_way), send(v2, value_way)
    yk2 = send(k2, other_group)

    key_part = project(ids, (0, -1, -2), mine, other, [key_weight, k1, k2])
    k3, yv1, key_part = after(k3, yv1, key_part)
    k4, yk3 = send(k3, key_way), send(k3, other_group)
    cos, sin, bias = tables(ids, segment_ids, behind)
    key_part = project(ids, (-3, 2, 1), mine, other, [k3, yk2, k1b], key_part)
    v3, key_part, cos, sin, bias = after(v3, key_part, cos, sin, bias)
    v4 = send(v3, value_way)
    yk3, v3y = after(yk3, v3)
    yv3 = send(v3y, other_group)
    v2b = send(yv1, key_way)
    value_part = project(ids, (0, 1, 2, -1, 3), mine, other, [value_weight, v1, v2, yv1, v3])

    own_k, *other_k = project(ids, (-4, 3), mine, other, [k4, yk3], key_part, 2)
    *other_k, value_part = after(*[swap(o) for o in other_k], value_part)
    keys, head_keys, tail = finish(keys_kernel, "keys", own_k, cos, sin, *other_k)
    prev_keys = from_behind(tail, "dp", 1)
    p1 = softmax_weights(1, queries, keys, keys, bias)
    value_part, p1, prev_keys = after(value_part, p1, prev_keys)
    own_v, other_v = project(ids, (4, -2, -3), mine, other, [v4, v2b, yv3], value_part)
    p0 = softmax_weights(0, queries, prev_keys, head_keys, bias)
    other_v, p0 = after(swap(other_v), p0)
    values, head_values, tail = finish(values_kernel, "values", own_v, other_v)
    prev_values = from_behind(tail, "dp", 1)
    later = contexts(1, p1, values, values)
    return contexts(0, p0, prev_values, head_values, later)


def rotary(block, positions):
    half = HD // 2
    freqs = 500000.0 ** (-(2.0 * jnp.arange(half, dtype=jnp.float32)) / HD)
    angles = positions[:, None] * freqs[None, :]
    cosine = jnp.cos(angles)[:, None, :]
    sine = jnp.sin(angles)[:, None, :]
    first = block[..., :half]
    second = block[..., half:]
    return jnp.concatenate(
        [first * cosine - second * sine, second * cosine + first * sine], axis=-1
    )


def on_any(hidden, norm_gain, key_weight, value_weight, queries, segment_ids):
    whole = lax.all_gather(hidden, "tensor", axis=1, tiled=True)
    states = whole.astype(jnp.float32)
    meansq = jnp.mean(states * states, axis=-1, keepdims=True)
    normed = (states * lax.rsqrt(meansq + EPS) * norm_gain.astype(jnp.float32)).astype(BF16)
    local_rows = normed.shape[0]
    head_cols = key_weight.shape[1]

    def add_rows(piece):
        return jnp.dot(normed, piece, preferred_element_type=jnp.float32)

    key_sum = add_rows(lax.all_gather(key_weight, "dp", axis=0, tiled=True))
    value_sum = add_rows(lax.all_gather(value_weight, "dp", axis=0, tiled=True))
    keys_raw = key_sum.astype(BF16)
    values = value_sum.astype(BF16)
    earlier_keys, earlier_values, earlier_segs = from_behind(
        (keys_raw, values, segment_ids), "dp", 1
    )
    earlier_count = earlier_keys.shape[0]
    has_earlier = lax.axis_index("dp") > 0
    earlier_segs = jnp.where(has_earlier, earlier_segs, -1)
    window_segs = jnp.concatenate([earlier_segs, segment_ids], axis=0)
    window_len = window_segs.shape[0]
    window_index = jnp.arange(window_len, dtype=jnp.int32)
    same_seg = window_segs[:, None] == window_segs[None, :]
    before = window_index[None, :] < window_index[:, None]
    positions = jnp.sum((same_seg & before).astype(jnp.int32), axis=1)
    heads_here = head_cols // HD
    window_raw = (
        jnp.concatenate([earlier_keys, keys_raw], axis=0)
        .astype(jnp.float32)
        .reshape(window_len, heads_here, HD)
    )
    window_keys = rotary(window_raw, positions.astype(jnp.float32)).astype(BF16)
    window_values = jnp.concatenate([earlier_values, values], axis=0).reshape(
        window_len, heads_here, HD
    )
    query_heads = queries.reshape(local_rows, heads_here, GROUP, HD)
    scale = 1.0 / HD**0.5
    scores = (
        jnp.einsum("tkgd,skd->kgts", query_heads, window_keys, preferred_element_type=jnp.float32)
        * scale
    )
    query_pos = jnp.arange(local_rows, dtype=jnp.int32)[:, None] + earlier_count
    allowed = (window_index[None, :] <= query_pos) & (segment_ids[:, None] == window_segs[None, :])
    masked = jnp.where(allowed, scores, -1e30)
    largest = jnp.max(masked, axis=-1, keepdims=True)
    expd = jnp.where(allowed, jnp.exp(masked - largest), 0.0)
    weights = (expd / jnp.sum(expd, axis=-1, keepdims=True)).astype(BF16)
    out_heads = jnp.einsum(
        "kgts,skd->tkgd", weights, window_values, preferred_element_type=jnp.float32
    )
    return out_heads.reshape(local_rows, heads_here * GROUP * HD).astype(BF16)


def solution(mesh):
    in_specs = (
        P(("groups", "dp"), "tensor"),
        P(),
        P("dp", "tensor"),
        P("dp", "tensor"),
        P(("groups", "dp"), "tensor"),
        P(("groups", "dp")),
    )
    out_specs = P(("groups", "dp"), "tensor")
    small = (mesh.shape["groups"], mesh.shape["dp"], mesh.shape["tensor"]) == (2, 16, 1)
    return jax.shard_map(
        on_ring if small else on_any,
        mesh=mesh,
        in_specs=in_specs,
        out_specs=out_specs,
        check_vma=False,
    )
```

```python
import functools
import math

import jax
import jax.numpy as jnp
import numpy as np
from jax import lax
from jax.experimental import pallas as pl
from jax.experimental.pallas import tpu as pltpu
from jax.sharding import PartitionSpec as P

HD = 128
GROUP = 8
REACH = 128
EPS = 1e-05
F32 = jnp.float32
BF16 = jnp.bfloat16
VMEM_LIMIT = 16 * 1024 * 1024


def params():
    return pltpu.CompilerParams(vmem_limit_bytes=VMEM_LIMIT)


def cost(flops, nbytes, trans=0):
    return pl.CostEstimate(flops=flops, bytes_accessed=nbytes, transcendentals=trans)


def from_behind(value, axis, steps):
    count = lax.axis_size(axis)
    initial, last = (max(0, -steps), min(count, count - steps))
    return lax.ppermute(value, axis, [(source, source + steps) for source in range(initial, last)])


def norm_kernel(core_ref, h_ref, g_ref, mine_ref, *theirs):
    width = h_ref.shape[1]
    half = width // 16
    x = h_ref[...].astype(F32)
    meansq = jnp.sum(x * x, axis=-1, keepdims=True) * (1.0 / width)
    scale = lax.rsqrt(meansq + EPS)
    first = lax.rem(core_ref[0], 2) == 0
    for b in range(8):
        lo = slice(2 * b * half, (2 * b + 1) * half)
        hi = slice((2 * b + 1) * half, (2 * b + 2) * half)
        n_lo = h_ref[:, lo].astype(F32) * scale * g_ref[:, lo].astype(F32)
        n_hi = h_ref[:, hi].astype(F32) * scale * g_ref[:, hi].astype(F32)
        out = slice(b * half, (b + 1) * half)
        mine_ref[:, out] = jnp.where(first, n_lo, n_hi).astype(BF16)
        other = jnp.where(first, n_hi, n_lo).astype(BF16)
        for part, theirs_ref in enumerate(theirs):

            @pl.when(pl.program_id(0) // (pl.num_programs(0) // len(theirs)) == part)
            def _():
                theirs_ref[:, out] = other


def normalise(core, hidden, gain):
    rows, width = hidden.shape
    step = 64
    mine = jax.ShapeDtypeStruct((rows, width // 2), BF16)
    parts = 2
    theirs = jax.ShapeDtypeStruct((rows // parts, width // 2), BF16)
    last = rows // step // parts - 1
    mine, *theirs = pl.pallas_call(
        norm_kernel,
        grid_spec=pltpu.PrefetchScalarGridSpec(
            num_scalar_prefetch=1,
            grid=(rows // step,),
            in_specs=[
                pl.BlockSpec((step, width), lambda i, c: (i, 0)),
                pl.BlockSpec((1, width), lambda i, c: (0, 0)),
            ],
            out_specs=[pl.BlockSpec((step, width // 2), lambda i, c: (i, 0))]
            + [
                pl.BlockSpec(
                    (step, width // 2),
                    functools.partial(lambda p, i, c: (jnp.clip(i - p * (last + 1), 0, last), 0), p),
                )
                for p in range(parts)
            ],
        ),
        out_shape=[mine] + [theirs] * parts,
        compiler_params=params(),
        cost_estimate=cost(8 * rows * width, 4 * rows * width),
        name="norm",
    )(core, hidden, gain.reshape(1, width))
    return mine, theirs


def block_at(step):
    me = lax.axis_index("dp")
    z, x = lax.div(me, 4), lax.rem(lax.div(me, 2), 2)
    p = jnp.where(x == 0, z, 7 - z) + jnp.where(lax.axis_index("groups") == 0, step, -step)
    p = jnp.where(p < 0, p + 8, p)
    p = jnp.where(p > 7, p - 8, p)
    return jnp.where(p < 4, 2 * p, 15 - 2 * p)


def project_kernel(steps, parts, carried, xa_ref, *refs):
    count = len(steps)
    others, refs = refs[:parts], refs[parts:]
    weights, refs = refs[:count], refs[count:]
    before, outs = refs[:carried], refs[carried:]
    depth = weights[0].shape[0]
    columns = [pl.ds(pl.multiple_of(block_at(step) * depth, depth), depth) for step in steps]
    x = [jnp.concatenate([ref[:, c] for c in columns], axis=1) for ref in (xa_ref, *others)]
    w = jnp.concatenate([ref[...] for ref in weights], axis=0)
    total = jnp.dot(jnp.concatenate(x, axis=0), w, preferred_element_type=F32)
    held = jnp.concatenate([ref[...] for ref in before], axis=0) if carried else None
    total = held + total if carried else total
    at = 0
    for ref in outs:
        ref[...] = total[at : at + ref.shape[0]]
        at += ref.shape[0]


def project(steps, xa, others, weights, before=(), split=1):
    rows = xa.shape[0]
    depth, feats = weights[0].shape
    outs = [jax.ShapeDtypeStruct((rows, feats), F32)]
    outs += [jax.ShapeDtypeStruct((rows // split, feats), F32)] * split
    whole = pl.BlockSpec(memory_space=pltpu.VMEM)
    operands = [xa, *others, *weights, *before]
    return pl.pallas_call(
        functools.partial(project_kernel, steps, len(others), len(before)),
        in_specs=[whole] * len(operands),
        out_specs=[whole] * len(outs),
        out_shape=outs,
        compiler_params=params(),
        cost_estimate=cost(
            4 * rows * depth * feats * len(weights), 2 * depth * feats * len(weights) + 4 * rows * 4096
        ),
        name="project",
    )(*operands)


def tables_kernel(ids_ref, own_ref, behind_ref, freq_ref, cos_ref, sin_ref, bias_ref):
    own = own_ref[...]
    rows = own.shape[1]
    behind = jnp.where(ids_ref[0] > 0, behind_ref[:, rows - REACH :], -1)
    window = jnp.concatenate([behind, own], axis=1)
    shape = (REACH, 2 * REACH)
    r, c = lax.broadcasted_iota(jnp.int32, shape, 0), lax.broadcasted_iota(jnp.int32, shape, 1)
    freq = freq_ref[...]
    for block in range(rows // REACH):
        keys = window[:, block * REACH : (block + 2) * REACH]
        mine = jnp.sum(jnp.where(c == r + REACH, keys, 0), axis=1, keepdims=True)
        same = mine == keys
        bias_ref[block] = jnp.where(same & (c <= r + REACH), 0.0, -1e30)
        position = jnp.sum(jnp.where(same & (c < r + REACH), 1.0, 0.0), axis=1, keepdims=True)
        angle = position * freq
        at = slice(block * REACH, (block + 1) * REACH)
        sign = jnp.where(lax.broadcasted_iota(jnp.int32, (REACH, HD), 1) < HD // 2, -1.0, 1.0)
        cos_ref[at, :] = jnp.cos(angle)
        sin_ref[at, :] = jnp.sin(angle) * sign


def tables(ids, own, behind):
    rows = own.shape[0]
    half = np.arange(HD // 2, dtype=np.float32)
    freq = np.float32(500000.0) ** (-(2.0 * half) / np.float32(HD))
    freq = jnp.asarray(np.concatenate([freq, freq]).astype(np.float32).reshape(1, HD))
    whole = pl.BlockSpec(memory_space=pltpu.VMEM)
    return pl.pallas_call(
        tables_kernel,
        in_specs=[pl.BlockSpec(memory_space=pltpu.SMEM)] + [whole] * 3,
        out_specs=[whole] * 3,
        out_shape=[
            jax.ShapeDtypeStruct((rows, HD), F32),
            jax.ShapeDtypeStruct((rows, HD), F32),
            jax.ShapeDtypeStruct((rows // REACH, REACH, 2 * REACH), F32),
        ],
        compiler_params=params(),
        cost_estimate=cost(20 * rows * 2 * REACH, 16 * rows * REACH, 2 * rows * HD),
        name="tables",
    )(ids, own.reshape(1, rows), behind.reshape(1, rows), freq)


def keys_kernel(a_ref, cos_ref, sin_ref, *refs):
    cos, sin = cos_ref[...], sin_ref[...]
    others, (out_ref, head_ref, tail_ref) = refs[:-3], refs[-3:]
    rows = out_ref.shape[0]
    for h in range(a_ref.shape[1] // HD):
        at = slice(h * HD, (h + 1) * HD)
        b = jnp.concatenate([ref[:, at] for ref in others], axis=0)
        raw = (a_ref[:, at] + b).astype(BF16).astype(F32)
        out = (raw * cos + pltpu.roll(raw, HD // 2, 1) * sin).astype(BF16)
        out_ref[:, at] = out
        head_ref[:, at] = out[:REACH]
        tail_ref[:, at] = out[rows - REACH :]


def values_kernel(a_ref, *refs):
    others, (out_ref, head_ref, tail_ref) = refs[:-3], refs[-3:]
    rows = out_ref.shape[0]
    out = (a_ref[...] + jnp.concatenate([ref[...] for ref in others], axis=0)).astype(BF16)
    out_ref[...] = out
    head_ref[...] = out[:REACH]
    tail_ref[...] = out[rows - REACH :]


def finish(kernel, name, *operands):
    rows, feats = operands[0].shape
    return pl.pallas_call(
        kernel,
        out_shape=[
            jax.ShapeDtypeStruct((rows, feats), BF16),
            jax.ShapeDtypeStruct((REACH, feats), BF16),
            jax.ShapeDtypeStruct((REACH, feats), BF16),
        ],
        compiler_params=params(),
        cost_estimate=cost(6 * rows * feats, 10 * rows * feats),
        name=name,
    )(*operands)


def scores_kernel(block, q_ref, ka_ref, kb_ref, bias_ref, out_ref):
    rows = REACH
    bias = bias_ref[block]
    ones = jnp.ones((2 * rows, rows), BF16)
    scale = math.log2(math.e) / HD**0.5
    for h in range(out_ref.shape[0]):
        at = slice(h * HD, (h + 1) * HD)
        keys = jnp.concatenate([ka_ref[:rows, at], kb_ref[-rows:, at]], axis=0)
        for j in range(GROUP):
            column = (h * GROUP + j) * HD
            q = q_ref[block * rows : (block + 1) * rows, column : column + HD]
            s = lax.dot_general(q, keys, (((1,), (1,)), ((), ())), preferred_element_type=F32)
            s = s * scale + bias
            e = jnp.exp2(s - jnp.max(s, axis=-1, keepdims=True))
            total = jnp.dot(e.astype(BF16), ones, preferred_element_type=F32)
            inverse = 1.0 / total
            w = e * jnp.concatenate([inverse, inverse], axis=1)
            out_ref[h, j * rows : (j + 1) * rows, :] = w.astype(BF16)


def softmax_weights(block, queries, keys_a, keys_b, bias):
    rows = REACH
    heads = keys_a.shape[1] // HD
    whole = pl.BlockSpec(memory_space=pltpu.VMEM)
    return pl.pallas_call(
        functools.partial(scores_kernel, block),
        in_specs=[whole] * 4,
        out_specs=whole,
        out_shape=jax.ShapeDtypeStruct((heads, GROUP * rows, 2 * rows), BF16),
        compiler_params=params(),
        cost_estimate=cost(
            4 * heads * GROUP * rows * rows * HD, 6 * rows * heads * GROUP * HD, 2 * heads * GROUP * rows * rows
        ),
        name="scores",
    )(queries, keys_a, keys_b, bias)


def context_kernel(block, p_ref, va_ref, vb_ref, *refs):
    out_ref, held, sems = refs[-3:]
    rows = held.shape[0]
    width = GROUP * HD
    copies = []
    for h in range(p_ref.shape[0]):
        at = slice(h * HD, (h + 1) * HD)
        values = jnp.concatenate([va_ref[:rows, at], vb_ref[-rows:, at]], axis=0)
        c = jnp.dot(p_ref[h], values, preferred_element_type=F32).astype(BF16)
        for j in range(GROUP):
            held[:, h * width + j * HD : h * width + (j + 1) * HD] = c[j * rows : (j + 1) * rows]
        here = (pl.ds(0, rows), pl.ds(h * width, width))
        there = (pl.ds(block * rows, rows), pl.ds(h * width, width))
        copies.append(pltpu.make_async_copy(held.at[here], out_ref.at[there], sems.at[h]))
        copies[-1].start()
    for copy in copies:
        copy.wait()


def contexts(block, weights, values_a, values_b, out=None):
    heads, _, span = weights.shape
    rows = REACH
    feats = heads * HD
    whole = pl.BlockSpec(memory_space=pltpu.VMEM)
    more = () if out is None else (out,)
    return pl.pallas_call(
        functools.partial(context_kernel, block),
        in_specs=[whole] * 3 + [pl.BlockSpec(memory_space=pl.ANY)] * len(more),
        out_specs=pl.BlockSpec(memory_space=pl.ANY),
        out_shape=jax.ShapeDtypeStruct((2 * rows, GROUP * feats), BF16),
        scratch_shapes=[
            pltpu.VMEM((rows, GROUP * feats), BF16),
            pltpu.SemaphoreType.DMA((heads,)),
        ],
        input_output_aliases={3: 0} if more else {},
        compiler_params=params(),
        cost_estimate=cost(2 * heads * GROUP * rows * span * HD, 6 * rows * heads * GROUP * HD),
        name="context",
    )(weights, values_a, values_b, *more)


def after(*values):
    return lax.optimization_barrier(values)


def place(p):
    z, x = (p, 0) if p < 4 else (7 - p, 1)
    return z * 2 + x


def ring(signs):
    return [
        (y * 16 + place(p) * 2 + c, y * 16 + place((p + sign) % 8) * 2 + c)
        for y, sign in enumerate(signs)
        for p in range(8)
        for c in range(2)
    ]


def on_ring(hidden, norm_gain, key_weight, value_weight, queries, segment_ids):
    both = ("groups", "dp")
    key_way, value_way = ring((1, -1)), ring((-1, 1))
    other_group = [(i, (i + 16) % 32) for i in range(32)]
    other_core = [(i, i ^ 1) for i in range(16)]

    def send(value, way):
        return lax.ppermute(value, both, way)

    def swap(value):
        return lax.ppermute(value, "dp", other_core)

    ids = jnp.stack([lax.axis_index("dp"), lax.axis_index("groups")]).astype(jnp.int32)
    mine, theirs = normalise(ids, hidden, norm_gain)
    other = [swap(t) for t in theirs]
    k1, v1 = send(key_weight, key_way), send(value_weight, value_way)
    behind = from_behind(segment_ids, "dp", 1)
    k1, mine, behind = after(k1, mine, behind)
    k2, v2 = send(k1, key_way), send(v1, value_way)
    k1b, yv1 = send(key_weight, value_way), send(v1, other_group)
    k3, v3 = send(k2, key_way), send(v2, value_way)
    yk2 = send(k2, other_group)

    key_part = project((0, -1, -2), mine, other, [key_weight, k1, k2])
    k3, yv1, key_part = after(k3, yv1, key_part)
    k4, yk3 = send(k3, key_way), send(k3, other_group)
    cos, sin, bias = tables(ids, segment_ids, behind)
    key_part = project((-3, 2, 1), mine, other, [k3, yk2, k1b], key_part)
    v3, key_part, cos, sin, bias = after(v3, key_part, cos, sin, bias)
    v4 = send(v3, value_way)
    yk3, v3y = after(yk3, v3)
    yv3 = send(v3y, other_group)
    v2b = send(yv1, key_way)
    value_part = project((0, 1, 2, -1, 3), mine, other, [value_weight, v1, v2, yv1, v3])

    own_k, *other_k = project((-4, 3), mine, other, [k4, yk3], key_part, 2)
    *other_k, value_part = after(*[swap(o) for o in other_k], value_part)
    keys, head_keys, tail = finish(keys_kernel, "keys", own_k, cos, sin, *other_k)
    prev_keys = from_behind(tail, "dp", 1)
    p1 = softmax_weights(1, queries, keys, keys, bias)
    value_part, p1, prev_keys = after(value_part, p1, prev_keys)
    own_v, other_v = project((4, -2, -3), mine, other, [v4, v2b, yv3], value_part)
    p0 = softmax_weights(0, queries, prev_keys, head_keys, bias)
    other_v, p0 = after(swap(other_v), p0)
    values, head_values, tail = finish(values_kernel, "values", own_v, other_v)
    prev_values = from_behind(tail, "dp", 1)
    later = contexts(1, p1, values, values)
    return contexts(0, p0, prev_values, head_values, later)


def rotary(block, positions):
    half = HD // 2
    freqs = 500000.0 ** (-(2.0 * jnp.arange(half, dtype=jnp.float32)) / HD)
    angles = positions[:, None] * freqs[None, :]
    cosine = jnp.cos(angles)[:, None, :]
    sine = jnp.sin(angles)[:, None, :]
    first = block[..., :half]
    second = block[..., half:]
    return jnp.concatenate(
        [first * cosine - second * sine, second * cosine + first * sine], axis=-1
    )


def on_any(hidden, norm_gain, key_weight, value_weight, queries, segment_ids):
    whole = lax.all_gather(hidden, "tensor", axis=1, tiled=True)
    states = whole.astype(jnp.float32)
    meansq = jnp.mean(states * states, axis=-1, keepdims=True)
    normed = (states * lax.rsqrt(meansq + EPS) * norm_gain.astype(jnp.float32)).astype(BF16)
    local_rows = normed.shape[0]
    head_cols = key_weight.shape[1]

    def add_rows(piece):
        return jnp.dot(normed, piece, preferred_element_type=jnp.float32)

    key_sum = add_rows(lax.all_gather(key_weight, "dp", axis=0, tiled=True))
    value_sum = add_rows(lax.all_gather(value_weight, "dp", axis=0, tiled=True))
    keys_raw = key_sum.astype(BF16)
    values = value_sum.astype(BF16)
    earlier_keys, earlier_values, earlier_segs = from_behind(
        (keys_raw, values, segment_ids), "dp", 1
    )
    earlier_count = earlier_keys.shape[0]
    has_earlier = lax.axis_index("dp") > 0
    earlier_segs = jnp.where(has_earlier, earlier_segs, -1)
    window_segs = jnp.concatenate([earlier_segs, segment_ids], axis=0)
    window_len = window_segs.shape[0]
    window_index = jnp.arange(window_len, dtype=jnp.int32)
    same_seg = window_segs[:, None] == window_segs[None, :]
    before = window_index[None, :] < window_index[:, None]
    positions = jnp.sum((same_seg & before).astype(jnp.int32), axis=1)
    heads_here = head_cols // HD
    window_raw = (
        jnp.concatenate([earlier_keys, keys_raw], axis=0)
        .astype(jnp.float32)
        .reshape(window_len, heads_here, HD)
    )
    window_keys = rotary(window_raw, positions.astype(jnp.float32)).astype(BF16)
    window_values = jnp.concatenate([earlier_values, values], axis=0).reshape(
        window_len, heads_here, HD
    )
    query_heads = queries.reshape(local_rows, heads_here, GROUP, HD)
    scale = 1.0 / HD**0.5
    scores = (
        jnp.einsum("tkgd,skd->kgts", query_heads, window_keys, preferred_element_type=jnp.float32)
        * scale
    )
    query_pos = jnp.arange(local_rows, dtype=jnp.int32)[:, None] + earlier_count
    allowed = (window_index[None, :] <= query_pos) & (segment_ids[:, None] == window_segs[None, :])
    masked = jnp.where(allowed, scores, -1e30)
    largest = jnp.max(masked, axis=-1, keepdims=True)
    expd = jnp.where(allowed, jnp.exp(masked - largest), 0.0)
    weights = (expd / jnp.sum(expd, axis=-1, keepdims=True)).astype(BF16)
    out_heads = jnp.einsum(
        "kgts,skd->tkgd", weights, window_values, preferred_element_type=jnp.float32
    )
    return out_heads.reshape(local_rows, heads_here * GROUP * HD).astype(BF16)


def solution(mesh):
    in_specs = (
        P(("groups", "dp"), "tensor"),
        P(),
        P("dp", "tensor"),
        P("dp", "tensor"),
        P(("groups", "dp"), "tensor"),
        P(("groups", "dp")),
    )
    out_specs = P(("groups", "dp"), "tensor")
    small = (mesh.shape["groups"], mesh.shape["dp"], mesh.shape["tensor"]) == (2, 16, 1)
    return jax.shard_map(
        on_ring if small else on_any,
        mesh=mesh,
        in_specs=in_specs,
        out_specs=out_specs,
        check_vma=False,
    )
```

```python
import functools
import math

import jax
import jax.numpy as jnp
import numpy as np
from jax import lax
from jax.experimental import pallas as pl
from jax.experimental.pallas import tpu as pltpu
from jax.sharding import PartitionSpec as P

HD = 128
GROUP = 8
REACH = 128
EPS = 1e-05
F32 = jnp.float32
BF16 = jnp.bfloat16
VMEM_LIMIT = 16 * 1024 * 1024


def params():
    return pltpu.CompilerParams(vmem_limit_bytes=VMEM_LIMIT)


def cost(flops, nbytes, trans=0):
    return pl.CostEstimate(flops=flops, bytes_accessed=nbytes, transcendentals=trans)


def from_behind(value, axis, steps):
    count = lax.axis_size(axis)
    initial, last = (max(0, -steps), min(count, count - steps))
    return lax.ppermute(value, axis, [(source, source + steps) for source in range(initial, last)])


def norm_kernel(h_ref, g_ref, mine_ref, *theirs):
    width = h_ref.shape[1]
    half = width // 16
    x = h_ref[...].astype(F32)
    meansq = jnp.sum(x * x, axis=-1, keepdims=True) * (1.0 / width)
    scale = lax.rsqrt(meansq + EPS)
    first = lax.rem(lax.axis_index("dp"), 2) == 0
    for b in range(8):
        lo = slice(2 * b * half, (2 * b + 1) * half)
        hi = slice((2 * b + 1) * half, (2 * b + 2) * half)
        n_lo = h_ref[:, lo].astype(F32) * scale * g_ref[:, lo].astype(F32)
        n_hi = h_ref[:, hi].astype(F32) * scale * g_ref[:, hi].astype(F32)
        out = slice(b * half, (b + 1) * half)
        mine_ref[:, out] = jnp.where(first, n_lo, n_hi).astype(BF16)
        other = jnp.where(first, n_hi, n_lo).astype(BF16)
        for part, theirs_ref in enumerate(theirs):

            @pl.when(pl.program_id(0) // (pl.num_programs(0) // len(theirs)) == part)
            def _():
                theirs_ref[:, out] = other


def normalise(hidden, gain):
    rows, width = hidden.shape
    step = 64
    mine = jax.ShapeDtypeStruct((rows, width // 2), BF16)
    parts = 2
    theirs = jax.ShapeDtypeStruct((rows // parts, width // 2), BF16)
    last = rows // step // parts - 1
    mine, *theirs = pl.pallas_call(
        norm_kernel,
        grid=(rows // step,),
        in_specs=[
            pl.BlockSpec((step, width), lambda i: (i, 0)),
            pl.BlockSpec((1, width), lambda i: (0, 0)),
        ],
        out_specs=[pl.BlockSpec((step, width // 2), lambda i: (i, 0))]
        + [
            pl.BlockSpec(
                (step, width // 2),
                functools.partial(lambda p, i: (jnp.clip(i - p * (last + 1), 0, last), 0), p),
            )
            for p in range(parts)
        ],
        out_shape=[mine] + [theirs] * parts,
        compiler_params=params(),
        cost_estimate=cost(8 * rows * width, 4 * rows * width),
        name="norm",
    )(hidden, gain.reshape(1, width))
    return mine, theirs


def block_at(step):
    me = lax.axis_index("dp")
    z, x = lax.div(me, 4), lax.rem(lax.div(me, 2), 2)
    p = jnp.where(x == 0, z, 7 - z) + jnp.where(lax.axis_index("groups") == 0, step, -step)
    p = jnp.where(p < 0, p + 8, p)
    p = jnp.where(p > 7, p - 8, p)
    return jnp.where(p < 4, 2 * p, 15 - 2 * p)


def project_kernel(steps, parts, carried, xa_ref, *refs):
    count = len(steps)
    others, refs = refs[:parts], refs[parts:]
    weights, refs = refs[:count], refs[count:]
    before, outs = refs[:carried], refs[carried:]
    depth = weights[0].shape[0]
    columns = [pl.ds(pl.multiple_of(block_at(step) * depth, depth), depth) for step in steps]
    x = [jnp.concatenate([ref[:, c] for c in columns], axis=1) for ref in (xa_ref, *others)]
    w = jnp.concatenate([ref[...] for ref in weights], axis=0)
    total = jnp.dot(jnp.concatenate(x, axis=0), w, preferred_element_type=F32)
    held = jnp.concatenate([ref[...] for ref in before], axis=0) if carried else None
    total = held + total if carried else total
    at = 0
    for ref in outs:
        ref[...] = total[at : at + ref.shape[0]]
        at += ref.shape[0]


def project(steps, xa, others, weights, before=(), split=1):
    rows = xa.shape[0]
    depth, feats = weights[0].shape
    outs = [jax.ShapeDtypeStruct((rows, feats), F32)]
    outs += [jax.ShapeDtypeStruct((rows // split, feats), F32)] * split
    whole = pl.BlockSpec(memory_space=pltpu.VMEM)
    operands = [xa, *others, *weights, *before]
    return pl.pallas_call(
        functools.partial(project_kernel, steps, len(others), len(before)),
        in_specs=[whole] * len(operands),
        out_specs=[whole] * len(outs),
        out_shape=outs,
        compiler_params=params(),
        cost_estimate=cost(
            4 * rows * depth * feats * len(weights), 2 * depth * feats * len(weights) + 4 * rows * 4096
        ),
        name="project",
    )(*operands)


def tables_kernel(own_ref, behind_ref, freq_ref, cos_ref, sin_ref, bias_ref):
    own = own_ref[...]
    rows = own.shape[1]
    behind = jnp.where(lax.axis_index("dp") > 0, behind_ref[:, rows - REACH :], -1)
    window = jnp.concatenate([behind, own], axis=1)
    shape = (REACH, 2 * REACH)
    r, c = lax.broadcasted_iota(jnp.int32, shape, 0), lax.broadcasted_iota(jnp.int32, shape, 1)
    freq = freq_ref[...]
    for block in range(rows // REACH):
        keys = window[:, block * REACH : (block + 2) * REACH]
        mine = jnp.sum(jnp.where(c == r + REACH, keys, 0), axis=1, keepdims=True)
        same = mine == keys
        bias_ref[block] = jnp.where(same & (c <= r + REACH), 0.0, -1e30)
        position = jnp.sum(jnp.where(same & (c < r + REACH), 1.0, 0.0), axis=1, keepdims=True)
        angle = position * freq
        at = slice(block * REACH, (block + 1) * REACH)
        sign = jnp.where(lax.broadcasted_iota(jnp.int32, (REACH, HD), 1) < HD // 2, -1.0, 1.0)
        cos_ref[at, :] = jnp.cos(angle)
        sin_ref[at, :] = jnp.sin(angle) * sign


def tables(own, behind):
    rows = own.shape[0]
    half = np.arange(HD // 2, dtype=np.float32)
    freq = np.float32(500000.0) ** (-(2.0 * half) / np.float32(HD))
    freq = jnp.asarray(np.concatenate([freq, freq]).astype(np.float32).reshape(1, HD))
    whole = pl.BlockSpec(memory_space=pltpu.VMEM)
    return pl.pallas_call(
        tables_kernel,
        in_specs=[whole] * 3,
        out_specs=[whole] * 3,
        out_shape=[
            jax.ShapeDtypeStruct((rows, HD), F32),
            jax.ShapeDtypeStruct((rows, HD), F32),
            jax.ShapeDtypeStruct((rows // REACH, REACH, 2 * REACH), F32),
        ],
        compiler_params=params(),
        cost_estimate=cost(20 * rows * 2 * REACH, 16 * rows * REACH, 2 * rows * HD),
        name="tables",
    )(own.reshape(1, rows), behind.reshape(1, rows), freq)


def keys_kernel(a_ref, cos_ref, sin_ref, *refs):
    cos, sin = cos_ref[...], sin_ref[...]
    others, (out_ref, head_ref, tail_ref) = refs[:-3], refs[-3:]
    rows = out_ref.shape[0]
    for h in range(a_ref.shape[1] // HD):
        at = slice(h * HD, (h + 1) * HD)
        b = jnp.concatenate([ref[:, at] for ref in others], axis=0)
        raw = (a_ref[:, at] + b).astype(BF16).astype(F32)
        out = (raw * cos + pltpu.roll(raw, HD // 2, 1) * sin).astype(BF16)
        out_ref[:, at] = out
        head_ref[:, at] = out[:REACH]
        tail_ref[:, at] = out[rows - REACH :]


def values_kernel(a_ref, *refs):
    others, (out_ref, head_ref, tail_ref) = refs[:-3], refs[-3:]
    rows = out_ref.shape[0]
    out = (a_ref[...] + jnp.concatenate([ref[...] for ref in others], axis=0)).astype(BF16)
    out_ref[...] = out
    head_ref[...] = out[:REACH]
    tail_ref[...] = out[rows - REACH :]


def finish(kernel, name, *operands):
    rows, feats = operands[0].shape
    return pl.pallas_call(
        kernel,
        out_shape=[
            jax.ShapeDtypeStruct((rows, feats), BF16),
            jax.ShapeDtypeStruct((REACH, feats), BF16),
            jax.ShapeDtypeStruct((REACH, feats), BF16),
        ],
        compiler_params=params(),
        cost_estimate=cost(6 * rows * feats, 10 * rows * feats),
        name=name,
    )(*operands)


def scores_kernel(block, q_ref, ka_ref, kb_ref, bias_ref, out_ref):
    rows = REACH
    bias = bias_ref[block]
    ones = jnp.ones((2 * rows, rows), BF16)
    scale = math.log2(math.e) / HD**0.5
    for h in range(out_ref.shape[0]):
        at = slice(h * HD, (h + 1) * HD)
        keys = jnp.concatenate([ka_ref[:rows, at], kb_ref[-rows:, at]], axis=0)
        for j in range(GROUP):
            column = (h * GROUP + j) * HD
            q = q_ref[block * rows : (block + 1) * rows, column : column + HD]
            s = lax.dot_general(q, keys, (((1,), (1,)), ((), ())), preferred_element_type=F32)
            s = s * scale + bias
            e = jnp.exp2(s - jnp.max(s, axis=-1, keepdims=True))
            total = jnp.dot(e.astype(BF16), ones, preferred_element_type=F32)
            inverse = 1.0 / total
            w = e * jnp.concatenate([inverse, inverse], axis=1)
            out_ref[h, j * rows : (j + 1) * rows, :] = w.astype(BF16)


def softmax_weights(block, queries, keys_a, keys_b, bias):
    rows = REACH
    heads = keys_a.shape[1] // HD
    whole = pl.BlockSpec(memory_space=pltpu.VMEM)
    return pl.pallas_call(
        functools.partial(scores_kernel, block),
        in_specs=[whole] * 4,
        out_specs=whole,
        out_shape=jax.ShapeDtypeStruct((heads, GROUP * rows, 2 * rows), BF16),
        compiler_params=params(),
        cost_estimate=cost(
            4 * heads * GROUP * rows * rows * HD, 6 * rows * heads * GROUP * HD, 2 * heads * GROUP * rows * rows
        ),
        name="scores",
    )(queries, keys_a, keys_b, bias)


def context_kernel(block, p_ref, va_ref, vb_ref, *refs):
    out_ref, held, sems = refs[-3:]
    rows = held.shape[0]
    width = GROUP * HD
    copies = []
    for h in range(p_ref.shape[0]):
        at = slice(h * HD, (h + 1) * HD)
        values = jnp.concatenate([va_ref[:rows, at], vb_ref[-rows:, at]], axis=0)
        c = jnp.dot(p_ref[h], values, preferred_element_type=F32).astype(BF16)
        for j in range(GROUP):
            held[:, h * width + j * HD : h * width + (j + 1) * HD] = c[j * rows : (j + 1) * rows]
        here = (pl.ds(0, rows), pl.ds(h * width, width))
        there = (pl.ds(block * rows, rows), pl.ds(h * width, width))
        copies.append(pltpu.make_async_copy(held.at[here], out_ref.at[there], sems.at[h]))
        copies[-1].start()
    for copy in copies:
        copy.wait()


def contexts(block, weights, values_a, values_b, out=None):
    heads, _, span = weights.shape
    rows = REACH
    feats = heads * HD
    whole = pl.BlockSpec(memory_space=pltpu.VMEM)
    more = () if out is None else (out,)
    return pl.pallas_call(
        functools.partial(context_kernel, block),
        in_specs=[whole] * 3 + [pl.BlockSpec(memory_space=pl.ANY)] * len(more),
        out_specs=pl.BlockSpec(memory_space=pl.ANY),
        out_shape=jax.ShapeDtypeStruct((2 * rows, GROUP * feats), BF16),
        scratch_shapes=[
            pltpu.VMEM((rows, GROUP * feats), BF16),
            pltpu.SemaphoreType.DMA((heads,)),
        ],
        input_output_aliases={3: 0} if more else {},
        compiler_params=params(),
        cost_estimate=cost(2 * heads * GROUP * rows * span * HD, 6 * rows * heads * GROUP * HD),
        name="context",
    )(weights, values_a, values_b, *more)


def after(*values):
    return lax.optimization_barrier(values)


def place(p):
    z, x = (p, 0) if p < 4 else (7 - p, 1)
    return z * 2 + x


def ring(signs):
    return [
        (y * 16 + place(p) * 2 + c, y * 16 + place((p + sign) % 8) * 2 + c)
        for y, sign in enumerate(signs)
        for p in range(8)
        for c in range(2)
    ]


def on_ring(hidden, norm_gain, key_weight, value_weight, queries, segment_ids):
    both = ("groups", "dp")
    key_way, value_way = ring((1, -1)), ring((-1, 1))
    other_group = [(i, (i + 16) % 32) for i in range(32)]
    other_core = [(i, i ^ 1) for i in range(16)]

    def send(value, way):
        return lax.ppermute(value, both, way)

    def swap(value):
        return lax.ppermute(value, "dp", other_core)

    mine, theirs = normalise(hidden, norm_gain)
    other = [swap(t) for t in theirs]
    k1, v1 = send(key_weight, key_way), send(value_weight, value_way)
    behind = from_behind(segment_ids, "dp", 1)
    k1, mine, behind = after(k1, mine, behind)
    k2, v2 = send(k1, key_way), send(v1, value_way)
    k1b, yv1 = send(key_weight, value_way), send(v1, other_group)
    k3, v3 = send(k2, key_way), send(v2, value_way)
    yk2 = send(k2, other_group)

    key_part = project((0, -1, -2), mine, other, [key_weight, k1, k2])
    k3, yv1, key_part = after(k3, yv1, key_part)
    k4, yk3 = send(k3, key_way), send(k3, other_group)
    cos, sin, bias = tables(segment_ids, behind)
    key_part = project((-3, 2, 1), mine, other, [k3, yk2, k1b], key_part)
    v3, key_part, cos, sin, bias = after(v3, key_part, cos, sin, bias)
    v4 = send(v3, value_way)
    yk3, v3y = after(yk3, v3)
    yv3 = send(v3y, other_group)
    v2b = send(yv1, key_way)
    value_part = project((0, 1, 2, -1, 3), mine, other, [value_weight, v1, v2, yv1, v3])

    own_k, *other_k = project((-4, 3), mine, other, [k4, yk3], key_part, 2)
    *other_k, value_part = after(*[swap(o) for o in other_k], value_part)
    keys, head_keys, tail = finish(keys_kernel, "keys", own_k, cos, sin, *other_k)
    prev_keys = from_behind(tail, "dp", 1)
    p1 = softmax_weights(1, queries, keys, keys, bias)
    value_part, p1, prev_keys = after(value_part, p1, prev_keys)
    own_v, other_v = project((4, -2, -3), mine, other, [v4, v2b, yv3], value_part)
    p0 = softmax_weights(0, queries, prev_keys, head_keys, bias)
    other_v, p0 = after(swap(other_v), p0)
    values, head_values, tail = finish(values_kernel, "values", own_v, other_v)
    prev_values = from_behind(tail, "dp", 1)
    later = contexts(1, p1, values, values)
    return contexts(0, p0, prev_values, head_values, later)


def rotary(block, positions):
    half = HD // 2
    freqs = 500000.0 ** (-(2.0 * jnp.arange(half, dtype=jnp.float32)) / HD)
    angles = positions[:, None] * freqs[None, :]
    cosine = jnp.cos(angles)[:, None, :]
    sine = jnp.sin(angles)[:, None, :]
    first = block[..., :half]
    second = block[..., half:]
    return jnp.concatenate(
        [first * cosine - second * sine, second * cosine + first * sine], axis=-1
    )


def on_any(hidden, norm_gain, key_weight, value_weight, queries, segment_ids):
    whole = lax.all_gather(hidden, "tensor", axis=1, tiled=True)
    states = whole.astype(jnp.float32)
    meansq = jnp.mean(states * states, axis=-1, keepdims=True)
    normed = (states * lax.rsqrt(meansq + EPS) * norm_gain.astype(jnp.float32)).astype(BF16)
    local_rows = normed.shape[0]
    head_cols = key_weight.shape[1]

    def add_rows(piece):
        return jnp.dot(normed, piece, preferred_element_type=jnp.float32)

    key_sum = add_rows(lax.all_gather(key_weight, "dp", axis=0, tiled=True))
    value_sum = add_rows(lax.all_gather(value_weight, "dp", axis=0, tiled=True))
    keys_raw = key_sum.astype(BF16)
    values = value_sum.astype(BF16)
    earlier_keys, earlier_values, earlier_segs = from_behind(
        (keys_raw, values, segment_ids), "dp", 1
    )
    earlier_count = earlier_keys.shape[0]
    has_earlier = lax.axis_index("dp") > 0
    earlier_segs = jnp.where(has_earlier, earlier_segs, -1)
    window_segs = jnp.concatenate([earlier_segs, segment_ids], axis=0)
    window_len = window_segs.shape[0]
    window_index = jnp.arange(window_len, dtype=jnp.int32)
    same_seg = window_segs[:, None] == window_segs[None, :]
    before = window_index[None, :] < window_index[:, None]
    positions = jnp.sum((same_seg & before).astype(jnp.int32), axis=1)
    heads_here = head_cols // HD
    window_raw = (
        jnp.concatenate([earlier_keys, keys_raw], axis=0)
        .astype(jnp.float32)
        .reshape(window_len, heads_here, HD)
    )
    window_keys = rotary(window_raw, positions.astype(jnp.float32)).astype(BF16)
    window_values = jnp.concatenate([earlier_values, values], axis=0).reshape(
        window_len, heads_here, HD
    )
    query_heads = queries.reshape(local_rows, heads_here, GROUP, HD)
    scale = 1.0 / HD**0.5
    scores = (
        jnp.einsum("tkgd,skd->kgts", query_heads, window_keys, preferred_element_type=jnp.float32)
        * scale
    )
    query_pos = jnp.arange(local_rows, dtype=jnp.int32)[:, None] + earlier_count
    allowed = (window_index[None, :] <= query_pos) & (segment_ids[:, None] == window_segs[None, :])
    masked = jnp.where(allowed, scores, -1e30)
    largest = jnp.max(masked, axis=-1, keepdims=True)
    expd = jnp.where(allowed, jnp.exp(masked - largest), 0.0)
    weights = (expd / jnp.sum(expd, axis=-1, keepdims=True)).astype(BF16)
    out_heads = jnp.einsum(
        "kgts,skd->tkgd", weights, window_values, preferred_element_type=jnp.float32
    )
    return out_heads.reshape(local_rows, heads_here * GROUP * HD).astype(BF16)


def solution(mesh):
    in_specs = (
        P(("groups", "dp"), "tensor"),
        P(),
        P("dp", "tensor"),
        P("dp", "tensor"),
        P(("groups", "dp"), "tensor"),
        P(("groups", "dp")),
    )
    out_specs = P(("groups", "dp"), "tensor")
    small = (mesh.shape["groups"], mesh.shape["dp"], mesh.shape["tensor"]) == (2, 16, 1)
    return jax.shard_map(
        on_ring if small else on_any,
        mesh=mesh,
        in_specs=in_specs,
        out_specs=out_specs,
        check_vma=False,
    )
```

```python
import functools
import math

import jax
import jax.numpy as jnp
import numpy as np
from jax import lax
from jax.experimental import pallas as pl
from jax.experimental.pallas import tpu as pltpu
from jax.sharding import PartitionSpec as P

HD = 128
GROUP = 8
REACH = 128
EPS = 1e-05
F32 = jnp.float32
BF16 = jnp.bfloat16
VMEM_LIMIT = 16 * 1024 * 1024


def params():
    return pltpu.CompilerParams(vmem_limit_bytes=VMEM_LIMIT)


def cost(flops, nbytes, trans=0):
    return pl.CostEstimate(flops=flops, bytes_accessed=nbytes, transcendentals=trans)


def from_behind(value, axis, steps):
    count = lax.axis_size(axis)
    initial, last = (max(0, -steps), min(count, count - steps))
    return lax.ppermute(value, axis, [(source, source + steps) for source in range(initial, last)])


def norm_kernel(h_ref, g_ref, mine_ref, *theirs):
    width = h_ref.shape[1]
    half = width // 16
    x = h_ref[...].astype(F32)
    meansq = jnp.sum(x * x, axis=-1, keepdims=True) * (1.0 / width)
    scale = lax.rsqrt(meansq + EPS)
    first = lax.rem(lax.axis_index("dp"), 2) == 0
    for b in range(8):
        lo = slice(2 * b * half, (2 * b + 1) * half)
        hi = slice((2 * b + 1) * half, (2 * b + 2) * half)
        n_lo = h_ref[:, lo].astype(F32) * scale * g_ref[:, lo].astype(F32)
        n_hi = h_ref[:, hi].astype(F32) * scale * g_ref[:, hi].astype(F32)
        out = slice(b * half, (b + 1) * half)
        mine_ref[:, out] = jnp.where(first, n_lo, n_hi).astype(BF16)
        other = jnp.where(first, n_hi, n_lo).astype(BF16)
        for part, theirs_ref in enumerate(theirs):

            @pl.when(pl.program_id(0) // (pl.num_programs(0) // len(theirs)) == part)
            def _():
                theirs_ref[:, out] = other


def normalise(hidden, gain):
    rows, width = hidden.shape
    step = 64
    mine = jax.ShapeDtypeStruct((rows, width // 2), BF16)
    parts = 2
    theirs = jax.ShapeDtypeStruct((rows // parts, width // 2), BF16)
    last = rows // step // parts - 1
    mine, *theirs = pl.pallas_call(
        norm_kernel,
        grid=(rows // step,),
        in_specs=[
            pl.BlockSpec((step, width), lambda i: (i, 0)),
            pl.BlockSpec((1, width), lambda i: (0, 0)),
        ],
        out_specs=[pl.BlockSpec((step, width // 2), lambda i: (i, 0))]
        + [
            pl.BlockSpec(
                (step, width // 2),
                functools.partial(lambda p, i: (jnp.clip(i - p * (last + 1), 0, last), 0), p),
            )
            for p in range(parts)
        ],
        out_shape=[mine] + [theirs] * parts,
        compiler_params=params(),
        cost_estimate=cost(8 * rows * width, 4 * rows * width),
        name="norm",
    )(hidden, gain.reshape(1, width))
    return mine, theirs


def block_at(step):
    me = lax.axis_index("dp")
    z, x = lax.div(me, 4), lax.rem(lax.div(me, 2), 2)
    p = jnp.where(x == 0, z, 7 - z) + jnp.where(lax.axis_index("groups") == 0, step, -step)
    p = jnp.where(p < 0, p + 8, p)
    p = jnp.where(p > 7, p - 8, p)
    return jnp.where(p < 4, 2 * p, 15 - 2 * p)


def project_kernel(steps, parts, carried, xa_ref, *refs):
    count = len(steps)
    others, refs = refs[:parts], refs[parts:]
    weights, refs = refs[:count], refs[count:]
    before, outs = refs[:carried], refs[carried:]
    depth = weights[0].shape[0]
    columns = [pl.ds(pl.multiple_of(block_at(step) * depth, depth), depth) for step in steps]
    x = [jnp.concatenate([ref[:, c] for c in columns], axis=1) for ref in (xa_ref, *others)]
    w = jnp.concatenate([ref[...] for ref in weights], axis=0)
    total = jnp.dot(jnp.concatenate(x, axis=0), w, preferred_element_type=F32)
    held = jnp.concatenate([ref[...] for ref in before], axis=0) if carried else None
    total = held + total if carried else total
    at = 0
    for ref in outs:
        ref[...] = total[at : at + ref.shape[0]]
        at += ref.shape[0]


def project(steps, xa, others, weights, before=(), split=1):
    rows = xa.shape[0]
    depth, feats = weights[0].shape
    outs = [jax.ShapeDtypeStruct((rows, feats), F32)]
    outs += [jax.ShapeDtypeStruct((rows // split, feats), F32)] * split
    whole = pl.BlockSpec(memory_space=pltpu.VMEM)
    operands = [xa, *others, *weights, *before]
    return pl.pallas_call(
        functools.partial(project_kernel, steps, len(others), len(before)),
        in_specs=[whole] * len(operands),
        out_specs=[whole] * len(outs),
        out_shape=outs,
        compiler_params=params(),
        cost_estimate=cost(
            4 * rows * depth * feats * len(weights), 2 * depth * feats * len(weights) + 4 * rows * 4096
        ),
        name="project",
    )(*operands)


def tables_kernel(own_ref, behind_ref, freq_ref, cos_ref, sin_ref, bias_ref):
    own = own_ref[...]
    rows = own.shape[1]
    behind = jnp.where(lax.axis_index("dp") > 0, behind_ref[:, rows - REACH :], -1)
    window = jnp.concatenate([behind, own], axis=1)
    shape = (REACH, 2 * REACH)
    r, c = lax.broadcasted_iota(jnp.int32, shape, 0), lax.broadcasted_iota(jnp.int32, shape, 1)
    freq = freq_ref[...]
    for block in range(rows // REACH):
        keys = window[:, block * REACH : (block + 2) * REACH]
        mine = jnp.sum(jnp.where(c == r + REACH, keys, 0), axis=1, keepdims=True)
        same = mine == keys
        bias_ref[block] = jnp.where(same & (c <= r + REACH), 0.0, -1e30)
        position = jnp.sum(jnp.where(same & (c < r + REACH), 1.0, 0.0), axis=1, keepdims=True)
        angle = position * freq
        at = slice(block * REACH, (block + 1) * REACH)
        sign = jnp.where(lax.broadcasted_iota(jnp.int32, (REACH, HD), 1) < HD // 2, -1.0, 1.0)
        cos_ref[at, :] = jnp.cos(angle)
        sin_ref[at, :] = jnp.sin(angle) * sign


def tables(own, behind):
    rows = own.shape[0]
    half = np.arange(HD // 2, dtype=np.float32)
    freq = np.float32(500000.0) ** (-(2.0 * half) / np.float32(HD))
    freq = jnp.asarray(np.concatenate([freq, freq]).astype(np.float32).reshape(1, HD))
    whole = pl.BlockSpec(memory_space=pltpu.VMEM)
    return pl.pallas_call(
        tables_kernel,
        in_specs=[whole] * 3,
        out_specs=[whole] * 3,
        out_shape=[
            jax.ShapeDtypeStruct((rows, HD), F32),
            jax.ShapeDtypeStruct((rows, HD), F32),
            jax.ShapeDtypeStruct((rows // REACH, REACH, 2 * REACH), F32),
        ],
        compiler_params=params(),
        cost_estimate=cost(20 * rows * 2 * REACH, 16 * rows * REACH, 2 * rows * HD),
        name="tables",
    )(own.reshape(1, rows), behind.reshape(1, rows), freq)


def keys_kernel(a_ref, cos_ref, sin_ref, *refs):
    cos, sin = cos_ref[...], sin_ref[...]
    others, (out_ref, head_ref, tail_ref) = refs[:-3], refs[-3:]
    rows = out_ref.shape[0]
    for h in range(a_ref.shape[1] // HD):
        at = slice(h * HD, (h + 1) * HD)
        b = jnp.concatenate([ref[:, at] for ref in others], axis=0)
        raw = (a_ref[:, at] + b).astype(BF16).astype(F32)
        out = (raw * cos + pltpu.roll(raw, HD // 2, 1) * sin).astype(BF16)
        out_ref[:, at] = out
        head_ref[:, at] = out[:REACH]
        tail_ref[:, at] = out[rows - REACH :]


def values_kernel(a_ref, *refs):
    others, (out_ref, head_ref, tail_ref) = refs[:-3], refs[-3:]
    rows = out_ref.shape[0]
    out = (a_ref[...] + jnp.concatenate([ref[...] for ref in others], axis=0)).astype(BF16)
    out_ref[...] = out
    head_ref[...] = out[:REACH]
    tail_ref[...] = out[rows - REACH :]


def finish(kernel, name, *operands):
    rows, feats = operands[0].shape
    return pl.pallas_call(
        kernel,
        out_shape=[
            jax.ShapeDtypeStruct((rows, feats), BF16),
            jax.ShapeDtypeStruct((REACH, feats), BF16),
            jax.ShapeDtypeStruct((REACH, feats), BF16),
        ],
        compiler_params=params(),
        cost_estimate=cost(6 * rows * feats, 10 * rows * feats),
        name=name,
    )(*operands)


def scores_kernel(block, q_ref, ka_ref, kb_ref, bias_ref, out_ref):
    rows = REACH
    bias = bias_ref[block]
    ones = jnp.ones((2 * rows, rows), BF16)
    scale = math.log2(math.e) / HD**0.5
    for h in range(out_ref.shape[0]):
        at = slice(h * HD, (h + 1) * HD)
        keys = jnp.concatenate([ka_ref[:rows, at], kb_ref[-rows:, at]], axis=0)
        for j in range(GROUP):
            column = (h * GROUP + j) * HD
            q = q_ref[block * rows : (block + 1) * rows, column : column + HD]
            s = lax.dot_general(q, keys, (((1,), (1,)), ((), ())), preferred_element_type=F32)
            s = s * scale + bias
            e = jnp.exp2(s - jnp.max(s, axis=-1, keepdims=True))
            total = jnp.dot(e.astype(BF16), ones, preferred_element_type=F32)
            inverse = 1.0 / total
            w = e * jnp.concatenate([inverse, inverse], axis=1)
            out_ref[h, j * rows : (j + 1) * rows, :] = w.astype(BF16)


def softmax_weights(block, queries, keys_a, keys_b, bias):
    rows = REACH
    heads = keys_a.shape[1] // HD
    whole = pl.BlockSpec(memory_space=pltpu.VMEM)
    return pl.pallas_call(
        functools.partial(scores_kernel, block),
        in_specs=[whole] * 4,
        out_specs=whole,
        out_shape=jax.ShapeDtypeStruct((heads, GROUP * rows, 2 * rows), BF16),
        compiler_params=params(),
        cost_estimate=cost(
            4 * heads * GROUP * rows * rows * HD, 6 * rows * heads * GROUP * HD, 2 * heads * GROUP * rows * rows
        ),
        name="scores",
    )(queries, keys_a, keys_b, bias)


def context_kernel(block, p_ref, va_ref, vb_ref, *refs):
    out_ref, held, sems = refs[-3:]
    rows = held.shape[0]
    width = GROUP * HD
    copies = []
    for h in range(p_ref.shape[0]):
        at = slice(h * HD, (h + 1) * HD)
        values = jnp.concatenate([va_ref[:rows, at], vb_ref[-rows:, at]], axis=0)
        for part in range(2):
            some = GROUP // 2
            p = p_ref[h, part * some * rows : (part + 1) * some * rows, :]
            c = jnp.dot(p, values, preferred_element_type=F32).astype(BF16)
            start = h * width + part * some * HD
            for j in range(some):
                held[:, start + j * HD : start + (j + 1) * HD] = c[j * rows : (j + 1) * rows]
            here = (pl.ds(0, rows), pl.ds(start, some * HD))
            there = (pl.ds(block * rows, rows), pl.ds(start, some * HD))
            copies.append(pltpu.make_async_copy(held.at[here], out_ref.at[there], sems.at[2 * h + part]))
            copies[-1].start()
    for copy in copies:
        copy.wait()


def contexts(block, weights, values_a, values_b, out=None):
    heads, _, span = weights.shape
    rows = REACH
    feats = heads * HD
    whole = pl.BlockSpec(memory_space=pltpu.VMEM)
    more = () if out is None else (out,)
    return pl.pallas_call(
        functools.partial(context_kernel, block),
        in_specs=[whole] * 3 + [pl.BlockSpec(memory_space=pl.ANY)] * len(more),
        out_specs=pl.BlockSpec(memory_space=pl.ANY),
        out_shape=jax.ShapeDtypeStruct((2 * rows, GROUP * feats), BF16),
        scratch_shapes=[
            pltpu.VMEM((rows, GROUP * feats), BF16),
            pltpu.SemaphoreType.DMA((2 * heads,)),
        ],
        input_output_aliases={3: 0} if more else {},
        compiler_params=params(),
        cost_estimate=cost(2 * heads * GROUP * rows * span * HD, 6 * rows * heads * GROUP * HD),
        name="context",
    )(weights, values_a, values_b, *more)


def after(*values):
    return lax.optimization_barrier(values)


def place(p):
    z, x = (p, 0) if p < 4 else (7 - p, 1)
    return z * 2 + x


def ring(signs):
    return [
        (y * 16 + place(p) * 2 + c, y * 16 + place((p + sign) % 8) * 2 + c)
        for y, sign in enumerate(signs)
        for p in range(8)
        for c in range(2)
    ]


def on_ring(hidden, norm_gain, key_weight, value_weight, queries, segment_ids):
    both = ("groups", "dp")
    key_way, value_way = ring((1, -1)), ring((-1, 1))
    other_group = [(i, (i + 16) % 32) for i in range(32)]
    other_core = [(i, i ^ 1) for i in range(16)]

    def send(value, way):
        return lax.ppermute(value, both, way)

    def swap(value):
        return lax.ppermute(value, "dp", other_core)

    mine, theirs = normalise(hidden, norm_gain)
    other = [swap(t) for t in theirs]
    k1, v1 = send(key_weight, key_way), send(value_weight, value_way)
    behind = from_behind(segment_ids, "dp", 1)
    k1, mine, behind = after(k1, mine, behind)
    k2, v2 = send(k1, key_way), send(v1, value_way)
    k1b, yv1 = send(key_weight, value_way), send(v1, other_group)
    k3, v3 = send(k2, key_way), send(v2, value_way)
    yk2 = send(k2, other_group)

    key_part = project((0, -1, -2), mine, other, [key_weight, k1, k2])
    k3, yv1, key_part = after(k3, yv1, key_part)
    k4, yk3 = send(k3, key_way), send(k3, other_group)
    cos, sin, bias = tables(segment_ids, behind)
    key_part = project((-3, 2, 1), mine, other, [k3, yk2, k1b], key_part)
    v3, key_part, cos, sin, bias = after(v3, key_part, cos, sin, bias)
    v4 = send(v3, value_way)
    yk3, v3y = after(yk3, v3)
    yv3 = send(v3y, other_group)
    v2b = send(yv1, key_way)
    value_part = project((0, 1, 2, -1, 3), mine, other, [value_weight, v1, v2, yv1, v3])

    own_k, *other_k = project((-4, 3), mine, other, [k4, yk3], key_part, 2)
    *other_k, value_part = after(*[swap(o) for o in other_k], value_part)
    keys, head_keys, tail = finish(keys_kernel, "keys", own_k, cos, sin, *other_k)
    prev_keys = from_behind(tail, "dp", 1)
    p1 = softmax_weights(1, queries, keys, keys, bias)
    value_part, p1, prev_keys = after(value_part, p1, prev_keys)
    own_v, other_v = project((4, -2, -3), mine, other, [v4, v2b, yv3], value_part)
    p0 = softmax_weights(0, queries, prev_keys, head_keys, bias)
    other_v, p0 = after(swap(other_v), p0)
    values, head_values, tail = finish(values_kernel, "values", own_v, other_v)
    prev_values = from_behind(tail, "dp", 1)
    later = contexts(1, p1, values, values)
    return contexts(0, p0, prev_values, head_values, later)


def rotary(block, positions):
    half = HD // 2
    freqs = 500000.0 ** (-(2.0 * jnp.arange(half, dtype=jnp.float32)) / HD)
    angles = positions[:, None] * freqs[None, :]
    cosine = jnp.cos(angles)[:, None, :]
    sine = jnp.sin(angles)[:, None, :]
    first = block[..., :half]
    second = block[..., half:]
    return jnp.concatenate(
        [first * cosine - second * sine, second * cosine + first * sine], axis=-1
    )


def on_any(hidden, norm_gain, key_weight, value_weight, queries, segment_ids):
    whole = lax.all_gather(hidden, "tensor", axis=1, tiled=True)
    states = whole.astype(jnp.float32)
    meansq = jnp.mean(states * states, axis=-1, keepdims=True)
    normed = (states * lax.rsqrt(meansq + EPS) * norm_gain.astype(jnp.float32)).astype(BF16)
    local_rows = normed.shape[0]
    head_cols = key_weight.shape[1]

    def add_rows(piece):
        return jnp.dot(normed, piece, preferred_element_type=jnp.float32)

    key_sum = add_rows(lax.all_gather(key_weight, "dp", axis=0, tiled=True))
    value_sum = add_rows(lax.all_gather(value_weight, "dp", axis=0, tiled=True))
    keys_raw = key_sum.astype(BF16)
    values = value_sum.astype(BF16)
    earlier_keys, earlier_values, earlier_segs = from_behind(
        (keys_raw, values, segment_ids), "dp", 1
    )
    earlier_count = earlier_keys.shape[0]
    has_earlier = lax.axis_index("dp") > 0
    earlier_segs = jnp.where(has_earlier, earlier_segs, -1)
    window_segs = jnp.concatenate([earlier_segs, segment_ids], axis=0)
    window_len = window_segs.shape[0]
    window_index = jnp.arange(window_len, dtype=jnp.int32)
    same_seg = window_segs[:, None] == window_segs[None, :]
    before = window_index[None, :] < window_index[:, None]
    positions = jnp.sum((same_seg & before).astype(jnp.int32), axis=1)
    heads_here = head_cols // HD
    window_raw = (
        jnp.concatenate([earlier_keys, keys_raw], axis=0)
        .astype(jnp.float32)
        .reshape(window_len, heads_here, HD)
    )
    window_keys = rotary(window_raw, positions.astype(jnp.float32)).astype(BF16)
    window_values = jnp.concatenate([earlier_values, values], axis=0).reshape(
        window_len, heads_here, HD
    )
    query_heads = queries.reshape(local_rows, heads_here, GROUP, HD)
    scale = 1.0 / HD**0.5
    scores = (
        jnp.einsum("tkgd,skd->kgts", query_heads, window_keys, preferred_element_type=jnp.float32)
        * scale
    )
    query_pos = jnp.arange(local_rows, dtype=jnp.int32)[:, None] + earlier_count
    allowed = (window_index[None, :] <= query_pos) & (segment_ids[:, None] == window_segs[None, :])
    masked = jnp.where(allowed, scores, -1e30)
    largest = jnp.max(masked, axis=-1, keepdims=True)
    expd = jnp.where(allowed, jnp.exp(masked - largest), 0.0)
    weights = (expd / jnp.sum(expd, axis=-1, keepdims=True)).astype(BF16)
    out_heads = jnp.einsum(
        "kgts,skd->tkgd", weights, window_values, preferred_element_type=jnp.float32
    )
    return out_heads.reshape(local_rows, heads_here * GROUP * HD).astype(BF16)


def solution(mesh):
    in_specs = (
        P(("groups", "dp"), "tensor"),
        P(),
        P("dp", "tensor"),
        P("dp", "tensor"),
        P(("groups", "dp"), "tensor"),
        P(("groups", "dp")),
    )
    out_specs = P(("groups", "dp"), "tensor")
    small = (mesh.shape["groups"], mesh.shape["dp"], mesh.shape["tensor"]) == (2, 16, 1)
    return jax.shard_map(
        on_ring if small else on_any,
        mesh=mesh,
        in_specs=in_specs,
        out_specs=out_specs,
        check_vma=False,
    )
```

```python
import functools
import math

import jax
import jax.numpy as jnp
import numpy as np
from jax import lax
from jax.experimental import pallas as pl
from jax.experimental.pallas import tpu as pltpu
from jax.sharding import PartitionSpec as P

HD = 128
GROUP = 8
REACH = 128
EPS = 1e-05
F32 = jnp.float32
BF16 = jnp.bfloat16
VMEM_LIMIT = 16 * 1024 * 1024


def params():
    return pltpu.CompilerParams(vmem_limit_bytes=VMEM_LIMIT)


def cost(flops, nbytes, trans=0):
    return pl.CostEstimate(flops=flops, bytes_accessed=nbytes, transcendentals=trans)


def from_behind(value, axis, steps):
    count = lax.axis_size(axis)
    initial, last = (max(0, -steps), min(count, count - steps))
    return lax.ppermute(value, axis, [(source, source + steps) for source in range(initial, last)])


def norm_kernel(h_ref, g_ref, mine_ref, *theirs):
    width = h_ref.shape[1]
    half = width // 16
    x = h_ref[...].astype(F32)
    meansq = jnp.sum(x * x, axis=-1, keepdims=True) * (1.0 / width)
    scale = lax.rsqrt(meansq + EPS)
    first = lax.rem(lax.axis_index("dp"), 2) == 0
    for b in range(8):
        lo = slice(2 * b * half, (2 * b + 1) * half)
        hi = slice((2 * b + 1) * half, (2 * b + 2) * half)
        n_lo = h_ref[:, lo].astype(F32) * scale * g_ref[:, lo].astype(F32)
        n_hi = h_ref[:, hi].astype(F32) * scale * g_ref[:, hi].astype(F32)
        out = slice(b * half, (b + 1) * half)
        mine_ref[:, out] = jnp.where(first, n_lo, n_hi).astype(BF16)
        other = jnp.where(first, n_hi, n_lo).astype(BF16)
        for part, theirs_ref in enumerate(theirs):

            @pl.when(pl.program_id(0) // (pl.num_programs(0) // len(theirs)) == part)
            def _():
                theirs_ref[:, out] = other


def normalise(hidden, gain):
    rows, width = hidden.shape
    step = 64
    mine = jax.ShapeDtypeStruct((rows, width // 2), BF16)
    parts = 2
    theirs = jax.ShapeDtypeStruct((rows // parts, width // 2), BF16)
    last = rows // step // parts - 1
    mine, *theirs = pl.pallas_call(
        norm_kernel,
        grid=(rows // step,),
        in_specs=[
            pl.BlockSpec((step, width), lambda i: (i, 0)),
            pl.BlockSpec((1, width), lambda i: (0, 0)),
        ],
        out_specs=[pl.BlockSpec((step, width // 2), lambda i: (i, 0))]
        + [
            pl.BlockSpec(
                (step, width // 2),
                functools.partial(lambda p, i: (jnp.clip(i - p * (last + 1), 0, last), 0), p),
            )
            for p in range(parts)
        ],
        out_shape=[mine] + [theirs] * parts,
        compiler_params=params(),
        cost_estimate=cost(8 * rows * width, 4 * rows * width),
        name="norm",
    )(hidden, gain.reshape(1, width))
    return mine, theirs


def block_at(step):
    me = lax.axis_index("dp")
    z, x = lax.div(me, 4), lax.rem(lax.div(me, 2), 2)
    p = jnp.where(x == 0, z, 7 - z) + jnp.where(lax.axis_index("groups") == 0, step, -step)
    p = jnp.where(p < 0, p + 8, p)
    p = jnp.where(p > 7, p - 8, p)
    return jnp.where(p < 4, 2 * p, 15 - 2 * p)


def project_kernel(steps, parts, carried, xa_ref, *refs):
    count = len(steps)
    others, refs = refs[:parts], refs[parts:]
    weights, refs = refs[:count], refs[count:]
    before, outs = refs[:carried], refs[carried:]
    depth = weights[0].shape[0]
    columns = [pl.ds(pl.multiple_of(block_at(step) * depth, depth), depth) for step in steps]
    x = [jnp.concatenate([ref[:, c] for c in columns], axis=1) for ref in (xa_ref, *others)]
    w = jnp.concatenate([ref[...] for ref in weights], axis=0)
    blocks = [x[0], jnp.concatenate(x[1:], axis=0)]
    for i, block in enumerate(blocks):
        total = jnp.dot(block, w, preferred_element_type=F32)
        total = before[i][...] + total if carried else total
        at = 0
        for ref in outs[:1] if i == 0 else outs[1:]:
            ref[...] = total[at : at + ref.shape[0]]
            at += ref.shape[0]


def project(steps, xa, others, weights, before=(), split=1):
    rows = xa.shape[0]
    depth, feats = weights[0].shape
    outs = [jax.ShapeDtypeStruct((rows, feats), F32)]
    outs += [jax.ShapeDtypeStruct((rows // split, feats), F32)] * split
    whole = pl.BlockSpec(memory_space=pltpu.VMEM)
    operands = [xa, *others, *weights, *before]
    return pl.pallas_call(
        functools.partial(project_kernel, steps, len(others), len(before)),
        in_specs=[whole] * len(operands),
        out_specs=[whole] * len(outs),
        out_shape=outs,
        compiler_params=params(),
        cost_estimate=cost(
            4 * rows * depth * feats * len(weights), 2 * depth * feats * len(weights) + 4 * rows * 4096
        ),
        name="project",
    )(*operands)


def tables_kernel(own_ref, behind_ref, freq_ref, cos_ref, sin_ref, bias_ref):
    own = own_ref[...]
    rows = own.shape[1]
    behind = jnp.where(lax.axis_index("dp") > 0, behind_ref[:, rows - REACH :], -1)
    window = jnp.concatenate([behind, own], axis=1)
    shape = (REACH, 2 * REACH)
    r, c = lax.broadcasted_iota(jnp.int32, shape, 0), lax.broadcasted_iota(jnp.int32, shape, 1)
    freq = freq_ref[...]
    for block in range(rows // REACH):
        keys = window[:, block * REACH : (block + 2) * REACH]
        mine = jnp.sum(jnp.where(c == r + REACH, keys, 0), axis=1, keepdims=True)
        same = mine == keys
        bias_ref[block] = jnp.where(same & (c <= r + REACH), 0.0, -1e30)
        position = jnp.sum(jnp.where(same & (c < r + REACH), 1.0, 0.0), axis=1, keepdims=True)
        angle = position * freq
        at = slice(block * REACH, (block + 1) * REACH)
        sign = jnp.where(lax.broadcasted_iota(jnp.int32, (REACH, HD), 1) < HD // 2, -1.0, 1.0)
        cos_ref[at, :] = jnp.cos(angle)
        sin_ref[at, :] = jnp.sin(angle) * sign


def tables(own, behind):
    rows = own.shape[0]
    half = np.arange(HD // 2, dtype=np.float32)
    freq = np.float32(500000.0) ** (-(2.0 * half) / np.float32(HD))
    freq = jnp.asarray(np.concatenate([freq, freq]).astype(np.float32).reshape(1, HD))
    whole = pl.BlockSpec(memory_space=pltpu.VMEM)
    return pl.pallas_call(
        tables_kernel,
        in_specs=[whole] * 3,
        out_specs=[whole] * 3,
        out_shape=[
            jax.ShapeDtypeStruct((rows, HD), F32),
            jax.ShapeDtypeStruct((rows, HD), F32),
            jax.ShapeDtypeStruct((rows // REACH, REACH, 2 * REACH), F32),
        ],
        compiler_params=params(),
        cost_estimate=cost(20 * rows * 2 * REACH, 16 * rows * REACH, 2 * rows * HD),
        name="tables",
    )(own.reshape(1, rows), behind.reshape(1, rows), freq)


def keys_kernel(a_ref, cos_ref, sin_ref, *refs):
    cos, sin = cos_ref[...], sin_ref[...]
    others, (out_ref, head_ref, tail_ref) = refs[:-3], refs[-3:]
    rows = out_ref.shape[0]
    for h in range(a_ref.shape[1] // HD):
        at = slice(h * HD, (h + 1) * HD)
        b = jnp.concatenate([ref[:, at] for ref in others], axis=0)
        raw = (a_ref[:, at] + b).astype(BF16).astype(F32)
        out = (raw * cos + pltpu.roll(raw, HD // 2, 1) * sin).astype(BF16)
        out_ref[:, at] = out
        head_ref[:, at] = out[:REACH]
        tail_ref[:, at] = out[rows - REACH :]


def values_kernel(a_ref, *refs):
    others, (out_ref, head_ref, tail_ref) = refs[:-3], refs[-3:]
    rows = out_ref.shape[0]
    out = (a_ref[...] + jnp.concatenate([ref[...] for ref in others], axis=0)).astype(BF16)
    out_ref[...] = out
    head_ref[...] = out[:REACH]
    tail_ref[...] = out[rows - REACH :]


def finish(kernel, name, *operands):
    rows, feats = operands[0].shape
    return pl.pallas_call(
        kernel,
        out_shape=[
            jax.ShapeDtypeStruct((rows, feats), BF16),
            jax.ShapeDtypeStruct((REACH, feats), BF16),
            jax.ShapeDtypeStruct((REACH, feats), BF16),
        ],
        compiler_params=params(),
        cost_estimate=cost(6 * rows * feats, 10 * rows * feats),
        name=name,
    )(*operands)


def scores_kernel(block, q_ref, ka_ref, kb_ref, bias_ref, out_ref):
    rows = REACH
    bias = bias_ref[block]
    ones = jnp.ones((2 * rows, rows), BF16)
    scale = math.log2(math.e) / HD**0.5
    for h in range(out_ref.shape[0]):
        at = slice(h * HD, (h + 1) * HD)
        keys = jnp.concatenate([ka_ref[:rows, at], kb_ref[-rows:, at]], axis=0)
        for j in range(GROUP):
            column = (h * GROUP + j) * HD
            q = q_ref[block * rows : (block + 1) * rows, column : column + HD]
            s = lax.dot_general(q, keys, (((1,), (1,)), ((), ())), preferred_element_type=F32)
            s = s * scale + bias
            e = jnp.exp2(s - jnp.max(s, axis=-1, keepdims=True))
            total = jnp.dot(e.astype(BF16), ones, preferred_element_type=F32)
            inverse = 1.0 / total
            w = e * jnp.concatenate([inverse, inverse], axis=1)
            out_ref[h, j * rows : (j + 1) * rows, :] = w.astype(BF16)


def softmax_weights(block, queries, keys_a, keys_b, bias):
    rows = REACH
    heads = keys_a.shape[1] // HD
    whole = pl.BlockSpec(memory_space=pltpu.VMEM)
    return pl.pallas_call(
        functools.partial(scores_kernel, block),
        in_specs=[whole] * 4,
        out_specs=whole,
        out_shape=jax.ShapeDtypeStruct((heads, GROUP * rows, 2 * rows), BF16),
        compiler_params=params(),
        cost_estimate=cost(
            4 * heads * GROUP * rows * rows * HD, 6 * rows * heads * GROUP * HD, 2 * heads * GROUP * rows * rows
        ),
        name="scores",
    )(queries, keys_a, keys_b, bias)


def context_kernel(block, p_ref, va_ref, vb_ref, *refs):
    out_ref, held, sems = refs[-3:]
    rows = held.shape[0]
    width = GROUP * HD
    copies = []
    for h in range(p_ref.shape[0]):
        at = slice(h * HD, (h + 1) * HD)
        values = jnp.concatenate([va_ref[:rows, at], vb_ref[-rows:, at]], axis=0)
        c = jnp.dot(p_ref[h], values, preferred_element_type=F32).astype(BF16)
        for j in range(GROUP):
            held[:, h * width + j * HD : h * width + (j + 1) * HD] = c[j * rows : (j + 1) * rows]
        here = (pl.ds(0, rows), pl.ds(h * width, width))
        there = (pl.ds(block * rows, rows), pl.ds(h * width, width))
        copies.append(pltpu.make_async_copy(held.at[here], out_ref.at[there], sems.at[h]))
        copies[-1].start()
    for copy in copies:
        copy.wait()


def contexts(block, weights, values_a, values_b, out=None):
    heads, _, span = weights.shape
    rows = REACH
    feats = heads * HD
    whole = pl.BlockSpec(memory_space=pltpu.VMEM)
    more = () if out is None else (out,)
    return pl.pallas_call(
        functools.partial(context_kernel, block),
        in_specs=[whole] * 3 + [pl.BlockSpec(memory_space=pl.ANY)] * len(more),
        out_specs=pl.BlockSpec(memory_space=pl.ANY),
        out_shape=jax.ShapeDtypeStruct((2 * rows, GROUP * feats), BF16),
        scratch_shapes=[
            pltpu.VMEM((rows, GROUP * feats), BF16),
            pltpu.SemaphoreType.DMA((heads,)),
        ],
        input_output_aliases={3: 0} if more else {},
        compiler_params=params(),
        cost_estimate=cost(2 * heads * GROUP * rows * span * HD, 6 * rows * heads * GROUP * HD),
        name="context",
    )(weights, values_a, values_b, *more)


def after(*values):
    return lax.optimization_barrier(values)


def place(p):
    z, x = (p, 0) if p < 4 else (7 - p, 1)
    return z * 2 + x


def ring(signs):
    return [
        (y * 16 + place(p) * 2 + c, y * 16 + place((p + sign) % 8) * 2 + c)
        for y, sign in enumerate(signs)
        for p in range(8)
        for c in range(2)
    ]


def on_ring(hidden, norm_gain, key_weight, value_weight, queries, segment_ids):
    both = ("groups", "dp")
    key_way, value_way = ring((1, -1)), ring((-1, 1))
    other_group = [(i, (i + 16) % 32) for i in range(32)]
    other_core = [(i, i ^ 1) for i in range(16)]

    def send(value, way):
        return lax.ppermute(value, both, way)

    def swap(value):
        return lax.ppermute(value, "dp", other_core)

    mine, theirs = normalise(hidden, norm_gain)
    other = [swap(t) for t in theirs]
    k1, v1 = send(key_weight, key_way), send(value_weight, value_way)
    behind = from_behind(segment_ids, "dp", 1)
    k1, mine, behind = after(k1, mine, behind)
    k2, v2 = send(k1, key_way), send(v1, value_way)
    k1b, yv1 = send(key_weight, value_way), send(v1, other_group)
    k3, v3 = send(k2, key_way), send(v2, value_way)
    yk2 = send(k2, other_group)

    key_part = project((0, -1, -2), mine, other, [key_weight, k1, k2])
    k3, yv1, key_part = after(k3, yv1, key_part)
    k4, yk3 = send(k3, key_way), send(k3, other_group)
    cos, sin, bias = tables(segment_ids, behind)
    key_part = project((-3, 2, 1), mine, other, [k3, yk2, k1b], key_part)
    v3, key_part, cos, sin, bias = after(v3, key_part, cos, sin, bias)
    v4 = send(v3, value_way)
    yk3, v3y = after(yk3, v3)
    yv3 = send(v3y, other_group)
    v2b = send(yv1, key_way)
    value_part = project((0, 1, 2, -1, 3), mine, other, [value_weight, v1, v2, yv1, v3])

    own_k, *other_k = project((-4, 3), mine, other, [k4, yk3], key_part, 2)
    *other_k, value_part = after(*[swap(o) for o in other_k], value_part)
    keys, head_keys, tail = finish(keys_kernel, "keys", own_k, cos, sin, *other_k)
    prev_keys = from_behind(tail, "dp", 1)
    p1 = softmax_weights(1, queries, keys, keys, bias)
    value_part, p1, prev_keys = after(value_part, p1, prev_keys)
    own_v, other_v = project((4, -2, -3), mine, other, [v4, v2b, yv3], value_part)
    p0 = softmax_weights(0, queries, prev_keys, head_keys, bias)
    other_v, p0 = after(swap(other_v), p0)
    values, head_values, tail = finish(values_kernel, "values", own_v, other_v)
    prev_values = from_behind(tail, "dp", 1)
    later = contexts(1, p1, values, values)
    return contexts(0, p0, prev_values, head_values, later)


def rotary(block, positions):
    half = HD // 2
    freqs = 500000.0 ** (-(2.0 * jnp.arange(half, dtype=jnp.float32)) / HD)
    angles = positions[:, None] * freqs[None, :]
    cosine = jnp.cos(angles)[:, None, :]
    sine = jnp.sin(angles)[:, None, :]
    first = block[..., :half]
    second = block[..., half:]
    return jnp.concatenate(
        [first * cosine - second * sine, second * cosine + first * sine], axis=-1
    )


def on_any(hidden, norm_gain, key_weight, value_weight, queries, segment_ids):
    whole = lax.all_gather(hidden, "tensor", axis=1, tiled=True)
    states = whole.astype(jnp.float32)
    meansq = jnp.mean(states * states, axis=-1, keepdims=True)
    normed = (states * lax.rsqrt(meansq + EPS) * norm_gain.astype(jnp.float32)).astype(BF16)
    local_rows = normed.shape[0]
    head_cols = key_weight.shape[1]

    def add_rows(piece):
        return jnp.dot(normed, piece, preferred_element_type=jnp.float32)

    key_sum = add_rows(lax.all_gather(key_weight, "dp", axis=0, tiled=True))
    value_sum = add_rows(lax.all_gather(value_weight, "dp", axis=0, tiled=True))
    keys_raw = key_sum.astype(BF16)
    values = value_sum.astype(BF16)
    earlier_keys, earlier_values, earlier_segs = from_behind(
        (keys_raw, values, segment_ids), "dp", 1
    )
    earlier_count = earlier_keys.shape[0]
    has_earlier = lax.axis_index("dp") > 0
    earlier_segs = jnp.where(has_earlier, earlier_segs, -1)
    window_segs = jnp.concatenate([earlier_segs, segment_ids], axis=0)
    window_len = window_segs.shape[0]
    window_index = jnp.arange(window_len, dtype=jnp.int32)
    same_seg = window_segs[:, None] == window_segs[None, :]
    before = window_index[None, :] < window_index[:, None]
    positions = jnp.sum((same_seg & before).astype(jnp.int32), axis=1)
    heads_here = head_cols // HD
    window_raw = (
        jnp.concatenate([earlier_keys, keys_raw], axis=0)
        .astype(jnp.float32)
        .reshape(window_len, heads_here, HD)
    )
    window_keys = rotary(window_raw, positions.astype(jnp.float32)).astype(BF16)
    window_values = jnp.concatenate([earlier_values, values], axis=0).reshape(
        window_len, heads_here, HD
    )
    query_heads = queries.reshape(local_rows, heads_here, GROUP, HD)
    scale = 1.0 / HD**0.5
    scores = (
        jnp.einsum("tkgd,skd->kgts", query_heads, window_keys, preferred_element_type=jnp.float32)
        * scale
    )
    query_pos = jnp.arange(local_rows, dtype=jnp.int32)[:, None] + earlier_count
    allowed = (window_index[None, :] <= query_pos) & (segment_ids[:, None] == window_segs[None, :])
    masked = jnp.where(allowed, scores, -1e30)
    largest = jnp.max(masked, axis=-1, keepdims=True)
    expd = jnp.where(allowed, jnp.exp(masked - largest), 0.0)
    weights = (expd / jnp.sum(expd, axis=-1, keepdims=True)).astype(BF16)
    out_heads = jnp.einsum(
        "kgts,skd->tkgd", weights, window_values, preferred_element_type=jnp.float32
    )
    return out_heads.reshape(local_rows, heads_here * GROUP * HD).astype(BF16)


def solution(mesh):
    in_specs = (
        P(("groups", "dp"), "tensor"),
        P(),
        P("dp", "tensor"),
        P("dp", "tensor"),
        P(("groups", "dp"), "tensor"),
        P(("groups", "dp")),
    )
    out_specs = P(("groups", "dp"), "tensor")
    small = (mesh.shape["groups"], mesh.shape["dp"], mesh.shape["tensor"]) == (2, 16, 1)
    return jax.shard_map(
        on_ring if small else on_any,
        mesh=mesh,
        in_specs=in_specs,
        out_specs=out_specs,
        check_vma=False,
    )
```
